32 devices in a mesh: seq: 2 (over x), shard: 16 (over z, y, core).
Axes of the slice: x: 2, y: 2, z: 4, core: 2. Of those that a mesh axis runs over, the one named last changes fastest.
Arguments:
- tokens: bfloat16 [16, 1024, 768], P('shard', 'seq'), may hold values from -6 to 6
- doc_lengths: int32 [16, 8], replicated, may hold values from 1 to 769, as said below
- qkv_weight: bfloat16 [768, 2304], P('shard'), may hold values from -0.21875 to 0.21875
- out_weight: bfloat16 [768, 768], P('shard'), may hold values from -2.5 to 2.5
- gate_weight: bfloat16 [768, 3072], P('shard'), may hold values from -0.21875 to 0.21875
- up_weight: bfloat16 [768, 3072], P('shard'), may hold values from -0.21875 to 0.21875
- down_weight: bfloat16 [3072, 768], P('shard'), may hold values from -0.109375 to 0.109375
- norm1_gain: bfloat16 [768], P('shard'), may hold values from 0.5 to 1.5
- norm1_bias: bfloat16 [768], P('shard'), may hold values from -3 to 3
- norm2_gain: bfloat16 [768], P('shard'), may hold values from 0.5 to 1.5
- norm2_bias: bfloat16 [768], P('shard'), may hold values from -3 to 3
- cotangent: bfloat16 [16, 1024, 768], P('shard', 'seq'), may hold values from -6 to 6
Outputs:
- layer_out: bfloat16 [16, 1024, 768], P('shard', 'seq')
- tokens_grad: float32 [16, 1024, 768], P('shard', 'seq')
- qkv_grad: float32 [768, 2304], P('shard')
- out_grad: float32 [768, 768], P('shard')
- gate_grad: float32 [768, 3072], P('shard')
- up_grad: float32 [768, 3072], P('shard')
- down_grad: float32 [3072, 768], P('shard')
- norm1_gain_grad: float32 [768], P('shard')
- norm1_bias_grad: float32 [768], P('shard')
- norm2_gain_grad: float32 [768], P('shard')
- norm2_bias_grad: float32 [768], P('shard')
The draws below stay inside these ranges and needn't reach their ends.
Inputs may be any that keep to these rules, and one draw needn't show every extreme that they name: `doc_lengths`: each row sums to 1024; in every row one document has length 769 and begins within the first quarter of its sequence.
All inputs are finite; a program needn't handle non-finite values.
Results may differ from the reference program's by a relative error of at most 0.017.
Values may be sent and summed in bfloat16 or wider, within the bound.
No kernel may reach another device: no remote copies, remote signals or barrier semaphores. Data moves between devices by JAX's collectives and lax.ppermute only.
A program may use at most 192 MiB of HBM per device.

```python
import jax
import jax.numpy as jnp
from jax import lax

D = 768
H = 12
HD = 64
FF = 3072
DOCS = 8
HALF = 512
SEQ_LEN = 1024
SEQS = 16


def draw_doc_lengths(key, part):
    key = jax.random.fold_in(key, 11)
    short_total = SEQ_LEN // 4 - 1

    def one_row(row_key):
        perm_key, place_key = jax.random.split(row_key)
        cut_points = jnp.sort(jax.random.permutation(perm_key, short_total - 1)[:DOCS - 2] + 1).astype(jnp.int32)
        bounds = jnp.concatenate([jnp.zeros((1,), jnp.int32), cut_points, jnp.full((1,), short_total, jnp.int32)])
        shorts = bounds[1:] - bounds[:-1]
        where_long = jax.random.randint(place_key, (), 0, DOCS)
        slot_ids = jnp.arange(DOCS, dtype=jnp.int32)
        before_long = shorts[jnp.clip(slot_ids, 0, DOCS - 2)]
        after_long = shorts[jnp.clip(slot_ids - 1, 0, DOCS - 2)]
        long_size = 3 * SEQ_LEN // 4 + 1
        return jnp.where(slot_ids < where_long, before_long, jnp.where(slot_ids == where_long, long_size, after_long)).astype(jnp.int32)
    return jax.vmap(one_row)(jax.random.split(key, SEQS))


def spiked(drawn, stream_key, source, target, shards_of, factor):
    owner, partner = [(jnp.arange(drawn.shape[dim]) // (drawn.shape[dim] // shards_of)).reshape([-1 if axis == dim else 1 for axis in range(drawn.ndim)]) for dim in (source, target)]
    chosen = jax.random.permutation(stream_key, shards_of)[partner]
    strong = (owner == chosen) | (owner == (partner + shards_of // 2) % shards_of)
    return jnp.where(strong, factor * drawn, drawn)


def levels(stream_key, dims, pieces, smallest, largest):
    def one(axis_at, parts):
        draws = jax.random.uniform(jax.random.fold_in(jax.random.fold_in(stream_key, 6), axis_at), (parts,), jnp.float32, smallest / len(pieces), largest / len(pieces))
        return jnp.repeat(jnp.exp(draws), dims[axis_at] // parts).reshape((-1,) + (1,) * (len(dims) - axis_at - 1))

    gain = one(*pieces[0])
    for cut in pieces[1:]:
        gain = gain * one(*cut)
    return gain


def scatter_about(stream_key, extent, deviation, limit, cuts=(), kind=jnp.bfloat16):
    drawn = jax.random.normal(stream_key, extent, jnp.float32) * deviation
    if len(cuts) > 0:
        drawn = levels(stream_key, extent, cuts, -0.22, 0.18) * drawn
    return jnp.clip(drawn, min=-limit, max=limit).astype(kind)


def noise_with(rng, dims, spread, limit, cuts, heavy, held_as=jnp.bfloat16):
    entries = spread * jax.random.normal(rng, dims, jnp.float32)
    if cuts:
        entries = entries * levels(rng, dims, cuts, -0.22, 0.18)
    return jnp.clip(spiked(entries, jax.random.fold_in(rng, 3), *heavy), -limit, limit).astype(held_as)


def setup_inputs(seed: int = 0) -> dict:
    arg_keys = jax.random.split(jax.random.key(seed), 13)
    tokens = noise_with(arg_keys[0], (SEQS, SEQ_LEN, D), 1.0, 6.0, ((0, 16), (1, 2)), (0, 2, 16, 2.0))
    doc_lengths = draw_doc_lengths(jax.random.fold_in(arg_keys[12], 71), 0)
    qkv_weight = scatter_about(arg_keys[2], (D, 3 * D), D ** -0.5, 0.21875, ((0, 16),))
    out_weight = scatter_about(arg_keys[3], (D, D), (D // 128) ** -0.5, 2.5, ((0, 16),))
    gate_weight = scatter_about(arg_keys[4], (D, FF), D ** -0.5, 0.21875, ((0, 16),))
    up_weight = scatter_about(arg_keys[5], (D, FF), D ** -0.5, 0.21875, ((0, 16),))
    down_weight = scatter_about(arg_keys[6], (FF, D), FF ** -0.5, 0.109375, ((0, 16),))
    norm1_gain = jnp.clip(1.0 + 0.1 * jax.random.normal(arg_keys[7], (D,), jnp.float32), 0.5, 1.5).astype(jnp.bfloat16)
    norm1_bias = scatter_about(arg_keys[8], (D,), 0.5, 3.0, ((0, 16),))
    norm2_gain = jnp.clip(1.0 + 0.1 * jax.random.normal(arg_keys[9], (D,), jnp.float32), 0.5, 1.5).astype(jnp.bfloat16)
    norm2_bias = scatter_about(arg_keys[10], (D,), 0.5, 3.0, ((0, 16),))
    cotangent = scatter_about(arg_keys[11], (SEQS, SEQ_LEN, D), 1.0, 6.0, ((0, 16), (1, 2)))
    return {"tokens": tokens, "doc_lengths": doc_lengths, "qkv_weight": qkv_weight, "out_weight": out_weight, "gate_weight": gate_weight, "up_weight": up_weight, "down_weight": down_weight, "norm1_gain": norm1_gain, "norm1_bias": norm1_bias, "norm2_gain": norm2_gain, "norm2_bias": norm2_bias, "cotangent": cotangent}


@jax.custom_vjp
def low(v):
    return lax.optimization_barrier(v.astype(jnp.bfloat16)).astype(jnp.float32)

@jax.custom_vjp
def low_back(v):
    return v

def low_keep(v):
    return (low(v), None)

def low_pass(kept, grad):
    return (grad,)

def back_keep(v):
    return (v, None)

def back_low(kept, grad):
    return (low(grad),)
low.defvjp(low_keep, low_pass)
low_back.defvjp(back_keep, back_low)
rope_base = 1000.0
norm_eps = 1e-05
big_negative = -1e+30
highest = lax.Precision.HIGHEST

def doc_layout(doc_sizes):
    doc_ends = jnp.cumsum(doc_sizes).astype(jnp.int32)
    doc_starts = (doc_ends - doc_sizes).astype(jnp.int32)
    places = jnp.arange(SEQ_LEN, dtype=jnp.int32)
    segment = lax.optimization_barrier(jnp.sum((places[:, None] >= doc_ends[None, :]).astype(jnp.int32), axis=1)).astype(jnp.int32)
    onehot = segment[:, None] == jnp.arange(DOCS, dtype=jnp.int32)[None, :]
    offset = lax.optimization_barrier(jnp.sum(jnp.where(onehot, doc_starts[None, :], 0), axis=1)).astype(jnp.int32)
    return (segment, (places - offset).astype(jnp.int32))

def rotate(features, places, direction):
    half_dim = HD // 2
    frequency = rope_base ** (-jnp.arange(half_dim, dtype=jnp.float32) * 2.0 / HD)
    angles = places.astype(jnp.float32)[:, None] * frequency[None, :]
    cosine = jnp.cos(angles)[:, None, :]
    sine_part = direction * jnp.sin(angles)[:, None, :]
    lower_half = features[..., :half_dim]
    upper_half = features[..., half_dim:]
    return jnp.concatenate([lower_half * cosine - upper_half * sine_part, upper_half * cosine + lower_half * sine_part], axis=-1)

def normalize(residual, gain_vec, bias_vec):
    average = lax.optimization_barrier(jnp.mean(residual, axis=-1, keepdims=True))
    centered = residual - average
    variance = lax.optimization_barrier(jnp.mean(centered * centered, axis=-1, keepdims=True))
    return centered * lax.rsqrt(variance + norm_eps) * gain_vec + bias_vec

def swiglu(gate_pre, up_branch):
    return gate_pre / (1.0 + jnp.exp(-gate_pre)) * up_branch

def sequence_layer(seq_rows, doc_sizes, weights):
    wqkv, wout, wgate, wup, wdown, gain_one, bias_one, gain_two, bias_two = weights
    segment, places = doc_layout(doc_sizes)
    qkv = low_back(jnp.dot(seq_rows, wqkv, precision=highest))
    queries = rotate(qkv[:, :D].reshape(SEQ_LEN, H, HD), places, 1.0)
    keys_rot = rotate(qkv[:, D:2 * D].reshape(SEQ_LEN, H, HD), places, 1.0)
    values = qkv[:, 2 * D:].reshape(SEQ_LEN, H, HD)
    queries = low(queries)
    keys_rot = low(keys_rot)
    values = low(values)
    token_idx = jnp.arange(SEQ_LEN, dtype=jnp.int32)
    allowed = (segment[:, None] == segment[None, :]) & (jnp.abs(token_idx[:, None] - token_idx[None, :]) <= HALF)
    scores = low_back(jnp.einsum('qhd,khd->hqk', queries, keys_rot, precision=highest) * HD ** (-0.5))
    scores = jnp.where(allowed[None], scores, big_negative)
    peak = lax.optimization_barrier(jnp.max(scores, axis=-1, keepdims=True))
    expo = jnp.exp(scores - peak)
    probabilities = low(expo / lax.optimization_barrier(jnp.sum(expo, axis=-1, keepdims=True)))
    attended = jnp.einsum('hqk,khd->qhd', probabilities, values, precision=highest).reshape(SEQ_LEN, D)
    attended = low(low_back(attended))
    branch = low_back(jnp.dot(attended, wout, precision=highest))
    normed_one = normalize(seq_rows + branch, gain_one, bias_one)
    first_low = low(normed_one)
    gate_pre = low_back(jnp.dot(first_low, wgate, precision=highest))
    up_branch = low_back(jnp.dot(first_low, wup, precision=highest))
    hidden = low(swiglu(gate_pre, up_branch))
    mlp_out = low_back(jnp.dot(hidden, wdown, precision=highest))
    return normalize(normed_one + mlp_out, gain_two, bias_two)

def reference(tokens, doc_lengths, qkv_weight, out_weight, gate_weight, up_weight, down_weight, norm1_gain, norm1_bias, norm2_gain, norm2_bias, cotangent):
    weights = tuple((w_item.astype(jnp.float32) for w_item in (qkv_weight, out_weight, gate_weight, up_weight, down_weight, norm1_gain, norm1_bias, norm2_gain, norm2_bias)))
    inputs = tokens.astype(jnp.float32)

    def forward(inputs, weights):

        def per_sequence(operands):
            return sequence_layer(operands[0], operands[1], weights)
        return lax.map(jax.checkpoint(per_sequence), (inputs, doc_lengths))
    result, pullback = jax.vjp(forward, inputs, weights)
    grads_in, grads_w = pullback(cotangent.astype(jnp.float32))
    layer_out = result.astype(jnp.bfloat16)
    return (layer_out, grads_in, grads_w[0], grads_w[1], grads_w[2], grads_w[3], grads_w[4], grads_w[5], grads_w[6], grads_w[7], grads_w[8])
```

```python
from functools import partial

import jax
import jax.numpy as jnp
from jax import lax
from jax.experimental import pallas as pl
from jax.experimental.pallas import tpu as pltpu
from jax.sharding import PartitionSpec as P

D = 768
H = 12
HD = 64
FF = 3072
HALF = 512
PAIRS = H // 2
BLK = 768
MIB = 1 << 20

rope_base = 1000.0
norm_eps = 1e-05
big_negative = -1e30

bf16 = jnp.bfloat16
f32 = jnp.float32
VM = pl.BlockSpec(memory_space=pltpu.VMEM)
SM = pl.BlockSpec(memory_space=pltpu.SMEM)
HBM = pl.BlockSpec(memory_space=pl.ANY)


def dot(a, b):
    return lax.dot_general(a, b, (((1,), (0,)), ((), ())), preferred_element_type=f32)


def dot_t(a, b):
    return lax.dot_general(a, b, (((1,), (1,)), ((), ())), preferred_element_type=f32)


def params(mib):
    return pltpu.CompilerParams(vmem_limit_bytes=mib * MIB)


def cost(flops, moved, trans=0):
    return pl.CostEstimate(flops=int(flops), bytes_accessed=int(moved), transcendentals=int(trans))


def shape(dims, kind):
    return jax.ShapeDtypeStruct(dims, kind)


def piece_copies(meta, pieces, dst, sems):
    x, z, y, c = meta[0], meta[1], meta[2], meta[3]
    rows = pieces[0].shape[1]
    copies = []
    for at, piece in enumerate(pieces):
        dc, dy, dh = at // 4, (at // 2) % 2, at % 2
        h = jnp.where(x == 0, dh, 1 - dh)
        yy = jnp.where(y == 0, dy, 1 - dy)
        cc = jnp.where(c == 0, dc, 1 - dc)
        for k in range(4):
            zz = lax.rem(z - k + 4, 4)
            row = pl.multiple_of(((zz * 2 + yy) * 2 + cc) * rows, rows)
            copies.append(
                pltpu.make_async_copy(
                    piece.at[k], dst.at[h, pl.ds(row, rows)], sems.at[at * 4 + k]
                )
            )
    return copies


def spin(u, cosine, sine):
    lane = lax.broadcasted_iota(jnp.int32, u.shape, 1)
    swapped = jnp.where(lane % HD < HD // 2, pltpu.roll(u, 96, 1), pltpu.roll(u, 32, 1))
    return u * cosine + swapped * sine


def qkv_kernel(meta, own, other, cosine, sine, *rest):
    pieces = rest[:8]
    q_out, k_out, kt_out, v_out, vt_out, w_out, w, sems, out_sem = rest[8:]
    step = pl.program_id(0)
    copies = piece_copies(meta, pieces, w, sems)

    @pl.when(step == 0)
    def _():
        for copy in copies:
            copy.start()
        for copy in copies:
            copy.wait()
        pltpu.make_async_copy(w, w_out, out_sem).start()

    col = pl.multiple_of(step * 256, 256)
    wq = w[0, :, pl.ds(col, 256)]
    wk = w[0, :, pl.ds(pl.multiple_of(col + D, 256), 256)]
    wv = w[1, :, pl.ds(col, 256)]
    for half, rows in enumerate((own, other)):
        at = slice(half * HALF, (half + 1) * HALF)
        xs = rows[...]
        cs, sn = cosine[at, :], sine[at, :]
        qs, ks, vs = dot(xs, wq), dot(xs, wk), dot(xs, wv).astype(bf16)
        for i in range(2):
            lanes = slice(i * 128, (i + 1) * 128)
            q_out[at, lanes] = spin(qs[:, lanes], cs, sn).astype(bf16)
            kr = spin(ks[:, lanes], cs, sn).astype(bf16)
            k_out[at, lanes] = kr
            kt_out[lanes, at] = kr.T
        v_out[at, :] = vs
        vt_out[:, at] = vs.T

    @pl.when(step == 2)
    def _():
        pltpu.make_async_copy(w, w_out, out_sem).wait()


def qkv_call(meta, own, other, cosine, sine, pieces):
    rows = 2 * HALF
    full = pl.BlockSpec((rows, 128), lambda i: (0, 0))
    x_spec = pl.BlockSpec((HALF, D), lambda i: (0, 0))
    nat = pl.BlockSpec((rows, 256), lambda i: (0, i))
    tr = pl.BlockSpec((256, rows), lambda i: (i, 0))
    return pl.pallas_call(
        qkv_kernel,
        grid=(3,),
        in_specs=[SM, x_spec, x_spec, full, full] + [HBM] * 8,
        out_specs=[nat, nat, tr, nat, tr, HBM],
        out_shape=[
            shape((rows, D), bf16),
            shape((rows, D), bf16),
            shape((D, rows), bf16),
            shape((rows, D), bf16),
            shape((D, rows), bf16),
            shape((2, D, 2 * BLK), bf16),
        ],
        scratch_shapes=[
            pltpu.VMEM((2, D, 2 * BLK), bf16),
            pltpu.SemaphoreType.DMA((32,)),
            pltpu.SemaphoreType.DMA,
        ],
        compiler_params=params(48),
        cost_estimate=cost(2 * rows * D * 3 * D, 20e6),
        name="qkv",
    )(meta, own, other, cosine, sine, *pieces)


def segment_of(meta, pos):
    seg = jnp.zeros(pos.shape, jnp.int32)
    for d in range(8):
        seg = seg + jnp.where(pos >= meta[8 + d], 1, 0)
    return seg


def bias_of(meta, key_base, keys, query_base):
    row = lax.broadcasted_iota(jnp.int32, (keys, 128), 0)
    key_pos = jnp.where(row < HALF, row + key_base[0], row - HALF + key_base[1])
    key_seg = segment_of(meta, key_pos)[:, :1]
    key_pos = key_pos[:, :1]
    query_pos = lax.broadcasted_iota(jnp.int32, (8, HALF), 1) + query_base
    query_seg = segment_of(meta, query_pos)[:1]
    query_pos = query_pos[:1]
    near = jnp.abs(key_pos - query_pos) <= HALF
    return jnp.where((key_seg == query_seg) & near, 0.0, big_negative).astype(f32)


def head_part(block, hh, scale=None):
    lane = lax.broadcasted_iota(jnp.int32, block.shape, 1)
    kept = jnp.where((lane // HD) == hh, block, jnp.zeros_like(block))
    return kept if scale is None else kept * jnp.asarray(scale, block.dtype)


def attend_kernel(meta, q, k, vt, att, att_t, lse, bias):
    @pl.when(pl.program_id(0) == 0)
    def _():
        own, other = meta[0] * HALF, HALF - meta[0] * HALF
        bias[...] = bias_of(meta, (own, other), 2 * HALF, own)

    parts = []
    for hh in range(2):
        qz = head_part(q[...], hh, HD**-0.5)
        s = dot_t(k[...], qz) + bias[...]
        peak = jnp.max(s, axis=0, keepdims=True)
        e = jnp.exp(s - peak)
        total = jnp.sum(e, axis=0, keepdims=True)
        o = dot(vt[hh * HD : (hh + 1) * HD, :], e.astype(bf16)) * (1.0 / total)
        parts.append(o.astype(bf16))
        lse[0, hh : hh + 1, :] = peak + jnp.log(total)
    both = jnp.concatenate(parts, axis=0)
    att_t[...] = both
    att[...] = both.T


def attend_call(meta, q, k, vt):
    return pl.pallas_call(
        attend_kernel,
        grid=(PAIRS,),
        in_specs=[
            SM,
            pl.BlockSpec((HALF, 128), lambda i: (0, i)),
            pl.BlockSpec((2 * HALF, 128), lambda i: (0, i)),
            pl.BlockSpec((128, 2 * HALF), lambda i: (i, 0)),
        ],
        out_specs=[
            pl.BlockSpec((HALF, 128), lambda i: (0, i)),
            pl.BlockSpec((128, HALF), lambda i: (i, 0)),
            pl.BlockSpec((1, 2, HALF), lambda i: (i, 0, 0)),
        ],
        out_shape=[
            shape((HALF, D), bf16),
            shape((D, HALF), bf16),
            shape((PAIRS, 2, HALF), f32),
        ],
        scratch_shapes=[pltpu.VMEM((2 * HALF, HALF), f32)],
        compiler_params=params(48),
        cost_estimate=cost(4 * 4 * H * 2 * HALF * HALF * HD, 8e6, H * 2 * HALF * HALF),
        name="attend",
    )(meta, q, k, vt)


def back_own_kernel(meta, q, k, kt, v, g, lse, delta, cosine, sine, dq, dk, dv, bias):
    @pl.when(pl.program_id(0) == 0)
    def _():
        own, other = meta[0] * HALF, HALF - meta[0] * HALF
        bias[...] = bias_of(meta, (own, other), 2 * HALF, own)

    parts = []
    for hh in range(2):
        qz = head_part(q[...], hh, HD**-0.5)
        gz = head_part(g[...], hh)
        s = dot_t(k[...], qz) + bias[...]
        p = jnp.exp(s - lse[0, hh : hh + 1, :])
        dp = dot_t(v[...], gz)
        ds = (p * (dp - delta[0, hh : hh + 1, :])).astype(bf16)
        parts.append(dot(kt[hh * HD : (hh + 1) * HD, :], ds) * HD**-0.5)
        gk = dot(ds[:HALF], qz)
        gv = dot(p[:HALF].astype(bf16), gz)
        if hh == 0:
            dk[...] = gk
            dv[...] = gv
        else:
            dk[...] += gk
            dv[...] += gv
    dq[...] = spin(jnp.concatenate(parts, axis=0).T, cosine[...], -sine[...]).astype(bf16)


def back_own_call(meta, q, k, kt, v, g, lse, delta, cosine, sine):
    nat = pl.BlockSpec((HALF, 128), lambda i: (0, i))
    wide = pl.BlockSpec((2 * HALF, 128), lambda i: (0, i))
    row = pl.BlockSpec((1, 2, HALF), lambda i: (i, 0, 0))
    table = pl.BlockSpec((HALF, 128), lambda i: (0, 0))
    return pl.pallas_call(
        back_own_kernel,
        grid=(PAIRS,),
        in_specs=[
            SM,
            nat,
            wide,
            pl.BlockSpec((128, 2 * HALF), lambda i: (i, 0)),
            wide,
            nat,
            row,
            row,
            table,
            table,
        ],
        out_specs=[nat, nat, nat],
        out_shape=[shape((HALF, D), bf16), shape((HALF, D), f32), shape((HALF, D), f32)],
        scratch_shapes=[pltpu.VMEM((2 * HALF, HALF), f32)],
        compiler_params=params(48),
        cost_estimate=cost(4 * 8 * H * 2 * HALF * HALF * HD, 12e6, H * 2 * HALF * HALF),
        name="back_own",
    )(meta, q, k, kt, v, g, lse, delta, cosine, sine)


def back_other_kernel(meta, q, k, v, g, lse, delta, cosine, sine, dk_in, dv_in, dk, dv, bias):
    @pl.when(pl.program_id(0) == 0)
    def _():
        own, other = meta[0] * HALF, HALF - meta[0] * HALF
        bias[...] = bias_of(meta, (own, own), HALF, other)

    gk = dk_in[...]
    gv = dv_in[...]
    for hh in range(2):
        qz = head_part(q[...], hh, HD**-0.5)
        gz = head_part(g[...], hh)
        s = dot_t(k[...], qz) + bias[...]
        p = jnp.exp(s - lse[0, hh : hh + 1, :])
        dp = dot_t(v[...], gz)
        ds = (p * (dp - delta[0, hh : hh + 1, :])).astype(bf16)
        gk = gk + dot(ds, qz)
        gv = gv + dot(p.astype(bf16), gz)
    dk[...] = spin(gk, cosine[...], -sine[...]).astype(bf16)
    dv[...] = gv.astype(bf16)


def back_other_call(meta, q, k, v, g, lse, delta, cosine, sine, dk_in, dv_in):
    nat = pl.BlockSpec((HALF, 128), lambda i: (0, i))
    second = pl.BlockSpec((HALF, 128), lambda i: (1, i))
    row = pl.BlockSpec((1, 2, HALF), lambda i: (i, 0, 0))
    table = pl.BlockSpec((HALF, 128), lambda i: (0, 0))
    return pl.pallas_call(
        back_other_kernel,
        grid=(PAIRS,),
        in_specs=[SM, second, nat, nat, nat, row, row, table, table, nat, nat],
        out_specs=[nat, nat],
        out_shape=[shape((HALF, D), bf16)] * 2,
        scratch_shapes=[pltpu.VMEM((HALF, HALF), f32)],
        compiler_params=params(48),
        cost_estimate=cost(4 * 4 * H * HALF * HALF * HD, 10e6, H * HALF * HALF),
        name="back_other",
    )(meta, q, k, v, g, lse, delta, cosine, sine, dk_in, dv_in)


def norm_parts(r):
    centered = r - jnp.mean(r, axis=-1, keepdims=True)
    scale = lax.rsqrt(jnp.mean(centered * centered, axis=-1, keepdims=True) + norm_eps)
    return centered * scale, scale


def norm_back(c, z, scale, gain):
    e = c * gain
    return (e - jnp.mean(e, axis=-1, keepdims=True) - z * jnp.mean(e * z, axis=-1, keepdims=True)) * scale


def branch_kernel(rows, att, w, res):
    res[...] = rows[...].astype(f32) + dot(att[...], w[0])


def branch_call(rows, att, w1):
    return pl.pallas_call(
        branch_kernel,
        grid=(2,),
        in_specs=[
            pl.BlockSpec((HALF // 2, D), lambda i: (i, 0)),
            pl.BlockSpec((HALF // 2, D), lambda i: (i, 0)),
            pl.BlockSpec((1, D, BLK), lambda i: (1, 0, 1)),
        ],
        out_specs=pl.BlockSpec((HALF // 2, D), lambda i: (i, 0)),
        out_shape=shape((HALF, D), f32),
        compiler_params=params(32),
        cost_estimate=cost(2 * HALF * D * D, 5e6),
        name="branch",
    )(rows, att, w1)


def split_core(c, val):
    parts = val.astype(bf16).reshape(8, 2, 48, val.shape[1])
    return (
        jnp.where(c == 0, parts[:, 0], parts[:, 1]),
        jnp.where(c == 0, parts[:, 1], parts[:, 0]),
    )


def mlp_kernel(meta, res, cot, vecs, wu, wd, *rest):
    pieces = rest[:8]
    (
        out,
        gnorm,
        vgrads,
        keep_g,
        send_g,
        keep_u,
        send_u,
        down_g,
        wg,
        gate,
        up,
        hidden,
        low,
        low_t,
        m,
        acc,
        sems,
    ) = rest[8:]
    step = pl.program_id(0)
    copies = piece_copies(meta, pieces, wg, sems)

    @pl.when(step == 0)
    def _():
        for copy in copies:
            copy.start()
        z, _ = norm_parts(res[...])
        n1 = z * vecs[0:1, :] + vecs[1:2, :]
        acc[...] = n1
        low[...] = n1.astype(bf16)
        low_t[...] = n1.astype(bf16).T
        for copy in copies:
            copy.wait()

    def gate_weight(j):
        return wg[j // 2, :, pl.ds(pl.multiple_of((j % 2) * BLK, BLK), BLK)]

    def up_weight():
        return wu[...].reshape(D, BLK)

    def down_weight():
        slab = wd[...]
        return jnp.concatenate(
            [slab[s, :, r * D : (r + 1) * D] for s in range(4) for r in range(4)], axis=0
        )

    @pl.when(step < 4)
    def _():
        g = dot(low[...], gate_weight(step))
        u = dot(low[...], up_weight())
        h = (g / (1.0 + jnp.exp(-g)) * u).astype(bf16)
        gate[step] = g
        up[step] = u
        hidden[step] = h
        acc[...] += dot(h, down_weight())

    @pl.when(step == 3)
    def _():
        z, scale = norm_parts(acc[...])
        out[...] = (z * vecs[2:3, :] + vecs[3:4, :]).astype(bf16)
        c = cot[...].astype(f32)
        vgrads[0:1, :] = jnp.sum(c * z, axis=0, keepdims=True)
        vgrads[1:2, :] = jnp.sum(c, axis=0, keepdims=True)
        back = norm_back(c, z, scale, vecs[2:3, :])
        acc[...] = back
        m[...] = back.astype(bf16)

    @pl.when(step >= 4)
    def _():
        j = step - 4
        c = meta[3]
        g, u = gate[j], up[j]
        down_g[...] = lax.dot_general(
            hidden[j], m[...], (((0,), (0,)), ((), ())), preferred_element_type=f32
        ).astype(bf16)
        hg = dot_t(m[...], down_weight())
        sig = 1.0 / (1.0 + jnp.exp(-g))
        gate_g = (hg * u * sig * (1.0 + g * (1.0 - sig))).astype(bf16)
        up_g = (hg * g * sig).astype(bf16)
        keep_g[0], send_g[0] = split_core(c, dot(low_t[...], gate_g))
        keep_u[0], send_u[0] = split_core(c, dot(low_t[...], up_g))
        acc[...] += dot_t(gate_g, gate_weight(j)) + dot_t(up_g, up_weight())

    @pl.when(step == 7)
    def _():
        gnorm[...] = acc[...]


def mlp_call(meta, res, cot, vecs, wud, pieces):
    def whole(dims):
        return pl.BlockSpec(dims, lambda i: (0,) * len(dims))

    def late(i):
        return jnp.maximum(i - 4, 0)

    grad = pl.BlockSpec((1, 8, 48, BLK), lambda i: (late(i) // 2, 0, 0, late(i) % 2))
    gshape = shape((2, 8, 48, 2 * BLK), bf16)
    return pl.pallas_call(
        mlp_kernel,
        grid=(8,),
        in_specs=[
            SM,
            whole((HALF, D)),
            whole((HALF, D)),
            whole((8, D)),
            pl.BlockSpec((16, 48, BLK), lambda i: (0, 0, i % 4)),
            pl.BlockSpec((4, 48, FF), lambda i: (i % 4, 1, 0)),
        ]
        + [HBM] * 8,
        out_specs=[
            whole((HALF, D)),
            whole((HALF, D)),
            whole((8, D)),
            grad,
            grad,
            grad,
            grad,
            pl.BlockSpec((BLK, D), lambda i: (late(i), 0)),
        ],
        out_shape=[
            shape((HALF, D), bf16),
            shape((HALF, D), f32),
            shape((8, D), f32),
            gshape,
            gshape,
            gshape,
            gshape,
            shape((FF, D), bf16),
        ],
        scratch_shapes=[
            pltpu.VMEM((2, D, 2 * BLK), bf16),
            pltpu.VMEM((4, HALF, BLK), f32),
            pltpu.VMEM((4, HALF, BLK), f32),
            pltpu.VMEM((4, HALF, BLK), bf16),
            pltpu.VMEM((HALF, D), bf16),
            pltpu.VMEM((D, HALF), bf16),
            pltpu.VMEM((HALF, D), bf16),
            pltpu.VMEM((HALF, D), f32),
            pltpu.SemaphoreType.DMA((32,)),
        ],
        compiler_params=params(60),
        cost_estimate=cost(9 * 2 * HALF * D * FF, 40e6, 2 * HALF * FF),
        name="mlp",
    )(meta, res, cot, vecs, wud, wud, *pieces)


def norm_one_kernel(res, gnorm, vecs, att, w, marks, g_one, low, att_g, delta, vgrads):
    z, scale = norm_parts(res[...])
    c = gnorm[...]
    vgrads[0:1, :] = jnp.sum(c * z, axis=0, keepdims=True)
    vgrads[1:2, :] = jnp.sum(c, axis=0, keepdims=True)
    back = norm_back(c, z, scale, vecs[0:1, :])
    g_one[...] = back
    back = back.astype(bf16)
    low[...] = back
    ag = dot_t(back, w[0]).astype(bf16)
    att_g[...] = ag
    prod = ag.astype(f32) * att[...].astype(f32)
    delta[...] = lax.dot_general(
        marks[...],
        prod,
        (((1,), (1,)), ((), ())),
        preferred_element_type=f32,
        precision=lax.Precision.HIGHEST,
    )


def norm_one_call(res, gnorm, vecs, att, w1, marks):
    def whole(dims):
        return pl.BlockSpec(dims, lambda i: (0,) * len(dims))

    return pl.pallas_call(
        norm_one_kernel,
        grid=(1,),
        in_specs=[
            whole((HALF, D)),
            whole((HALF, D)),
            whole((8, D)),
            whole((HALF, D)),
            pl.BlockSpec((1, D, BLK), lambda i: (1, 0, 1)),
            whole((16, D)),
        ],
        out_specs=[
            whole((HALF, D)),
            whole((HALF, D)),
            whole((HALF, D)),
            whole((16, HALF)),
            whole((8, D)),
        ],
        out_shape=[
            shape((HALF, D), f32),
            shape((HALF, D), bf16),
            shape((HALF, D), bf16),
            shape((16, HALF), f32),
            shape((8, D), f32),
        ],
        compiler_params=params(40),
        cost_estimate=cost(2 * HALF * D * D, 9e6),
        name="norm_one",
    )(res, gnorm, vecs, att, w1, marks)


def first_grads_kernel(meta, rows, att_t, dq, dk, dv, low, keep, send, rows_t):
    step = pl.program_id(0)

    @pl.when(step == 0)
    def _():
        rows_t[...] = rows[...].T

    for j, right in enumerate((dq, dk, dv, low)):

        @pl.when(step == j)
        def _():
            left = att_t[...] if j == 3 else rows_t[...]
            keep[0], send[0] = split_core(meta[3], dot(left, right[...]))


def first_grads_call(meta, rows, att_t, dq, dk, dv, low):
    def whole(dims):
        return pl.BlockSpec(dims, lambda i: (0,) * len(dims))

    grad = pl.BlockSpec((1, 8, 48, BLK), lambda i: (i // 2, 0, 0, i % 2))
    nat = whole((HALF, D))
    return pl.pallas_call(
        first_grads_kernel,
        grid=(4,),
        in_specs=[SM, nat, whole((D, HALF)), nat, nat, nat, nat],
        out_specs=[grad, grad],
        out_shape=[shape((2, 8, 48, 2 * BLK), bf16)] * 2,
        scratch_shapes=[pltpu.VMEM((D, HALF), bf16)],
        compiler_params=params(40),
        cost_estimate=cost(2 * HALF * D * D * 4, 10e6),
        name="first_grads",
    )(meta, rows, att_t, dq, dk, dv, low)


def tokens_grad_kernel(g_one, dq, dk, dv, w, out):
    out[...] = (
        g_one[...]
        + dot_t(dq[...], w[0, :, :D])
        + dot_t(dk[...], w[0, :, D:])
        + dot_t(dv[...], w[1, :, :D])
    )


def tokens_grad_call(g_one, dq, dk, dv, w1):
    part = pl.BlockSpec((HALF // 2, D), lambda i: (i, 0))
    return pl.pallas_call(
        tokens_grad_kernel,
        grid=(2,),
        in_specs=[part, part, part, part, pl.BlockSpec((2, D, 2 * BLK), lambda i: (0, 0, 0))],
        out_specs=part,
        out_shape=shape((HALF, D), f32),
        compiler_params=params(40),
        cost_estimate=cost(2 * HALF * D * D * 3, 12e6),
        name="tokens_grad",
    )(g_one, dq, dk, dv, w1)


def pick(a, at, axis):
    return lax.dynamic_index_in_dim(a, at, axis, keepdims=False)


def flip_x(a):
    return lax.ppermute(a, "seq", [(0, 1), (1, 0)])


def flip(bit):
    def go(a):
        n = lax.axis_size("shard")
        return lax.ppermute(a, "shard", [(s, s ^ bit) for s in range(n)])

    return go


flip_c, flip_y = flip(1), flip(2)


def turn_z(a, k):
    return lax.ppermute(a, "shard", [(s, (s + 4 * k) % 16) for s in range(16)])


def gather_pieces(block, x, y_first):
    mine = pick(block, x, 0)
    a = jnp.stack([mine] + [turn_z(mine, k) for k in (1, 2, 3)])
    if y_first:
        by = flip_y(a)
        bx, bxy = flip_x(a), flip_x(by)
    else:
        bx = flip_x(a)
        by, bxy = flip_y(a), flip_y(bx)
    near = [a, bx, by, bxy]
    return near + [flip_c(t) for t in near]


def pieces_of_whole(full):
    cols = full.shape[1] // 2
    cut = full.reshape(4, 2, 2, 48, 2, cols)
    order = jnp.array([0, 3, 2, 1])
    return [
        cut[:, dy, dc, :, dh][order] for dc in range(2) for dy in range(2) for dh in range(2)
    ]


def add(a, b):
    return a.astype(f32) + b.astype(f32)


def scatter_sum(keep, send, spot, x_first):
    x, z, y = spot
    rows, cols = keep.shape[2:]
    cut = (2, 4, 2, rows, cols)
    got = flip_c(send).reshape(cut)
    kept = keep.reshape(cut)

    def half(at, axis):
        return add(pick(kept, at, axis), pick(got, at, axis))

    if x_first:
        near = add(half(x, 0), flip_x(half(1 - x, 0).astype(bf16)))
        near = add(pick(near, y, 1), flip_y(pick(near, 1 - y, 1).astype(bf16)))
    else:
        near = add(half(y, 2), flip_y(half(1 - y, 2).astype(bf16)))
        near = add(pick(near, x, 0), flip_x(pick(near, 1 - x, 0).astype(bf16)))
    total = pick(near, z, 0)
    for k in (1, 2, 3):
        total = total + turn_z(pick(near, (z + k) % 4, 0).astype(bf16), k).astype(f32)
    total = total.astype(bf16)
    other = flip_x(total)
    return jnp.where(
        x == 0, jnp.stack([total, other]), jnp.stack([other, total])
    ).astype(f32)


def whole_of_split(keep, send):
    both = jnp.stack([keep, send], axis=2)
    return both.transpose(1, 2, 3, 0, 4).reshape(D, -1)


def all_sum_small(v, fast):
    if not fast:
        return lax.psum(v, ("seq", "shard"))
    v = v + flip_x(v)
    v = v + flip_c(v)
    v = v + flip_y(v)
    return v + turn_z(v, 1) + turn_z(v, 2) + turn_z(v, 3)


def gather_small(v, z, y, c):
    a = jnp.stack([v] + [turn_z(v, k) for k in (1, 2, 3)])
    near = jnp.stack([a, flip_y(a)])
    every = jnp.stack([near, flip_c(near)]).astype(f32)
    steps = jnp.arange(4)
    by_z = ((z - steps[:, None]) % 4 == steps[None, :]).astype(f32)
    bits = jnp.arange(2)
    by_y = ((y ^ bits[:, None]) == bits[None, :]).astype(f32)
    by_c = ((c ^ bits[:, None]) == bits[None, :]).astype(f32)
    pick_all = (
        by_z[:, None, None, None, None, :]
        * by_y[None, :, None, None, :, None]
        * by_c[None, None, :, :, None, None]
    )
    out = jnp.sum(pick_all[..., None, None] * every[None, None, None], axis=(3, 4, 5))
    return out.transpose(3, 0, 1, 2, 4).reshape(4, D)


def local(
    tokens,
    doc_lengths,
    qkv_weight,
    out_weight,
    gate_weight,
    up_weight,
    down_weight,
    norm1_gain,
    norm1_bias,
    norm2_gain,
    norm2_bias,
    cotangent,
):
    n = lax.axis_size("shard")
    fast = n == 16
    x = lax.axis_index("seq").astype(jnp.int32)
    shard = lax.axis_index("shard").astype(jnp.int32)
    zero = jnp.zeros((), jnp.int32)
    z, y, c = (shard // 4, (shard // 2) % 2, shard % 2) if fast else (zero, zero, zero)

    rows = tokens[0]
    rows_other = flip_x(rows)

    first_block = jnp.concatenate([qkv_weight, out_weight], axis=1)
    vec_block = jnp.stack([norm1_gain, norm1_bias, norm2_gain, norm2_bias])
    if fast:
        first = jnp.stack([first_block[:, : 2 * BLK], first_block[:, 2 * BLK :]])
        first_pieces = gather_pieces(first, x, True)
        second = jnp.stack([gate_weight[:, : 2 * BLK], gate_weight[:, 2 * BLK :]])
        second, _ = lax.optimization_barrier((second, first_pieces[0]))
        gate_pieces = gather_pieces(second, x, False)
        vecs = gather_small(vec_block, z, y, c)
        slab = jnp.concatenate(
            [
                up_weight,
                down_weight.reshape(4, 48, D).transpose(1, 0, 2).reshape(48, FF),
            ],
            axis=0,
        )
        up_down = lax.all_gather(slab, "shard", axis=0)
    else:
        first_pieces = pieces_of_whole(lax.all_gather(first_block, "shard", axis=0, tiled=True))
        gate_pieces = pieces_of_whole(lax.all_gather(gate_weight, "shard", axis=0, tiled=True))
        vecs = lax.all_gather(vec_block, "shard", axis=1, tiled=True).astype(f32)
        up_all = lax.all_gather(up_weight, "shard", axis=0, tiled=True)
        down_all = lax.all_gather(down_weight, "shard", axis=0, tiled=True)
        up_down = jnp.concatenate(
            [
                up_all.reshape(16, 48, FF),
                down_all.reshape(16, 4, 48, D).transpose(0, 2, 1, 3).reshape(16, 48, FF),
            ],
            axis=1,
        )
    vecs = jnp.pad(vecs.astype(f32), ((0, 4), (0, 0)))

    lengths = lax.dynamic_slice_in_dim(doc_lengths, shard, 1, 0)[0]
    ends = jnp.cumsum(lengths).astype(jnp.int32)
    meta = jnp.concatenate([jnp.stack([x, z, y, c]), jnp.zeros((4,), jnp.int32), ends])
    spots = jnp.arange(2 * HALF, dtype=jnp.int32)
    spots = jnp.where(spots < HALF, spots + x * HALF, spots - x * HALF)
    passed = spots[:, None] >= ends[None, :]
    place = spots - jnp.sum(jnp.where(passed, lengths[None, :], 0), axis=1)
    frequency = rope_base ** (-jnp.arange(HD // 2, dtype=f32) * 2.0 / HD)
    angles = place.astype(f32)[:, None] * frequency[None, :]
    cosine = jnp.tile(jnp.cos(angles), (1, 4))
    sine = jnp.sin(angles)
    sine = jnp.concatenate([-sine, sine, -sine, sine], axis=1)

    q, k, kt, v, vt, w1 = qkv_call(meta, rows, rows_other, cosine, sine, first_pieces)
    att, att_t, lse = attend_call(meta, q, k, vt)
    res = branch_call(rows, att, w1)
    out, gnorm, vg_two, keep_g, send_g, keep_u, send_u, down_g = mlp_call(
        meta, res, cotangent[0], vecs, up_down, gate_pieces
    )
    marks = (
        jnp.arange(16, dtype=jnp.int32)[:, None] == jnp.arange(D, dtype=jnp.int32)[None, :] // HD
    ).astype(f32)
    g_one, g_low, att_g, delta, vg_one = norm_one_call(res, gnorm, vecs, att, w1, marks)
    delta = delta[:H].reshape(PAIRS, 2, HALF)
    stats = jnp.concatenate([lse, delta], axis=0)
    att_g_other = flip_x(att_g)
    stats_other = flip_x(stats)
    vec_grads = all_sum_small(jnp.concatenate([vg_one[:2], vg_two[:2]], axis=0), fast)

    dq, dk, dv = back_own_call(meta, q, k, kt, v, att_g, lse, delta, cosine, sine)
    dk, dv = back_other_call(
        meta, q, k, v, att_g_other, stats_other[:PAIRS], stats_other[PAIRS:], cosine, sine, dk, dv
    )
    keep_f, send_f = first_grads_call(meta, rows, att_t, dq, dk, dv, g_low)
    grad_in = tokens_grad_call(g_one, dq, dk, dv, w1)

    if fast:
        spot = (x, z, y)
        grad_gate = scatter_sum(keep_g, send_g, spot, False)
        grad_up = scatter_sum(keep_u, send_u, spot, True)
        grad_first = scatter_sum(keep_f, send_f, spot, True)
        grad_gate = jnp.concatenate([grad_gate[0], grad_gate[1]], axis=1)
        grad_up = jnp.concatenate([grad_up[0], grad_up[1]], axis=1)
        grad_first = jnp.concatenate([grad_first[0], grad_first[1]], axis=1)
        vec_own = lax.dynamic_slice_in_dim(vec_grads, shard * 48, 48, 1)
    else:
        def owned(a):
            part = lax.psum_scatter(a, "shard", scatter_dimension=0, tiled=True)
            return lax.psum(part, "seq").astype(f32)

        grad_gate = owned(whole_of_split(keep_g, send_g))
        grad_up = owned(whole_of_split(keep_u, send_u))
        grad_first = owned(whole_of_split(keep_f, send_f))
        vec_own = lax.dynamic_slice_in_dim(vec_grads, shard * (D // n), D // n, 1)
    down_part = lax.psum_scatter(down_g, "shard", scatter_dimension=0, tiled=True)
    grad_down = add(down_part, flip_x(down_part))
    return (
        out[None],
        grad_in[None],
        grad_first[:, : 3 * D],
        grad_first[:, 3 * D :],
        grad_gate,
        grad_up,
        grad_down,
        vec_own[0],
        vec_own[1],
        vec_own[2],
        vec_own[3],
    )


def solution(mesh):
    placed = (
        P("shard", "seq", None),
        P(),
        P("shard", None),
        P("shard", None),
        P("shard", None),
        P("shard", None),
        P("shard", None),
        P("shard"),
        P("shard"),
        P("shard"),
        P("shard"),
        P("shard", "seq", None),
    )
    return jax.shard_map(
        local,
        mesh=mesh,
        in_specs=placed,
        out_specs=(
            P("shard", "seq", None),
            P("shard", "seq", None),
            P("shard", None),
            P("shard", None),
            P("shard", None),
            P("shard", None),
            P("shard", None),
            P("shard"),
            P("shard"),
            P("shard"),
            P("shard"),
        ),
        check_vma=False,
    )
```

```python
from functools import partial

import jax
import jax.numpy as jnp
from jax import lax
from jax.experimental import pallas as pl
from jax.experimental.pallas import tpu as pltpu
from jax.sharding import PartitionSpec as P

D = 768
H = 12
HD = 64
FF = 3072
HALF = 512
PAIRS = H // 2
BLK = 768
HW = D // 2
GW = 2 * BLK + HW
MW = GW + 2 * BLK
GA = 1024
QW = 3 * HW + 128
MIB = 1 << 20

rope_base = 1000.0
norm_eps = 1e-05
big_negative = -1e30

bf16 = jnp.bfloat16
f32 = jnp.float32
VM = pl.BlockSpec(memory_space=pltpu.VMEM)
SM = pl.BlockSpec(memory_space=pltpu.SMEM)
HBM = pl.BlockSpec(memory_space=pl.ANY)


def dot(a, b):
    return lax.dot_general(a, b, (((1,), (0,)), ((), ())), preferred_element_type=f32)


def dot_t(a, b):
    return lax.dot_general(a, b, (((1,), (1,)), ((), ())), preferred_element_type=f32)


def params(mib):
    return pltpu.CompilerParams(vmem_limit_bytes=mib * MIB)


def cost(flops, moved, trans=0):
    return pl.CostEstimate(flops=int(flops), bytes_accessed=int(moved), transcendentals=int(trans))


def shape(dims, kind):
    return jax.ShapeDtypeStruct(dims, kind)


def piece_copies(meta, pieces, dst, sems):
    x, z, y, c = meta[4], meta[1], meta[2], meta[3]
    copies = []
    for at in range(8):
        dc, dy, dh = at // 4, (at // 2) % 2, at % 2
        h = jnp.where(x == 0, dh, 1 - dh)
        yy = jnp.where(y == 0, dy, 1 - dy)
        cc = jnp.where(c == 0, dc, 1 - dc)
        for k in range(4):
            zz = lax.rem(z - k + 4, 4)
            row = pl.multiple_of(((zz * 2 + yy) * 2 + cc) * 48, 48)
            copies.append(
                pltpu.make_async_copy(
                    pieces[at * 2 + k // 2].at[k % 2], dst.at[h, pl.ds(row, 48)], sems.at[at * 4 + k]
                )
            )
    return copies


def spin(u, cosine, sine):
    lane = lax.broadcasted_iota(jnp.int32, u.shape, 1)
    swapped = jnp.where(lane % HD < HD // 2, pltpu.roll(u, 96, 1), pltpu.roll(u, 32, 1))
    return u * cosine + swapped * sine


def qkv_kernel(meta, own, other, cosine, sine, *rest):
    pieces = rest[:4]
    q_out, k_out, kt_out, v_out, vt_out, w_out, vecs, w, sems, out_sem = rest[4:]
    step = pl.program_id(0)

    @pl.when(step == 0)
    def _():
        z, y, c = meta[1], meta[2], meta[3]
        copies = []
        for at, piece in enumerate(pieces):
            yy = jnp.where(y == 0, at % 2, 1 - at % 2)
            cc = jnp.where(c == 0, at // 2, 1 - at // 2)
            for k in range(4):
                zz = lax.rem(z - k + 4, 4)
                row = pl.multiple_of(((zz * 2 + yy) * 2 + cc) * 48, 48)
                copies.append(
                    pltpu.make_async_copy(piece.at[k], w.at[pl.ds(row, 48)], sems.at[at * 4 + k])
                )
        for copy in copies:
            copy.start()
        for copy in copies:
            copy.wait()
        pltpu.make_async_copy(w, w_out, out_sem).start()
        vecs[...] = w[:, 3 * HW :].astype(f32).T[:8]

    part = w[:, pl.ds(pl.multiple_of(step * HW, HW), HW)]
    for half, rows in enumerate((own, other)):
        at = slice(half * HALF, (half + 1) * HALF)
        cs, sn = cosine[at, :], sine[at, :]
        qkv = dot(rows[...], part)
        q_out[at, :] = spin(qkv[:, :128], cs, sn).astype(bf16)
        kr = spin(qkv[:, 128:256], cs, sn).astype(bf16)
        vs = qkv[:, 256:].astype(bf16)
        k_out[at, :] = kr
        kt_out[:, at] = kr.T
        v_out[at, :] = vs
        vt_out[:, at] = vs.T

    @pl.when(step == 2)
    def _():
        pltpu.make_async_copy(w, w_out, out_sem).wait()


def qkv_call(meta, own, other, cosine, sine, pieces):
    rows = 2 * HALF
    full = pl.BlockSpec((rows, 128), lambda i: (0, 0))
    x_spec = pl.BlockSpec((HALF, D), lambda i: (0, 0))
    nat = pl.BlockSpec((rows, 128), lambda i: (0, i))
    tr = pl.BlockSpec((128, rows), lambda i: (i, 0))
    return pl.pallas_call(
        qkv_kernel,
        grid=(3,),
        in_specs=[SM, x_spec, x_spec, full, full] + [HBM] * 4,
        out_specs=[nat, nat, tr, nat, tr, HBM, pl.BlockSpec((8, D), lambda i: (0, 0))],
        out_shape=[
            shape((rows, HW), bf16),
            shape((rows, HW), bf16),
            shape((HW, rows), bf16),
            shape((rows, HW), bf16),
            shape((HW, rows), bf16),
            shape((D, QW), bf16),
            shape((8, D), f32),
        ],
        scratch_shapes=[
            pltpu.VMEM((D, QW), bf16),
            pltpu.SemaphoreType.DMA((16,)),
            pltpu.SemaphoreType.DMA,
        ],
        compiler_params=params(62),
        cost_estimate=cost(2 * rows * D * 3 * HW, 14e6),
        name="qkv",
    )(meta, own, other, cosine, sine, *pieces)


def segment_of(meta, pos):
    seg = jnp.zeros(pos.shape, jnp.int32)
    for d in range(8):
        seg = seg + jnp.where(pos >= meta[8 + d], 1, 0)
    return seg


def bias_of(meta, key_base, keys, query_base):
    row = lax.broadcasted_iota(jnp.int32, (keys, 128), 0)
    key_pos = jnp.where(row < HALF, row + key_base[0], row - HALF + key_base[1])
    key_seg = segment_of(meta, key_pos)[:, :1]
    key_pos = key_pos[:, :1]
    query_pos = lax.broadcasted_iota(jnp.int32, (8, HALF), 1) + query_base
    query_seg = segment_of(meta, query_pos)[:1]
    query_pos = query_pos[:1]
    near = jnp.abs(key_pos - query_pos) <= HALF
    return jnp.where((key_seg == query_seg) & near, 0.0, big_negative).astype(f32)


def head_part(block, hh, scale=None):
    lane = lax.broadcasted_iota(jnp.int32, block.shape, 1)
    kept = jnp.where((lane // HD) == hh, block, jnp.zeros_like(block))
    return kept if scale is None else kept * jnp.asarray(scale, block.dtype)


def bases(meta):
    return meta[0] * HALF, HALF - meta[0] * HALF


def attend_kernel(side, meta, q, k, vt, att, att_t, lse, bias):
    @pl.when(pl.program_id(0) == 0)
    def _():
        both = bases(meta)
        bias[...] = bias_of(meta, both, 2 * HALF, both[side])

    parts = []
    for hh in range(2):
        qz = head_part(q[...], hh, HD**-0.5)
        s = dot_t(k[...], qz) + bias[...]
        peak = jnp.max(s, axis=0, keepdims=True)
        e = jnp.exp(s - peak)
        total = jnp.sum(e, axis=0, keepdims=True)
        o = dot(vt[hh * HD : (hh + 1) * HD, :], e.astype(bf16)) * (1.0 / total)
        parts.append(o.astype(bf16))
        lse[0, hh : hh + 1, :] = peak + jnp.log(total)
    both = jnp.concatenate(parts, axis=0)
    att_t[...] = both
    att[...] = both.T


def attend_call(meta, q, k, vt, side):
    return pl.pallas_call(
        partial(attend_kernel, side),
        grid=(3,),
        in_specs=[
            SM,
            pl.BlockSpec((HALF, 128), lambda i: (side, i)),
            pl.BlockSpec((2 * HALF, 128), lambda i: (0, i)),
            pl.BlockSpec((128, 2 * HALF), lambda i: (i, 0)),
        ],
        out_specs=[
            pl.BlockSpec((HALF, 128), lambda i: (0, i)),
            pl.BlockSpec((128, HALF), lambda i: (i, 0)),
            pl.BlockSpec((1, 2, HALF), lambda i: (i, 0, 0)),
        ],
        out_shape=[
            shape((HALF, HW), bf16),
            shape((HW, HALF), bf16),
            shape((3, 2, HALF), f32),
        ],
        scratch_shapes=[pltpu.VMEM((2 * HALF, HALF), f32)],
        compiler_params=params(62),
        cost_estimate=cost(4 * 4 * 6 * 2 * HALF * HALF * HD, 4e6, 6 * 2 * HALF * HALF),
        name="attend",
    )(meta, q, k, vt)


def attend_back_kernel(
    meta, q, k, kt, v, g_own, g_other, at_own, at_other, lse_own, lse_other, cosine, sine, grads, bias,
):
    @pl.when(pl.program_id(0) == 0)
    def _():
        both = bases(meta)
        for side in range(2):
            bias[side] = bias_of(meta, both, 2 * HALF, both[side])

    dk = dv = None
    for side, (g, at, lse) in enumerate(((g_own, at_own, lse_own), (g_other, at_other, lse_other))):
        rows = slice(side * HALF, (side + 1) * HALF)
        prod = g[...].T.astype(f32) * at[...].astype(f32)
        parts = []
        for hh in range(2):
            qz = head_part(q[rows, :], hh, HD**-0.5)
            gz = head_part(g[...], hh)
            delta = jnp.sum(prod[hh * HD : (hh + 1) * HD, :], axis=0, keepdims=True)
            s = dot_t(k[...], qz) + bias[side]
            p = jnp.exp(s - lse[0, hh : hh + 1, :])
            dp = dot_t(v[...], gz)
            ds = (p * (dp - delta)).astype(bf16)
            parts.append(dot(kt[hh * HD : (hh + 1) * HD, :], ds) * HD**-0.5)
            gk, gv = dot(ds, qz), dot(p.astype(bf16), gz)
            dk, dv = (gk, gv) if dk is None else (dk + gk, dv + gv)
        dq = jnp.concatenate(parts, axis=0).T
        grads[rows, :128] = spin(dq, cosine[rows, :], -sine[rows, :]).astype(bf16)
    grads[:, 128:256] = spin(dk, cosine[...], -sine[...]).astype(bf16)
    grads[:, 256:] = dv.astype(bf16)


def attend_back_call(meta, q, k, kt, v, g_own, g_other, at_own, at_other, lse_own, lse_other, cosine, sine, begin, count, done=None):
    nat = pl.BlockSpec((HALF, 128), lambda i: (0, begin + i))
    wide = pl.BlockSpec((2 * HALF, 128), lambda i: (0, begin + i))
    tall = pl.BlockSpec((128, HALF), lambda i: (begin + i, 0))
    row = pl.BlockSpec((1, 2, HALF), lambda i: (begin + i, 0, 0))
    table = pl.BlockSpec((2 * HALF, 128), lambda i: (0, 0))
    extra = () if done is None else (done,)

    def kernel(*refs):
        attend_back_kernel(*refs[:13], *refs[13 + len(extra) :])

    return pl.pallas_call(
        kernel,
        grid=(count,),
        in_specs=[
            SM, wide, wide, pl.BlockSpec((128, 2 * HALF), lambda i: (begin + i, 0)), wide,
            nat, nat, tall, tall, row, row, table, table,
        ] + [HBM] * len(extra),
        out_specs=pl.BlockSpec((2 * HALF, HW), lambda i: (0, begin + i)),
        out_shape=shape((2 * HALF, 3 * HW), bf16),
        input_output_aliases={13: 0} if extra else {},
        scratch_shapes=[pltpu.VMEM((2, 2 * HALF, HALF), f32)],
        compiler_params=params(62),
        cost_estimate=cost(4 * 10 * 2 * count * 4 * HALF * HALF * HD, 12e6, 2 * count * 4 * HALF * HALF),
        name="attend_back",
    )(meta, q, k, kt, v, g_own, g_other, at_own, at_other, lse_own, lse_other, cosine, sine, *extra)


def norm_parts(r):
    centered = r - jnp.mean(r, axis=-1, keepdims=True)
    scale = lax.rsqrt(jnp.mean(centered * centered, axis=-1, keepdims=True) + norm_eps)
    return centered * scale, scale


def norm_back(c, z, scale, gain):
    e = c * gain
    return (e - jnp.mean(e, axis=-1, keepdims=True) - z * jnp.mean(e * z, axis=-1, keepdims=True)) * scale


def split_core(c, val):
    parts = val.astype(bf16).reshape(8, 2, 48, val.shape[1])
    return (
        jnp.where(c == 0, parts[:, 0], parts[:, 1]),
        jnp.where(c == 0, parts[:, 1], parts[:, 0]),
    )


def whole(dims):
    return pl.BlockSpec(dims, lambda i: (0,) * len(dims))


NAT = whole((HALF, D))
PART = pl.BlockSpec((1, HALF, BLK), lambda i: (i % 4, 0, 0))
WIDE = pl.BlockSpec((1, D, BLK), lambda i: ((i % 4) // 2, 0, i % 2))
DOWN = pl.BlockSpec((BLK, D), lambda i: (i % 4, 0))
HEADS = whole((HALF, HW))


def hidden_kernel(meta, rows, mine, theirs, vecs, *rest):
    res, low, low_t, att_t, hid, a_out, b_out, w_out, w, sems, out_sem = rest[16:]
    step = pl.program_id(0)
    copies = piece_copies(meta, rest[:16], w, sems)
    save = pltpu.make_async_copy(w, w_out, out_sem)

    @pl.when(step == 0)
    def _():
        for copy in copies:
            copy.start()
        first = meta[0] == 0
        m, t = mine[...], theirs[...]
        left, right = jnp.where(first, m, t), jnp.where(first, t, m)
        att_t[:HW, :] = left.T
        att_t[HW:, :] = right.T
        att = jnp.concatenate([left, right], axis=1)
        for copy in copies:
            copy.wait()
        save.start()
        branch = jnp.concatenate(
            [dot(att, w[0, :, 2 * BLK : GW]), dot(att, w[1, :, 2 * BLK : GW])], axis=1
        )
        r = rows[...].astype(f32) + branch
        res[...] = r
        z, _ = norm_parts(r)
        n1 = (z * vecs[0:1, :] + vecs[1:2, :]).astype(bf16)
        low[...] = n1
        low_t[...] = n1.T

    half = step // 2
    at = (step % 2) * BLK
    g = dot(low[...], w[half, :, pl.ds(pl.multiple_of(at, BLK), BLK)])
    u = dot(low[...], w[half, :, pl.ds(pl.multiple_of(GW + at, HW), BLK)])
    sig = 1.0 / (1.0 + jnp.exp(-g))
    gs = g * sig
    hid[0] = (gs * u).astype(bf16)
    a_out[0] = (u * (sig + gs * (1.0 - sig))).astype(bf16)
    b_out[0] = gs.astype(bf16)

    @pl.when(step == 3)
    def _():
        save.wait()


def hidden_call(meta, rows, mine, theirs, vecs, pieces):
    part = shape((4, HALF, BLK), bf16)
    return pl.pallas_call(
        hidden_kernel,
        grid=(4,),
        in_specs=[SM, NAT, HEADS, HEADS, whole((8, D))] + [HBM] * 16,
        out_specs=[NAT, NAT, whole((D, HALF)), whole((D, HALF)), PART, PART, PART, HBM],
        out_shape=[
            shape((HALF, D), f32),
            shape((HALF, D), bf16),
            shape((D, HALF), bf16),
            shape((D, HALF), bf16),
            part,
            part,
            part,
            shape((2, D, MW), bf16),
        ],
        scratch_shapes=[
            pltpu.VMEM((2, D, MW), bf16),
            pltpu.SemaphoreType.DMA((32,)),
            pltpu.SemaphoreType.DMA,
        ],
        compiler_params=params(62),
        cost_estimate=cost(2 * HALF * D * (2 * FF + D), 30e6, HALF * FF),
        name="hidden",
    )(meta, rows, mine, theirs, vecs, *pieces)


def down_copies(meta, pieces, dst, sems):
    z, y, c = meta[1], meta[2], meta[3]
    copies = []
    for at, piece in enumerate(pieces):
        dc, k = at // 4, at % 4
        zz = lax.rem(z - k + 4, 4)
        cc = jnp.where(c == 0, dc, 1 - dc)
        for dy in range(2):
            yy = jnp.where(y == 0, dy, 1 - dy)
            row = pl.multiple_of(((zz * 2 + yy) * 2 + cc) * 192, 192)
            copies.append(
                pltpu.make_async_copy(piece.at[dy], dst.at[pl.ds(row, 192)], sems.at[at * 2 + dy])
            )
    return copies


def output_kernel(meta, res, cot, vecs, hid, *rest):
    pieces = rest[:8]
    out, g_two, m, vgrads, keep, send, wd_out, acc, held, ms, wd, sems, out_sem = rest[8:]
    step = pl.program_id(0)
    copies = down_copies(meta, pieces, wd, sems)
    save = pltpu.make_async_copy(wd, wd_out, out_sem)

    @pl.when(step == 0)
    def _():
        for copy in copies:
            copy.start()
        for copy in copies:
            copy.wait()
        save.start()

    @pl.when(step == 7)
    def _():
        save.wait()

    @pl.when(step < 4)
    def _():
        held[step] = hid[0]
        part = dot(hid[0], wd[pl.ds(pl.multiple_of(step * BLK, BLK), BLK), :])

        @pl.when(step == 0)
        def _():
            z, _ = norm_parts(res[...])
            acc[...] = z * vecs[0:1, :] + vecs[1:2, :] + part

        @pl.when(step > 0)
        def _():
            acc[...] += part

    @pl.when(step == 3)
    def _():
        z, scale = norm_parts(acc[...])
        out[...] = (z * vecs[2:3, :] + vecs[3:4, :]).astype(bf16)
        c = cot[...].astype(f32)
        vgrads[0:1, :] = jnp.sum(c * z, axis=0, keepdims=True)
        vgrads[1:2, :] = jnp.sum(c, axis=0, keepdims=True)
        back = norm_back(c, z, scale, vecs[2:3, :])
        g_two[...] = back
        m[...] = back.astype(bf16)
        ms[...] = back.astype(bf16)

    @pl.when(step >= 4)
    def _():
        val = lax.dot_general(
            held[step - 4], ms[...], (((0,), (0,)), ((), ())), preferred_element_type=f32
        )
        c = meta[3]
        parts = val.astype(bf16).reshape(2, 2, 2, 96, D)
        for y in range(2):
            for h in range(2):
                keep[h, 0, y] = jnp.where(c == 0, parts[y, 0, h], parts[y, 1, h])
                send[h, 0, y] = jnp.where(c == 0, parts[y, 1, h], parts[y, 0, h])


def output_call(meta, res, cot, vecs, hid, pieces):
    grad = pl.BlockSpec((2, 1, 2, 96, D), lambda i: (0, jnp.maximum(i - 4, 0), 0, 0, 0))
    gshape = shape((2, 4, 2, 96, D), bf16)
    first = lambda i: jnp.minimum(i, 3)
    return pl.pallas_call(
        output_kernel,
        grid=(8,),
        in_specs=[
            SM,
            NAT,
            NAT,
            whole((8, D)),
            pl.BlockSpec((1, HALF, BLK), lambda i: (first(i), 0, 0)),
        ]
        + [HBM] * 8,
        out_specs=[NAT, NAT, NAT, whole((8, D)), grad, grad, HBM],
        out_shape=[
            shape((HALF, D), bf16),
            shape((HALF, D), f32),
            shape((HALF, D), bf16),
            shape((8, D), f32),
            gshape,
            gshape,
            shape((FF, D), bf16),
        ],
        scratch_shapes=[
            pltpu.VMEM((HALF, D), f32),
            pltpu.VMEM((4, HALF, BLK), bf16),
            pltpu.VMEM((HALF, D), bf16),
            pltpu.VMEM((FF, D), bf16),
            pltpu.SemaphoreType.DMA((16,)),
            pltpu.SemaphoreType.DMA,
        ],
        compiler_params=params(62),
        cost_estimate=cost(2 * 2 * HALF * D * FF, 20e6),
        name="output",
    )(meta, res, cot, vecs, hid, *pieces)


def back_kernel(last, m, a, b, wg, wu0, wu1, wd, so_far, *rest):
    step = pl.program_id(0)
    if last:
        meta, res, vecs, w_out, gate_g, up_g, g_one, low, mine, theirs, vgrads, acc = rest
    else:
        gate_g, up_g, acc = rest
    hg = dot_t(m[...], wd[...])
    gg = (hg * a[0].astype(f32)).astype(bf16)
    ug = (hg * b[0].astype(f32)).astype(bf16)
    gate_g[0] = gg
    up_g[0] = ug
    part = dot_t(gg, wg[0]) + dot_t(ug[:, :HW], wu0[0]) + dot_t(ug[:, HW:], wu1[0])

    @pl.when(step == 0)
    def _():
        acc[...] = so_far[...] + part

    @pl.when(step == 1)
    def _():
        acc[...] += part

    if last:

        @pl.when(step == 1)
        def _():
            z, scale = norm_parts(res[...])
            c = acc[...]
            vgrads[0:1, :] = jnp.sum(c * z, axis=0, keepdims=True)
            vgrads[1:2, :] = jnp.sum(c, axis=0, keepdims=True)
            back = norm_back(c, z, scale, vecs[0:1, :])
            g_one[...] = back
            back = back.astype(bf16)
            low[...] = back
            ag = (dot_t(back[:, :HW], w_out[0]) + dot_t(back[:, HW:], w_out[1])).astype(bf16)
            first = meta[0] == 0
            mine[...] = jnp.where(first, ag[:, :HW], ag[:, HW:])
            theirs[...] = jnp.where(first, ag[:, HW:], ag[:, :HW])


def back_call(m, a, b, w, wd, so_far, ends=None):
    last = ends is not None
    at = 2 if last else 0
    part = pl.BlockSpec((1, HALF, BLK), lambda i: (i + at, 0, 0))
    grad = pl.BlockSpec((1, HALF, BLK), lambda i: (i, 0, 0))
    wide = pl.BlockSpec((1, D, BLK), lambda i: (at // 2, 0, i))
    ups = [pl.BlockSpec((1, D, HW), lambda i, k=k: (at // 2, 0, GW // HW + 2 * i + k)) for k in range(2)]
    in_specs = [NAT, part, part, wide, *ups, pl.BlockSpec((BLK, D), lambda i: (i + at, 0)), NAT]
    out_specs = [grad, grad]
    out_shape = [shape((2, HALF, BLK), bf16)] * 2
    if last:
        in_specs += [SM, NAT, whole((8, D)), pl.BlockSpec((2, D, HW), lambda i: (0, 0, 4))]
        out_specs += [NAT, NAT, HEADS, HEADS, whole((8, D))]
        out_shape += [
            shape((HALF, D), f32),
            shape((HALF, D), bf16),
            shape((HALF, HW), bf16),
            shape((HALF, HW), bf16),
            shape((8, D), f32),
        ]
        scratch = [pltpu.VMEM((HALF, D), f32)]
    else:
        out_specs.append(NAT)
        out_shape.append(shape((HALF, D), f32))
        scratch = []
    return pl.pallas_call(
        partial(back_kernel, last),
        grid=(2,),
        in_specs=in_specs,
        out_specs=out_specs,
        out_shape=out_shape,
        scratch_shapes=scratch,
        compiler_params=params(62),
        cost_estimate=cost(2 * HALF * D * 3 * FF / 2, 18e6),
        name="back",
    )(m, a, b, w, w, w, wd, so_far, *(ends or ()))


def wide_grads_kernel(width, meta, low_t, first, second, *rest):
    step = pl.program_id(0)
    c = meta[3]
    keep, send = rest[-2:]

    def put(at, val):
        stay, leave = split_core(c, val)
        cols = slice(at, at + val.shape[1])
        for z in range(4):
            for y in range(2):
                keep[0, z, y, :, cols] = stay[2 * z + y]
                send[0, z, y, :, cols] = leave[2 * z + y]

    for h, grad in enumerate((first, second)):

        @pl.when(step == h)
        def _():
            for i in range(2):
                put(i * BLK, dot(low_t[...], grad[i]))

    if width == GW:
        put(2 * BLK, dot(rest[0][...], rest[1][...]))


def wide_grads_call(meta, low_t, first, second, *out_part):
    width = GW if out_part else 2 * BLK
    tall = whole((D, HALF))
    halves_spec = whole((2, HALF, BLK))
    grad = pl.BlockSpec((1, 4, 2, 48, width), lambda i: (i, 0, 0, 0, 0))
    extra = [tall, pl.BlockSpec((HALF, HW), lambda i: (0, i))] if out_part else []
    return pl.pallas_call(
        partial(wide_grads_kernel, width),
        grid=(2,),
        in_specs=[SM, tall, halves_spec, halves_spec] + extra,
        out_specs=[grad] * 2,
        out_shape=[shape((2, 4, 2, 48, width), bf16)] * 2,
        compiler_params=params(62),
        cost_estimate=cost(2 * HALF * D * FF, 9e6),
        name="wide_grads",
    )(meta, low_t, first, second, *out_part)


def first_grads_kernel(meta, own, other, grads, vg_one, vg_two, keep, send, rows_t):
    step = pl.program_id(0)

    @pl.when(step == 0)
    def _():
        rows_t[:, :HALF] = own[...].T
        rows_t[:, HALF:] = other[...].T
        row = lax.broadcasted_iota(jnp.int32, (8, D), 0)
        four = jnp.where(row < 2, vg_one[...], jnp.roll(vg_two[...], 2, axis=0))
        four = jnp.where(row < 4, four, 0.0)
        four = jnp.concatenate([four, jnp.zeros((120, D), f32)], axis=0).T
        keep[:, :, 3 * HW :], send[:, :, 3 * HW :] = split_core(meta[3], four)

    for j in range(3):

        @pl.when(step == j)
        def _():
            at = slice(j * HW, (j + 1) * HW)
            keep[:, :, at], send[:, :, at] = split_core(meta[3], dot(rows_t[...], grads[...]))


def first_grads_call(meta, own, other, grads, vg_one, vg_two):
    grad = whole((8, 48, QW))
    return pl.pallas_call(
        first_grads_kernel,
        grid=(3,),
        in_specs=[SM, NAT, NAT, pl.BlockSpec((2 * HALF, HW), lambda i: (0, i)), whole((8, D)), whole((8, D))],
        out_specs=[grad] * 2,
        out_shape=[shape((8, 48, QW), bf16)] * 2,
        scratch_shapes=[pltpu.VMEM((D, 2 * HALF), bf16)],
        compiler_params=params(62),
        cost_estimate=cost(2 * 2 * HALF * D * 3 * HW, 8e6),
        name="first_grads",
    )(meta, own, other, grads, vg_one, vg_two)


def tokens_part_kernel(grads, w, out):
    out[...] = dot_t(grads[...], w[:, : 3 * HW]).astype(out.dtype)


def tokens_part_call(grads, w):
    return pl.pallas_call(
        tokens_part_kernel,
        grid=(2,),
        in_specs=[pl.BlockSpec((HALF // 2, 3 * HW), lambda i: (i + 2, 0)), whole((D, QW))],
        out_specs=pl.BlockSpec((HALF // 2, D), lambda i: (i, 0)),
        out_shape=shape((HALF, D), bf16),
        compiler_params=params(62),
        cost_estimate=cost(2 * HALF * D * 3 * HW, 5e6),
        name="tokens_part",
    )(grads, w)


def tokens_grad_kernel(g_one, theirs, grads, w, out):
    out[...] = g_one[...] + theirs[...].astype(f32) + dot_t(grads[...], w[:, : 3 * HW])


def tokens_grad_call(g_one, theirs, grads, w):
    part = pl.BlockSpec((HALF // 2, D), lambda i: (i, 0))
    return pl.pallas_call(
        tokens_grad_kernel,
        grid=(2,),
        in_specs=[part, part, pl.BlockSpec((HALF // 2, 3 * HW), lambda i: (i, 0)), whole((D, QW))],
        out_specs=part,
        out_shape=shape((HALF, D), f32),
        compiler_params=params(62),
        cost_estimate=cost(2 * HALF * D * 3 * HW, 8e6),
        name="tokens_grad",
    )(g_one, theirs, grads, w)


def pick(a, at, axis):
    return lax.dynamic_index_in_dim(a, at, axis, keepdims=False)


def flip_x(a):
    return lax.ppermute(a, "seq", [(0, 1), (1, 0)])


def flip(bit):
    def go(a):
        n = lax.axis_size("shard")
        return lax.ppermute(a, "shard", [(s, s ^ bit) for s in range(n)])

    return go


flip_c, flip_y = flip(1), flip(2)


def turn_z(a, k):
    return lax.ppermute(a, "shard", [(s, (s + 4 * k) % 16) for s in range(16)])


def after(a, *deps):
    return lax.optimization_barrier((a,) + deps)[0]


def slot(*arrays):
    return lax.optimization_barrier(arrays)


def around(mine):
    return [turn_z(mine, k) for k in (1, 2, 3)]


def pieces_of_whole(full):
    cut = full.reshape(full.shape[0], 4, 2, 2, 48, full.shape[2])
    order = jnp.array([0, 3, 2, 1])
    return [
        cut[dh, :, dy, dc][order]
        for dc in range(2)
        for dy in range(2)
        for dh in range(full.shape[0])
    ]


def in_two(pieces):
    return [part for piece in pieces for part in (piece[:2], piece[2:])]


def add(a, b):
    return a.astype(f32) + b.astype(f32)


def turns(sends):
    return [turn_z(send, k + 1) for k, send in enumerate(sends)]


def fold(meta, ins, outs, name):
    def kernel(*refs):
        spot = refs[0][0], refs[0][1], refs[0][2]
        for (_, give), out in zip(outs, refs[1 + len(ins) :]):
            out[...] = give(spot, *refs[1 : 1 + len(ins)]).astype(bf16)

    moved = 2 * sum(a.size for a in ins)
    return pl.pallas_call(
        kernel,
        grid=(1,),
        in_specs=[SM] + [whole(a.shape) for a in ins],
        out_specs=[whole(dims) for dims, _ in outs],
        out_shape=[shape(dims, bf16) for dims, _ in outs],
        compiler_params=params(62),
        cost_estimate=cost(moved, 2 * moved),
        name=name,
    )(meta, *ins)


def cut_core(rows, cols_x, cols_y):
    def along_x(flip):
        def give(spot, keep, got):
            at = spot[0] if flip == 0 else 1 - spot[0]
            return add(keep[at, :, :, :, :cols_x], got[at, :, :, :, :cols_x])

        return give

    def along_y(flip):
        def give(spot, keep, got):
            at = spot[2] if flip == 0 else 1 - spot[2]
            return add(keep[:, :, at, :, cols_x:], got[:, :, at, :, cols_x:])

        return give

    dims_x, dims_y = (4, 2, rows, cols_x), (2, 4, rows, cols_y)
    return [(dims_x, along_x(0)), (dims_x, along_x(1)), (dims_y, along_y(0)), (dims_y, along_y(1))]


def cut_plane(rows, cols_x, cols_y, first):
    def along_y(flip):
        def give(spot, *refs):
            at = spot[2] if flip == 0 else 1 - spot[2]
            return add(refs[first][:, at], refs[first + 1][:, at])

        return give

    def along_x(flip):
        def give(spot, *refs):
            at = spot[0] if flip == 0 else 1 - spot[0]
            return add(refs[first + 2][at], refs[first + 3][at])

        return give

    dims_a, dims_b = (4, rows, cols_x), (4, rows, cols_y)
    return [(dims_a, along_y(0)), (dims_a, along_y(1)), (dims_b, along_x(0)), (dims_b, along_x(1))]


def cut_line(rows, cols, first, count):
    def part(k):
        def give(spot, *refs):
            at = lax.rem(spot[1] + k, 4)
            sums = [
                add(refs[first + 2 * i][at], refs[first + 2 * i + 1][at]) for i in range(count)
            ]
            return sums[0] if count == 1 else jnp.concatenate(sums, axis=-1)

        return give

    return [((rows, cols), part(k)) for k in range(4)]


def total_of(rows, cols, first):
    def give(spot, *refs):
        near, *gots = [refs[first + i][...].astype(f32) for i in range(4)]
        return near + gots[0] + gots[1] + gots[2]

    return [((rows, cols), give)]


def halves(mine, other, x):
    return jnp.where(x == 0, jnp.stack([mine, other]), jnp.stack([other, mine])).astype(f32)


def whole_of_split(keep, send):
    both = jnp.stack([keep, send], axis=3)
    return both.transpose(1, 2, 3, 4, 0, 5).reshape(D, -1)


def whole_of_down(keep, send):
    return jnp.stack([keep, send], axis=3).transpose(1, 2, 3, 0, 4, 5).reshape(FF, D)


def local(
    tokens,
    doc_lengths,
    qkv_weight,
    out_weight,
    gate_weight,
    up_weight,
    down_weight,
    norm1_gain,
    norm1_bias,
    norm2_gain,
    norm2_bias,
    cotangent,
):
    n = lax.axis_size("shard")
    fast = n == 16
    x = lax.axis_index("seq").astype(jnp.int32)
    shard = lax.axis_index("shard").astype(jnp.int32)
    zero = jnp.zeros((), jnp.int32)
    z, y, c = (shard // 4, (shard // 2) % 2, shard % 2) if fast else (zero, zero, zero)

    rows = tokens[0]
    cot = cotangent[0]
    lengths = lax.dynamic_slice_in_dim(doc_lengths, shard, 1, 0)[0]
    ends = jnp.cumsum(lengths).astype(jnp.int32)
    hx = x if fast else zero
    meta = jnp.concatenate([jnp.stack([x, z, y, c, hx]), jnp.zeros((3,), jnp.int32), ends])
    spots = jnp.arange(2 * HALF, dtype=jnp.int32)
    spots = jnp.where(spots < HALF, spots + x * HALF, spots - x * HALF)
    passed = spots[:, None] >= ends[None, :]
    place = spots - jnp.sum(jnp.where(passed, lengths[None, :], 0), axis=1)
    frequency = rope_base ** (-jnp.arange(HD // 2, dtype=f32) * 2.0 / HD)
    angles = place.astype(f32)[:, None] * frequency[None, :]
    cosine = jnp.tile(jnp.cos(angles), (1, 4))
    sine = jnp.sin(angles)
    sine = jnp.concatenate([-sine, sine, -sine, sine], axis=1)

    vec_block = jnp.stack([norm1_gain, norm1_bias, norm2_gain, norm2_bias], axis=1)
    vec_block = jnp.pad(vec_block, ((0, 0), (0, 124)))

    def my_heads(w):
        mine = lax.dynamic_slice_in_dim(w.reshape(w.shape[0], 3, 2, HW), x, 1, 2)
        mine = mine.reshape(w.shape[0], 3, 3, 128).transpose(0, 2, 1, 3)
        return mine.reshape(w.shape[0], 3 * HW)

    def half_of(w):
        cols = w.shape[1] // 2
        return jnp.where(x == 0, w[:, :cols], w[:, cols:])

    if fast:
        first = jnp.concatenate([my_heads(qkv_weight), vec_block], axis=1)
        wide = jnp.concatenate([half_of(gate_weight), half_of(out_weight), half_of(up_weight)], axis=1)
        zq, yd, wide1 = around(first), flip_y(down_weight), turn_z(wide, 1)
        first, zq, wide_late, cosine, sine, rows_late, yd = slot(
            first, zq, wide, cosine, sine, rows, yd
        )
        aq = jnp.stack([first] + zq)
        byq, rows_other = flip_y(aq), flip_x(rows_late)
        wide2, wide3 = turn_z(wide_late, 2), turn_z(wide_late, 3)
        aq, byq, wide, wide1, wide3, down, yd = slot(aq, byq, wide, wide1, wide3, down_weight, yd)
        a0 = jnp.stack([wide, wide1])
        d0 = jnp.stack([down, yd])
        caq, cbyq = flip_c(aq), flip_c(byq)
        caq, cbyq, a0, rows_other, d0 = slot(caq, cbyq, a0, rows_other, d0)
        by0, bx0 = flip_y(a0), flip_x(a0)
        first_pieces = [aq, byq, caq, cbyq]
    else:
        rows_other = flip_x(rows)

        def gathered(w):
            return lax.all_gather(w, "shard", axis=0, tiled=True)

        first = jnp.concatenate([my_heads(gathered(qkv_weight)), gathered(vec_block)], axis=1)
        first_pieces = pieces_of_whole(first[None])

        def in_halves(w):
            return gathered(w).reshape(D, 2, -1).transpose(1, 0, 2)

        wide_all = jnp.concatenate([in_halves(w) for w in (gate_weight, out_weight, up_weight)], axis=2)
        pieces = in_two(pieces_of_whole(wide_all))
        down_all = gathered(down_weight).reshape(4, 2, 2, 192, D)
        down_pieces = [down_all[(4 - k) % 4, :, dc] for dc in range(2) for k in range(4)]

    q, k, kt, v, vt, w1, vecs = qkv_call(meta, rows, rows_other, cosine, sine, first_pieces)
    if fast:
        q, a0, by0, bx0, wide2, d0 = slot(q, a0, by0, bx0, wide2, d0)
        a1 = jnp.stack([wide2, wide3])
        q, a1 = slot(q, a1)
        by1, bx1, d1 = flip_y(a1), flip_x(a1), turn_z(d0, 1)
        ca0, cby0 = flip_c(a0), flip_c(by0)
    att_theirs, at_other, lse_other = attend_call(meta, q, k, vt, 1)
    if fast:
        q, att_theirs, by1, bx1, ca0, cby0, d1, by0, bx0, a1 = slot(
            q, att_theirs, by1, bx1, ca0, cby0, d1, by0, bx0, a1
        )
    att_got = flip_x(att_theirs)
    if fast:
        bxy0, bxy1, d2 = flip_x(by0), flip_y(bx1), turn_z(d1, 1)
        cbx0 = flip_c(bx0)
    att_mine, at_own, lse_own = attend_call(meta, q, k, vt, 0)
    if fast:
        att_mine, att_got, bxy0, bxy1, d2, cbx0, by1, a1, bx1 = slot(
            att_mine, att_got, bxy0, bxy1, d2, cbx0, by1, a1, bx1
        )
        cby1 = flip_c(by1)
        cbx1, cbxy0, cbxy1, ca1 = flip_c(bx1), flip_c(bxy0), flip_c(bxy1), flip_c(a1)
        att_mine, cbx1, cby1, cbxy0, cbxy1, ca1, d0, d1, d2 = slot(
            att_mine, cbx1, cby1, cbxy0, cbxy1, ca1, d0, d1, d2
        )
        d3, cd0, cd1, cd2 = turn_z(d2, 1), flip_c(d0), flip_c(d1), flip_c(d2)
        pieces = [a0, a1, bx0, bx1, by0, by1, bxy0, bxy1]
        pieces += [ca0, ca1, cbx0, cbx1, cby0, cby1, cbxy0, cbxy1]
    res, low, low_t, att_t, hid, part_a, part_b, w2 = hidden_call(
        meta, rows, att_mine, att_got, vecs, pieces
    )
    if fast:
        hid, d3, cd0, cd1, cd2 = slot(hid, d3, cd0, cd1, cd2)
        down_pieces = [d0, d1, d2, d3, cd0, cd1, cd2, flip_c(d3)]
    out, g_two, m, vg_two, keep_d, send_d, wd = output_call(meta, res, cot, vecs, hid, down_pieces)

    if fast:
        keep_d, send_d, m = slot(keep_d, send_d, m)
        got_d = flip_c(send_d)
    gate_g0, up_g0, acc = back_call(m, part_a, part_b, w2, wd, g_two)
    if fast:
        got_d, acc = slot(got_d, acc)
        near_da, sent_da, near_db, sent_db = fold(meta, (keep_d, got_d), cut_core(96, HW, HW), "fold")
        acc, sent_da, sent_db = slot(acc, sent_da, sent_db)
        got_da, got_db = flip_x(sent_da), flip_y(sent_db)
    gate_g1, up_g1, g_one, g_low, g_mine, g_theirs, vg_one = back_call(
        m, part_a, part_b, w2, wd, acc, (meta, res, vecs, w2)
    )
    if fast:
        g_theirs, g_low, got_da, got_db = slot(g_theirs, g_low, got_da, got_db)
        near_da, sent_da, near_db, sent_db = fold(
            meta, (near_da, got_da, near_db, got_db), cut_plane(96, HW, HW, 0), "fold"
        )
        g_low, sent_da, sent_db, g_theirs = slot(g_low, sent_da, sent_db, g_theirs)
        got_da = flip_y(sent_da)
    g_other = flip_x(g_theirs)
    keep_g, send_g = wide_grads_call(meta, low_t, gate_g0, gate_g1, att_t, g_low)
    if fast:
        send_g, g_other, got_da, up_g1 = slot(send_g, g_other, got_da, up_g1)
        got_g, got_db = flip_c(send_g), flip_x(sent_db)
    keep_u, send_u = wide_grads_call(meta, low_t, up_g0, up_g1)
    if fast:
        send_u, got_g, got_db, g_other = slot(send_u, got_g, got_db, g_other)
        near_ga, sent_ga, near_gb, sent_gb, near_d, *sent_d = fold(
            meta,
            (keep_g, got_g, near_da, got_da, near_db, got_db),
            [(dims, lambda spot, *refs, give=give: give(spot, *refs[:2])) for dims, give in cut_core(48, GA, GW - GA)]
            + cut_line(96, D, 2, 2),
            "fold",
        )
        sent_ga, sent_gb, g_other, sent_d, send_u = slot(sent_ga, sent_gb, g_other, sent_d, send_u)
        got_ga, got_gb, got_u = flip_x(sent_ga), flip_y(sent_gb), flip_c(send_u)
        got_d1, got_d3 = turn_z(sent_d[0], 1), turn_z(sent_d[2], 3)
    back_args = (q, k, kt, v, g_mine, g_other, at_own, at_other, lse_own, lse_other, cosine, sine)
    grads = attend_back_call(meta, *back_args, 0, 2)
    if fast:
        grads, got_ga, got_gb, got_u, got_d1, got_d3 = slot(grads, got_ga, got_gb, got_u, got_d1, got_d3)
        near_ga, sent_ga, near_gb, sent_gb, near_ua, sent_ua, near_ub, sent_ub = fold(
            meta,
            (keep_u, got_u, near_ga, got_ga, near_gb, got_gb),
            cut_plane(48, GA, GW - GA, 2)
            + [(dims, lambda spot, *refs, give=give: give(spot, *refs[:2])) for dims, give in cut_core(48, BLK, BLK)],
            "fold",
        )
        grads, sent_ua, sent_ub, sent_ga, sent_gb, sent_d = slot(
            grads, sent_ua, sent_ub, sent_ga, sent_gb, sent_d
        )
        got_ua, got_ub, got_d2 = flip_x(sent_ua), flip_y(sent_ub), turn_z(sent_d[1], 2)
    grads = attend_back_call(meta, *back_args, 2, 1, grads)
    if fast:
        grads, got_ua, got_ub, got_d2, sent_ga, sent_gb = slot(
            grads, got_ua, got_ub, got_d2, sent_ga, sent_gb
        )
        near_ua, sent_ua, near_ub, sent_ub, total_d = fold(
            meta,
            (near_ua, got_ua, near_ub, got_ub, near_d, got_d1, got_d2, got_d3),
            cut_plane(48, BLK, BLK, 0) + total_of(96, D, 4),
            "fold",
        )
        grads, sent_ga, sent_gb, sent_ua, sent_ub, total_d = slot(
            grads, sent_ga, sent_gb, sent_ua, sent_ub, total_d
        )
        got_ga, got_gb, got_ua, got_ub = flip_y(sent_ga), flip_x(sent_gb), flip_y(sent_ua), flip_x(sent_ub)
    keep_q, send_q = first_grads_call(meta, rows, rows_other, grads, vg_one, vg_two)
    if fast:
        keep_q, send_q, got_ga, got_gb, got_ua, got_ub, grads = slot(
            keep_q, send_q, got_ga, got_gb, got_ua, got_ub, grads
        )
        got_q = flip_c(send_q)
    theirs = tokens_part_call(grads, w1)
    if fast:
        got_q, theirs = slot(got_q, theirs)
        cut = (4, 2, 48, QW)
        outs = cut_line(48, GW, 2, 2) + cut_line(48, 2 * BLK, 6, 2)
        outs += [
            ((4, 48, QW), lambda spot, keep, got, *_: add(keep[:, spot[2]], got[:, spot[2]])),
            ((4, 48, QW), lambda spot, keep, got, *_: add(keep[:, 1 - spot[2]], got[:, 1 - spot[2]])),
        ]
        near_g, *rest = fold(
            meta,
            (
                keep_q.reshape(cut), got_q.reshape(cut), near_ga, got_ga, near_gb, got_gb,
                near_ua, got_ua, near_ub, got_ub,
            ),
            outs,
            "fold",
        )
        sent_g, near_u, sent_u, near_q, sent_q = rest[:3], rest[3], rest[4:7], rest[7], rest[8]
        sent_q, sent_g, theirs = slot(sent_q, sent_g, theirs)
        got_q, got_g, theirs = flip_y(sent_q), turns(sent_g), flip_x(theirs)
        got_q, got_g = slot(got_q, got_g)
        near_q, *rest = fold(
            meta,
            (near_q, got_q, near_g, *got_g),
            cut_line(48, QW, 0, 1) + total_of(48, GW, 2),
            "fold",
        )
        sent_q, total_g = rest[:3], rest[3]
        sent_q, total_g, theirs, sent_u, total_d = slot(sent_q, total_g, theirs, sent_u, total_d)
        got_q, other_d = turns(sent_q), flip_x(total_d)
        got_q, other_d, sent_u, total_g = slot(got_q, other_d, sent_u, total_g)
        (total_q,) = fold(meta, (near_q, *got_q), total_of(48, QW, 0), "fold")
        got_u, other_q, other_g = turns(sent_u), flip_x(total_q), flip_x(total_g)
    else:
        theirs = flip_x(theirs)
    grad_in = tokens_grad_call(g_one, theirs, grads, w1)
    if fast:
        got_u, grad_in, other_q, other_g = slot(got_u, grad_in, other_q, other_g)
        (total_u,) = fold(meta, (near_u, *got_u), total_of(48, 2 * BLK, 0), "fold")
        other_u = flip_x(total_u)

    def joined(part):
        n_rows = part.shape[1]
        part = part.reshape(2, n_rows, 3, 3, 128).transpose(1, 3, 0, 2, 4)
        return part.reshape(n_rows, 3 * D)

    if fast:
        grad_qkv = joined(halves(total_q[:, : 3 * HW], other_q[:, : 3 * HW], x))
        grad_g = halves(total_g, other_g, x)
        grad_gate = jnp.concatenate([grad_g[0, :, : 2 * BLK], grad_g[1, :, : 2 * BLK]], axis=1)
        grad_out = jnp.concatenate([grad_g[0, :, 2 * BLK :], grad_g[1, :, 2 * BLK :]], axis=1)
        grad_up = jnp.concatenate(list(halves(total_u, other_u, x)), axis=1)
        grad_down = halves(total_d, other_d, x).reshape(-1, D)
        vec_own = add(total_q[:, 3 * HW : 3 * HW + 4], other_q[:, 3 * HW : 3 * HW + 4]).T
    else:

        def owned(a):
            part = lax.psum_scatter(a, "shard", scatter_dimension=0, tiled=True)
            return lax.psum(part, "seq").astype(f32)

        grad_g = whole_of_split(keep_g, send_g)
        grad_gate = owned(jnp.concatenate([grad_g[:, : 2 * BLK], grad_g[:, GW : GW + 2 * BLK]], axis=1))
        grad_out = owned(jnp.concatenate([grad_g[:, 2 * BLK : GW], grad_g[:, GW + 2 * BLK :]], axis=1))
        grad_up = owned(whole_of_split(keep_u, send_u))
        grad_down = owned(whole_of_down(keep_d, send_d))
        mine = jnp.stack([keep_q, send_q], axis=1).reshape(D, QW)[:, : 3 * HW]
        none = jnp.zeros_like(mine)
        both = jnp.stack([jnp.where(x == 0, mine, none), jnp.where(x == 0, none, mine)])
        grad_qkv = owned(joined(both))
        vec_grads = lax.psum(jnp.concatenate([vg_one[:2], vg_two[:2]]), ("seq", "shard"))
        vec_own = lax.dynamic_slice_in_dim(vec_grads, shard * (D // n), D // n, 1)
    return (
        out[None],
        grad_in[None],
        grad_qkv,
        grad_out,
        grad_gate,
        grad_up,
        grad_down,
        vec_own[0],
        vec_own[1],
        vec_own[2],
        vec_own[3],
    )


def solution(mesh):
    placed = (
        P("shard", "seq", None),
        P(),
        P("shard", None),
        P("shard", None),
        P("shard", None),
        P("shard", None),
        P("shard", None),
        P("shard"),
        P("shard"),
        P("shard"),
        P("shard"),
        P("shard", "seq", None),
    )
    return jax.shard_map(
        local,
        mesh=mesh,
        in_specs=placed,
        out_specs=(
            P("shard", "seq", None),
            P("shard", "seq", None),
            P("shard", None),
            P("shard", None),
            P("shard", None),
            P("shard", None),
            P("shard", None),
            P("shard"),
            P("shard"),
            P("shard"),
            P("shard"),
        ),
        check_vma=False,
    )
```

```python
from functools import partial

import jax
import jax.numpy as jnp
from jax import lax
from jax.experimental import pallas as pl
from jax.experimental.pallas import tpu as pltpu
from jax.sharding import PartitionSpec as P

D = 768
H = 12
HD = 64
FF = 3072
HALF = 512
PAIRS = H // 2
BLK = 768
HW = D // 2
GW = 2 * BLK + HW
MW = GW + 2 * BLK
GA = 1024
QW = 3 * HW + 128
MIB = 1 << 20

rope_base = 1000.0
norm_eps = 1e-05
big_negative = -1e30

bf16 = jnp.bfloat16
f32 = jnp.float32
VM = pl.BlockSpec(memory_space=pltpu.VMEM)
SM = pl.BlockSpec(memory_space=pltpu.SMEM)
HBM = pl.BlockSpec(memory_space=pl.ANY)


def dot(a, b):
    return lax.dot_general(a, b, (((1,), (0,)), ((), ())), preferred_element_type=f32)


def dot_t(a, b):
    return lax.dot_general(a, b, (((1,), (1,)), ((), ())), preferred_element_type=f32)


def params(mib):
    return pltpu.CompilerParams(vmem_limit_bytes=mib * MIB)


def cost(flops, moved, trans=0):
    return pl.CostEstimate(flops=int(flops), bytes_accessed=int(moved), transcendentals=int(trans))


def shape(dims, kind):
    return jax.ShapeDtypeStruct(dims, kind)


def piece_copies(meta, pieces, dst, sems):
    x, z, y, c = meta[4], meta[1], meta[2], meta[3]
    copies = []
    for at in range(8):
        dc, dy, dh = at // 4, (at // 2) % 2, at % 2
        h = jnp.where(x == 0, dh, 1 - dh)
        yy = jnp.where(y == 0, dy, 1 - dy)
        cc = jnp.where(c == 0, dc, 1 - dc)
        for k in range(4):
            zz = lax.rem(z - k + 4, 4)
            row = pl.multiple_of(((zz * 2 + yy) * 2 + cc) * 48, 48)
            copies.append(
                pltpu.make_async_copy(
                    pieces[at * 2 + k // 2].at[k % 2], dst.at[h, pl.ds(row, 48)], sems.at[at * 4 + k]
                )
            )
    return copies


def spin(u, cosine, sine):
    lane = lax.broadcasted_iota(jnp.int32, u.shape, 1)
    swapped = jnp.where(lane % HD < HD // 2, pltpu.roll(u, 96, 1), pltpu.roll(u, 32, 1))
    return u * cosine + swapped * sine


def qkv_kernel(meta, own, other, cosine, sine, *rest):
    pieces = rest[:4]
    q_out, k_out, kt_out, v_out, vt_out, w_out, vecs, w, sems, out_sem = rest[4:]
    step = pl.program_id(0)

    @pl.when(step == 0)
    def _():
        z, y, c = meta[1], meta[2], meta[3]
        copies = []
        for at, piece in enumerate(pieces):
            yy = jnp.where(y == 0, at % 2, 1 - at % 2)
            cc = jnp.where(c == 0, at // 2, 1 - at // 2)
            for k in range(4):
                zz = lax.rem(z - k + 4, 4)
                row = pl.multiple_of(((zz * 2 + yy) * 2 + cc) * 48, 48)
                copies.append(
                    pltpu.make_async_copy(piece.at[k], w.at[pl.ds(row, 48)], sems.at[at * 4 + k])
                )
        for copy in copies:
            copy.start()
        for copy in copies:
            copy.wait()
        pltpu.make_async_copy(w, w_out, out_sem).start()
        vecs[...] = w[:, 3 * HW :].astype(f32).T[:8]

    part = w[:, pl.ds(pl.multiple_of(step * HW, HW), HW)]
    for half, rows in enumerate((own, other)):
        at = slice(half * HALF, (half + 1) * HALF)
        cs, sn = cosine[at, :], sine[at, :]
        qkv = dot(rows[...], part)
        q_out[at, :] = spin(qkv[:, :128], cs, sn).astype(bf16)
        kr = spin(qkv[:, 128:256], cs, sn).astype(bf16)
        vs = qkv[:, 256:].astype(bf16)
        k_out[at, :] = kr
        kt_out[:, at] = kr.T
        v_out[at, :] = vs
        vt_out[:, at] = vs.T

    @pl.when(step == 2)
    def _():
        pltpu.make_async_copy(w, w_out, out_sem).wait()


def qkv_call(meta, own, other, cosine, sine, pieces):
    rows = 2 * HALF
    full = pl.BlockSpec((rows, 128), lambda i: (0, 0))
    x_spec = pl.BlockSpec((HALF, D), lambda i: (0, 0))
    nat = pl.BlockSpec((rows, 128), lambda i: (0, i))
    tr = pl.BlockSpec((128, rows), lambda i: (i, 0))
    return pl.pallas_call(
        qkv_kernel,
        grid=(3,),
        in_specs=[SM, x_spec, x_spec, full, full] + [HBM] * 4,
        out_specs=[nat, nat, tr, nat, tr, HBM, pl.BlockSpec((8, D), lambda i: (0, 0))],
        out_shape=[
            shape((rows, HW), bf16),
            shape((rows, HW), bf16),
            shape((HW, rows), bf16),
            shape((rows, HW), bf16),
            shape((HW, rows), bf16),
            shape((D, QW), bf16),
            shape((8, D), f32),
        ],
        scratch_shapes=[
            pltpu.VMEM((D, QW), bf16),
            pltpu.SemaphoreType.DMA((16,)),
            pltpu.SemaphoreType.DMA,
        ],
        compiler_params=params(62),
        cost_estimate=cost(2 * rows * D * 3 * HW, 14e6),
        name="qkv",
    )(meta, own, other, cosine, sine, *pieces)


def segment_of(meta, pos):
    seg = jnp.zeros(pos.shape, jnp.int32)
    for d in range(8):
        seg = seg + jnp.where(pos >= meta[8 + d], 1, 0)
    return seg


def bias_of(meta, key_base, keys, query_base):
    row = lax.broadcasted_iota(jnp.int32, (keys, 128), 0)
    key_pos = jnp.where(row < HALF, row + key_base[0], row - HALF + key_base[1])
    key_seg = segment_of(meta, key_pos)[:, :1]
    key_pos = key_pos[:, :1]
    query_pos = lax.broadcasted_iota(jnp.int32, (8, HALF), 1) + query_base
    query_seg = segment_of(meta, query_pos)[:1]
    query_pos = query_pos[:1]
    near = jnp.abs(key_pos - query_pos) <= HALF
    return jnp.where((key_seg == query_seg) & near, 0.0, big_negative).astype(f32)


def head_part(block, hh, scale=None):
    lane = lax.broadcasted_iota(jnp.int32, block.shape, 1)
    kept = jnp.where((lane // HD) == hh, block, jnp.zeros_like(block))
    return kept if scale is None else kept * jnp.asarray(scale, block.dtype)


def bases(meta):
    return meta[0] * HALF, HALF - meta[0] * HALF


def attend_kernel(side, meta, q, k, vt, att, att_t, lse, bias):
    @pl.when(pl.program_id(0) == 0)
    def _():
        both = bases(meta)
        bias[...] = bias_of(meta, both, 2 * HALF, both[side])

    parts = []
    for hh in range(2):
        qz = head_part(q[...], hh, HD**-0.5)
        s = dot_t(k[...], qz) + bias[...]
        peak = jnp.max(s, axis=0, keepdims=True)
        e = jnp.exp(s - peak)
        total = jnp.sum(e, axis=0, keepdims=True)
        o = dot(vt[hh * HD : (hh + 1) * HD, :], e.astype(bf16)) * (1.0 / total)
        parts.append(o.astype(bf16))
        lse[0, hh : hh + 1, :] = peak + jnp.log(total)
    both = jnp.concatenate(parts, axis=0)
    att_t[...] = both
    att[...] = both.T


def attend_call(meta, q, k, vt, side):
    return pl.pallas_call(
        partial(attend_kernel, side),
        grid=(3,),
        in_specs=[
            SM,
            pl.BlockSpec((HALF, 128), lambda i: (side, i)),
            pl.BlockSpec((2 * HALF, 128), lambda i: (0, i)),
            pl.BlockSpec((128, 2 * HALF), lambda i: (i, 0)),
        ],
        out_specs=[
            pl.BlockSpec((HALF, 128), lambda i: (0, i)),
            pl.BlockSpec((128, HALF), lambda i: (i, 0)),
            pl.BlockSpec((1, 2, HALF), lambda i: (i, 0, 0)),
        ],
        out_shape=[
            shape((HALF, HW), bf16),
            shape((HW, HALF), bf16),
            shape((3, 2, HALF), f32),
        ],
        scratch_shapes=[pltpu.VMEM((2 * HALF, HALF), f32)],
        compiler_params=params(24),
        cost_estimate=cost(4 * 4 * 6 * 2 * HALF * HALF * HD, 4e6, 6 * 2 * HALF * HALF),
        name="attend",
    )(meta, q, k, vt)


def attend_back_kernel(
    meta, q, k, kt, v, g_own, g_other, at_own, at_other, lse_own, lse_other, cosine, sine, grads, bias,
):
    @pl.when(pl.program_id(0) == 0)
    def _():
        both = bases(meta)
        for side in range(2):
            bias[side] = bias_of(meta, both, 2 * HALF, both[side])

    dk = dv = None
    for side, (g, at, lse) in enumerate(((g_own, at_own, lse_own), (g_other, at_other, lse_other))):
        rows = slice(side * HALF, (side + 1) * HALF)
        prod = g[...].T.astype(f32) * at[...].astype(f32)
        parts = []
        for hh in range(2):
            qz = head_part(q[rows, :], hh, HD**-0.5)
            gz = head_part(g[...], hh)
            delta = jnp.sum(prod[hh * HD : (hh + 1) * HD, :], axis=0, keepdims=True)
            s = dot_t(k[...], qz) + bias[side]
            p = jnp.exp(s - lse[0, hh : hh + 1, :])
            dp = dot_t(v[...], gz)
            ds = (p * (dp - delta)).astype(bf16)
            parts.append(dot(kt[hh * HD : (hh + 1) * HD, :], ds) * HD**-0.5)
            gk, gv = dot(ds, qz), dot(p.astype(bf16), gz)
            dk, dv = (gk, gv) if dk is None else (dk + gk, dv + gv)
        dq = jnp.concatenate(parts, axis=0).T
        grads[rows, :128] = spin(dq, cosine[rows, :], -sine[rows, :]).astype(bf16)
    grads[:, 128:256] = spin(dk, cosine[...], -sine[...]).astype(bf16)
    grads[:, 256:] = dv.astype(bf16)


def attend_back_call(meta, q, k, kt, v, g_own, g_other, at_own, at_other, lse_own, lse_other, cosine, sine, begin, count, done=None):
    nat = pl.BlockSpec((HALF, 128), lambda i: (0, begin + i))
    wide = pl.BlockSpec((2 * HALF, 128), lambda i: (0, begin + i))
    tall = pl.BlockSpec((128, HALF), lambda i: (begin + i, 0))
    row = pl.BlockSpec((1, 2, HALF), lambda i: (begin + i, 0, 0))
    table = pl.BlockSpec((2 * HALF, 128), lambda i: (0, 0))
    extra = () if done is None else (done,)

    def kernel(*refs):
        attend_back_kernel(*refs[:13], *refs[13 + len(extra) :])

    return pl.pallas_call(
        kernel,
        grid=(count,),
        in_specs=[
            SM, wide, wide, pl.BlockSpec((128, 2 * HALF), lambda i: (begin + i, 0)), wide,
            nat, nat, tall, tall, row, row, table, table,
        ] + [HBM] * len(extra),
        out_specs=pl.BlockSpec((2 * HALF, HW), lambda i: (0, begin + i)),
        out_shape=shape((2 * HALF, 3 * HW), bf16),
        input_output_aliases={13: 0} if extra else {},
        scratch_shapes=[pltpu.VMEM((2, 2 * HALF, HALF), f32)],
        compiler_params=params(36),
        cost_estimate=cost(4 * 10 * 2 * count * 4 * HALF * HALF * HD, 12e6, 2 * count * 4 * HALF * HALF),
        name="attend_back",
    )(meta, q, k, kt, v, g_own, g_other, at_own, at_other, lse_own, lse_other, cosine, sine, *extra)


def norm_parts(r):
    centered = r - jnp.mean(r, axis=-1, keepdims=True)
    scale = lax.rsqrt(jnp.mean(centered * centered, axis=-1, keepdims=True) + norm_eps)
    return centered * scale, scale


def norm_back(c, z, scale, gain):
    e = c * gain
    return (e - jnp.mean(e, axis=-1, keepdims=True) - z * jnp.mean(e * z, axis=-1, keepdims=True)) * scale


def split_core(c, val):
    parts = val.astype(bf16).reshape(8, 2, 48, val.shape[1])
    return (
        jnp.where(c == 0, parts[:, 0], parts[:, 1]),
        jnp.where(c == 0, parts[:, 1], parts[:, 0]),
    )


def whole(dims):
    return pl.BlockSpec(dims, lambda i: (0,) * len(dims))


NAT = whole((HALF, D))
PART = pl.BlockSpec((1, HALF, BLK), lambda i: (i % 4, 0, 0))
WIDE = pl.BlockSpec((1, D, BLK), lambda i: ((i % 4) // 2, 0, i % 2))
DOWN = pl.BlockSpec((BLK, D), lambda i: (i % 4, 0))
HEADS = whole((HALF, HW))


def hidden_kernel(meta, rows, mine, theirs, vecs, *rest):
    res, low_t, att_t, hid, a_out, b_out, low, w, sems = rest[16:]
    step = pl.program_id(0)
    copies = piece_copies(meta, rest[:16], w, sems)

    @pl.when(step == 0)
    def _():
        for copy in copies:
            copy.start()
        first = meta[0] == 0
        m, t = mine[...], theirs[...]
        left, right = jnp.where(first, m, t), jnp.where(first, t, m)
        att_t[:HW, :] = left.T
        att_t[HW:, :] = right.T
        att = jnp.concatenate([left, right], axis=1)
        for copy in copies:
            copy.wait()
        branch = jnp.concatenate(
            [dot(att, w[0, :, 2 * BLK : GW]), dot(att, w[1, :, 2 * BLK : GW])], axis=1
        )
        r = rows[...].astype(f32) + branch
        res[...] = r
        z, _ = norm_parts(r)
        n1 = (z * vecs[0:1, :] + vecs[1:2, :]).astype(bf16)
        low[...] = n1
        low_t[...] = n1.T

    half = step // 2
    at = (step % 2) * BLK
    g = dot(low[...], w[half, :, pl.ds(pl.multiple_of(at, BLK), BLK)])
    u = dot(low[...], w[half, :, pl.ds(pl.multiple_of(GW + at, HW), BLK)])
    sig = 1.0 / (1.0 + jnp.exp(-g))
    gs = g * sig
    hid[0] = (gs * u).astype(bf16)
    a_out[0] = (u * (sig + gs * (1.0 - sig))).astype(bf16)
    b_out[0] = gs.astype(bf16)


def hidden_call(meta, rows, mine, theirs, vecs, pieces):
    part = shape((4, HALF, BLK), bf16)
    return pl.pallas_call(
        hidden_kernel,
        grid=(4,),
        in_specs=[SM, NAT, HEADS, HEADS, whole((8, D))] + [HBM] * 16,
        out_specs=[NAT, whole((D, HALF)), whole((D, HALF)), PART, PART, PART],
        out_shape=[
            shape((HALF, D), f32),
            shape((D, HALF), bf16),
            shape((D, HALF), bf16),
            part,
            part,
            part,
        ],
        scratch_shapes=[
            pltpu.VMEM((HALF, D), bf16),
            pltpu.VMEM((2, D, MW), bf16),
            pltpu.SemaphoreType.DMA((32,)),
        ],
        compiler_params=params(62),
        cost_estimate=cost(2 * HALF * D * (2 * FF + D), 30e6, HALF * FF),
        name="hidden",
    )(meta, rows, mine, theirs, vecs, *pieces)


def down_copies(meta, pieces, dst, sems):
    z, y, c = meta[1], meta[2], meta[3]
    copies = []
    for at, piece in enumerate(pieces):
        dc, k = at // 4, at % 4
        zz = lax.rem(z - k + 4, 4)
        cc = jnp.where(c == 0, dc, 1 - dc)
        for dy in range(2):
            yy = jnp.where(y == 0, dy, 1 - dy)
            row = pl.multiple_of(((zz * 2 + yy) * 2 + cc) * 192, 192)
            copies.append(
                pltpu.make_async_copy(piece.at[dy], dst.at[pl.ds(row, 192)], sems.at[at * 2 + dy])
            )
    return copies


def mlp_back_kernel(meta, res, cot, vecs, hid, a, b, *rest):
    pieces, downs = rest[:16], rest[16:24]
    out, keep, send, gate_g, up_g, g_one, low, mine, theirs, vgrads = rest[24:34]
    acc, held, m, w, wd, sems, down_sems = rest[34:]
    step = pl.program_id(0)
    copies = piece_copies(meta, pieces, w, sems)
    down = down_copies(meta, downs, wd, down_sems)

    @pl.when(step == 0)
    def _():
        for copy in down + copies:
            copy.start()
        z, _ = norm_parts(res[...])
        acc[...] = z * vecs[0:1, :] + vecs[1:2, :]
        for copy in down:
            copy.wait()

    @pl.when(step < 4)
    def _():
        held[step] = hid[0]
        acc[...] += dot(hid[0], wd[pl.ds(pl.multiple_of(step * BLK, BLK), BLK), :])

    @pl.when(step == 3)
    def _():
        z, scale = norm_parts(acc[...])
        out[...] = (z * vecs[2:3, :] + vecs[3:4, :]).astype(bf16)
        c = cot[...].astype(f32)
        vgrads[2:3, :] = jnp.sum(c * z, axis=0, keepdims=True)
        vgrads[3:4, :] = jnp.sum(c, axis=0, keepdims=True)
        back = norm_back(c, z, scale, vecs[2:3, :])
        acc[...] = back
        m[...] = back.astype(bf16)

    @pl.when(step == 4)
    def _():
        for copy in copies:
            copy.wait()

    @pl.when(step >= 4)
    def _():
        j = step - 4
        half, at = j // 2, (j % 2) * BLK
        hg = dot_t(m[...], wd[pl.ds(pl.multiple_of(j * BLK, BLK), BLK), :])
        gg = (hg * a[0].astype(f32)).astype(bf16)
        ug = (hg * b[0].astype(f32)).astype(bf16)
        gate_g[0] = gg
        up_g[0] = ug
        acc[...] += dot_t(gg, w[half, :, pl.ds(pl.multiple_of(at, BLK), BLK)]) + dot_t(
            ug, w[half, :, pl.ds(pl.multiple_of(GW + at, HW), BLK)]
        )
        val = lax.dot_general(held[j], m[...], (((0,), (0,)), ((), ())), preferred_element_type=f32)
        c = meta[3]
        parts = val.astype(bf16).reshape(2, 2, 2, 96, D)
        for y in range(2):
            for h in range(2):
                keep[h, 0, y] = jnp.where(c == 0, parts[y, 0, h], parts[y, 1, h])
                send[h, 0, y] = jnp.where(c == 0, parts[y, 1, h], parts[y, 0, h])

    @pl.when(step == 7)
    def _():
        z, scale = norm_parts(res[...])
        c = acc[...]
        vgrads[0:1, :] = jnp.sum(c * z, axis=0, keepdims=True)
        vgrads[1:2, :] = jnp.sum(c, axis=0, keepdims=True)
        back = norm_back(c, z, scale, vecs[0:1, :])
        g_one[...] = back
        back = back.astype(bf16)
        low[...] = back
        ag = dot_t(back[:, :HW], w[0, :, 2 * BLK : GW]) + dot_t(back[:, HW:], w[1, :, 2 * BLK : GW])
        ag = ag.astype(bf16)
        first = meta[0] == 0
        mine[...] = jnp.where(first, ag[:, :HW], ag[:, HW:])
        theirs[...] = jnp.where(first, ag[:, HW:], ag[:, :HW])


def mlp_back_call(meta, res, cot, vecs, hid, a, b, pieces, downs):
    early = lambda i: jnp.minimum(i, 3)
    late = lambda i: jnp.maximum(i - 4, 0)
    part = pl.BlockSpec((1, HALF, BLK), lambda i: (late(i), 0, 0))
    grad = pl.BlockSpec((2, 1, 2, 96, D), lambda i: (0, late(i), 0, 0, 0))
    return pl.pallas_call(
        mlp_back_kernel,
        grid=(8,),
        in_specs=[
            SM, NAT, NAT, whole((8, D)), pl.BlockSpec((1, HALF, BLK), lambda i: (early(i), 0, 0)), part, part,
        ] + [HBM] * 24,
        out_specs=[NAT, grad, grad, part, part, NAT, NAT, HEADS, HEADS, whole((8, D))],
        out_shape=[
            shape((HALF, D), bf16),
            shape((2, 4, 2, 96, D), bf16),
            shape((2, 4, 2, 96, D), bf16),
            shape((4, HALF, BLK), bf16),
            shape((4, HALF, BLK), bf16),
            shape((HALF, D), f32),
            shape((HALF, D), bf16),
            shape((HALF, HW), bf16),
            shape((HALF, HW), bf16),
            shape((8, D), f32),
        ],
        scratch_shapes=[
            pltpu.VMEM((HALF, D), f32),
            pltpu.VMEM((4, HALF, BLK), bf16),
            pltpu.VMEM((HALF, D), bf16),
            pltpu.VMEM((2, D, MW), bf16),
            pltpu.VMEM((FF, D), bf16),
            pltpu.SemaphoreType.DMA((32,)),
            pltpu.SemaphoreType.DMA((16,)),
        ],
        compiler_params=params(62),
        cost_estimate=cost(2 * HALF * D * 5 * FF, 40e6),
        name="mlp_back",
    )(meta, res, cot, vecs, hid, a, b, *pieces, *downs)


def wide_grads_kernel(width, meta, low_t, grads, *rest):
    c = meta[3]
    keep, send = rest[-2:]

    def put(at, val):
        stay, leave = split_core(c, val)
        cols = slice(at, at + val.shape[1])
        for z in range(4):
            for y in range(2):
                keep[0, z, y, :, cols] = stay[2 * z + y]
                send[0, z, y, :, cols] = leave[2 * z + y]

    for i in range(2):
        put(i * BLK, dot(low_t[...], grads[i]))
    if width == GW:
        put(2 * BLK, dot(rest[0][...], rest[1][...]))


def wide_grads_call(meta, low_t, grads, *out_part):
    width = GW if out_part else 2 * BLK
    tall = whole((D, HALF))
    grad = pl.BlockSpec((1, 4, 2, 48, width), lambda i: (i, 0, 0, 0, 0))
    extra = [tall, pl.BlockSpec((HALF, HW), lambda i: (0, i))] if out_part else []
    return pl.pallas_call(
        partial(wide_grads_kernel, width),
        grid=(2,),
        in_specs=[SM, tall, pl.BlockSpec((2, HALF, BLK), lambda i: (i, 0, 0))] + extra,
        out_specs=[grad] * 2,
        out_shape=[shape((2, 4, 2, 48, width), bf16)] * 2,
        compiler_params=params(28),
        cost_estimate=cost(2 * HALF * D * FF, 9e6),
        name="wide_grads",
    )(meta, low_t, grads, *out_part)


def first_grads_kernel(meta, own, other, grads, vgrads, keep, send, rows_t):
    step = pl.program_id(0)

    @pl.when(step == 0)
    def _():
        rows_t[:, :HALF] = own[...].T
        rows_t[:, HALF:] = other[...].T
        row = lax.broadcasted_iota(jnp.int32, (8, D), 0)
        four = jnp.where(row < 4, vgrads[...], 0.0)
        four = jnp.concatenate([four, jnp.zeros((120, D), f32)], axis=0).T
        keep[:, :, 3 * HW :], send[:, :, 3 * HW :] = split_core(meta[3], four)

    for j in range(3):

        @pl.when(step == j)
        def _():
            at = slice(j * HW, (j + 1) * HW)
            keep[:, :, at], send[:, :, at] = split_core(meta[3], dot(rows_t[...], grads[...]))


def first_grads_call(meta, own, other, grads, vgrads):
    grad = whole((8, 48, QW))
    return pl.pallas_call(
        first_grads_kernel,
        grid=(3,),
        in_specs=[SM, NAT, NAT, pl.BlockSpec((2 * HALF, HW), lambda i: (0, i)), whole((8, D))],
        out_specs=[grad] * 2,
        out_shape=[shape((8, 48, QW), bf16)] * 2,
        scratch_shapes=[pltpu.VMEM((D, 2 * HALF), bf16)],
        compiler_params=params(24),
        cost_estimate=cost(2 * 2 * HALF * D * 3 * HW, 8e6),
        name="first_grads",
    )(meta, own, other, grads, vgrads)


def tokens_part_kernel(grads, w, out):
    out[...] = dot_t(grads[...], w[:, : 3 * HW]).astype(out.dtype)


def tokens_part_call(grads, w):
    return pl.pallas_call(
        tokens_part_kernel,
        grid=(2,),
        in_specs=[pl.BlockSpec((HALF // 2, 3 * HW), lambda i: (i + 2, 0)), whole((D, QW))],
        out_specs=pl.BlockSpec((HALF // 2, D), lambda i: (i, 0)),
        out_shape=shape((HALF, D), bf16),
        compiler_params=params(16),
        cost_estimate=cost(2 * HALF * D * 3 * HW, 5e6),
        name="tokens_part",
    )(grads, w)


def tokens_grad_kernel(g_one, theirs, grads, w, out):
    out[...] = g_one[...] + theirs[...].astype(f32) + dot_t(grads[...], w[:, : 3 * HW])


def tokens_grad_call(g_one, theirs, grads, w):
    part = pl.BlockSpec((HALF // 2, D), lambda i: (i, 0))
    return pl.pallas_call(
        tokens_grad_kernel,
        grid=(2,),
        in_specs=[part, part, pl.BlockSpec((HALF // 2, 3 * HW), lambda i: (i, 0)), whole((D, QW))],
        out_specs=part,
        out_shape=shape((HALF, D), f32),
        compiler_params=params(16),
        cost_estimate=cost(2 * HALF * D * 3 * HW, 8e6),
        name="tokens_grad",
    )(g_one, theirs, grads, w)


def pick(a, at, axis):
    return lax.dynamic_index_in_dim(a, at, axis, keepdims=False)


def flip_x(a):
    return lax.ppermute(a, "seq", [(0, 1), (1, 0)])


def flip(bit):
    def go(a):
        n = lax.axis_size("shard")
        return lax.ppermute(a, "shard", [(s, s ^ bit) for s in range(n)])

    return go


flip_c, flip_y = flip(1), flip(2)


def turn_z(a, k):
    return lax.ppermute(a, "shard", [(s, (s + 4 * k) % 16) for s in range(16)])


def after(a, *deps):
    return lax.optimization_barrier((a,) + deps)[0]


def slot(*arrays):
    return lax.optimization_barrier(arrays)


def around(mine):
    return [turn_z(mine, k) for k in (1, 2, 3)]


def pieces_of_whole(full):
    cut = full.reshape(full.shape[0], 4, 2, 2, 48, full.shape[2])
    order = jnp.array([0, 3, 2, 1])
    return [
        cut[dh, :, dy, dc][order]
        for dc in range(2)
        for dy in range(2)
        for dh in range(full.shape[0])
    ]


def in_two(pieces):
    return [part for piece in pieces for part in (piece[:2], piece[2:])]


def add(a, b):
    return a.astype(f32) + b.astype(f32)


def turns(sends):
    return [turn_z(send, k + 1) for k, send in enumerate(sends)]


def fold(meta, ins, outs, name):
    def kernel(*refs):
        spot = refs[0][0], refs[0][1], refs[0][2]
        for (_, give), out in zip(outs, refs[1 + len(ins) :]):
            out[...] = give(spot, *refs[1 : 1 + len(ins)]).astype(bf16)

    moved = 2 * sum(a.size for a in ins)
    return pl.pallas_call(
        kernel,
        grid=(1,),
        in_specs=[SM] + [whole(a.shape) for a in ins],
        out_specs=[whole(dims) for dims, _ in outs],
        out_shape=[shape(dims, bf16) for dims, _ in outs],
        compiler_params=params(32),
        cost_estimate=cost(moved, 2 * moved),
        name=name,
    )(meta, *ins)


def cut_core(rows, cols_x, cols_y):
    def along_x(flip):
        def give(spot, keep, got):
            at = spot[0] if flip == 0 else 1 - spot[0]
            return add(keep[at, :, :, :, :cols_x], got[at, :, :, :, :cols_x])

        return give

    def along_y(flip):
        def give(spot, keep, got):
            at = spot[2] if flip == 0 else 1 - spot[2]
            return add(keep[:, :, at, :, cols_x:], got[:, :, at, :, cols_x:])

        return give

    dims_x, dims_y = (4, 2, rows, cols_x), (2, 4, rows, cols_y)
    return [(dims_x, along_x(0)), (dims_x, along_x(1)), (dims_y, along_y(0)), (dims_y, along_y(1))]


def first_two(outs):
    return [(dims, lambda spot, *refs, give=give: give(spot, *refs[:2])) for dims, give in outs]


def cut_plane(rows, cols_x, cols_y, first):
    def along_y(flip):
        def give(spot, *refs):
            at = spot[2] if flip == 0 else 1 - spot[2]
            return add(refs[first][:, at], refs[first + 1][:, at])

        return give

    def along_x(flip):
        def give(spot, *refs):
            at = spot[0] if flip == 0 else 1 - spot[0]
            return add(refs[first + 2][at], refs[first + 3][at])

        return give

    dims_a, dims_b = (4, rows, cols_x), (4, rows, cols_y)
    return [(dims_a, along_y(0)), (dims_a, along_y(1)), (dims_b, along_x(0)), (dims_b, along_x(1))]


def cut_line(rows, cols, first, count):
    def part(k):
        def give(spot, *refs):
            at = lax.rem(spot[1] + k, 4)
            sums = [
                add(refs[first + 2 * i][at], refs[first + 2 * i + 1][at]) for i in range(count)
            ]
            return sums[0] if count == 1 else jnp.concatenate(sums, axis=-1)

        return give

    return [((rows, cols), part(k)) for k in range(4)]


def cut_z(rows, cols):
    def part(k):
        def give(spot, keep, got, *_):
            at = lax.rem(spot[1] + k, 4)
            return add(keep[:, at], got[:, at])

        return give

    return [((2, 2, rows, cols), part(k)) for k in range(4)]


def pair(dims, first):
    return [(dims, lambda spot, *refs: add(refs[first][...], refs[first + 1][...]))]


def total_of(rows, cols, first):
    def give(spot, *refs):
        near, *gots = [refs[first + i][...].astype(f32) for i in range(4)]
        return near + gots[0] + gots[1] + gots[2]

    return [((rows, cols), give)]


def halves(mine, other, x):
    return jnp.where(x == 0, jnp.stack([mine, other]), jnp.stack([other, mine])).astype(f32)


def whole_of_split(keep, send):
    both = jnp.stack([keep, send], axis=3)
    return both.transpose(1, 2, 3, 4, 0, 5).reshape(D, -1)


def whole_of_down(keep, send):
    return jnp.stack([keep, send], axis=3).transpose(1, 2, 3, 0, 4, 5).reshape(FF, D)


def local(
    tokens,
    doc_lengths,
    qkv_weight,
    out_weight,
    gate_weight,
    up_weight,
    down_weight,
    norm1_gain,
    norm1_bias,
    norm2_gain,
    norm2_bias,
    cotangent,
):
    n = lax.axis_size("shard")
    fast = n == 16
    x = lax.axis_index("seq").astype(jnp.int32)
    shard = lax.axis_index("shard").astype(jnp.int32)
    zero = jnp.zeros((), jnp.int32)
    z, y, c = (shard // 4, (shard // 2) % 2, shard % 2) if fast else (zero, zero, zero)

    rows = tokens[0]
    cot = cotangent[0]
    lengths = lax.dynamic_slice_in_dim(doc_lengths, shard, 1, 0)[0]
    ends = jnp.cumsum(lengths).astype(jnp.int32)
    hx = x if fast else zero
    meta = jnp.concatenate([jnp.stack([x, z, y, c, hx]), jnp.zeros((3,), jnp.int32), ends])
    spots = jnp.arange(2 * HALF, dtype=jnp.int32)
    spots = jnp.where(spots < HALF, spots + x * HALF, spots - x * HALF)
    passed = spots[:, None] >= ends[None, :]
    place = spots - jnp.sum(jnp.where(passed, lengths[None, :], 0), axis=1)
    frequency = rope_base ** (-jnp.arange(HD // 2, dtype=f32) * 2.0 / HD)
    angles = place.astype(f32)[:, None] * frequency[None, :]
    cosine = jnp.tile(jnp.cos(angles), (1, 4))
    sine = jnp.sin(angles)
    sine = jnp.concatenate([-sine, sine, -sine, sine], axis=1)

    vec_block = jnp.stack([norm1_gain, norm1_bias, norm2_gain, norm2_bias], axis=1)
    vec_block = jnp.pad(vec_block, ((0, 0), (0, 124)))

    def my_heads(w):
        mine = lax.dynamic_slice_in_dim(w.reshape(w.shape[0], 3, 2, HW), x, 1, 2)
        mine = mine.reshape(w.shape[0], 3, 3, 128).transpose(0, 2, 1, 3)
        return mine.reshape(w.shape[0], 3 * HW)

    def half_of(w):
        cols = w.shape[1] // 2
        return jnp.where(x == 0, w[:, :cols], w[:, cols:])

    if fast:
        first = jnp.concatenate([my_heads(qkv_weight), vec_block], axis=1)
        wide = jnp.concatenate([half_of(gate_weight), half_of(out_weight), half_of(up_weight)], axis=1)
        zq, yd, wide1 = around(first), flip_y(down_weight), turn_z(wide, 1)
        first, zq, wide_late, cosine, sine, rows_late, yd = slot(
            first, zq, wide, cosine, sine, rows, yd
        )
        aq = jnp.stack([first] + zq)
        byq, rows_other = flip_y(aq), flip_x(rows_late)
        wide2, wide3 = turn_z(wide_late, 2), turn_z(wide_late, 3)
        aq, byq, wide, wide1, wide3, down, yd = slot(aq, byq, wide, wide1, wide3, down_weight, yd)
        a0 = jnp.stack([wide, wide1])
        d0 = jnp.stack([down, yd])
        caq, cbyq = flip_c(aq), flip_c(byq)
        caq, cbyq, a0, rows_other, d0 = slot(caq, cbyq, a0, rows_other, d0)
        by0, bx0 = flip_y(a0), flip_x(a0)
        first_pieces = [aq, byq, caq, cbyq]
    else:
        rows_other = flip_x(rows)

        def gathered(w):
            return lax.all_gather(w, "shard", axis=0, tiled=True)

        first = jnp.concatenate([my_heads(gathered(qkv_weight)), gathered(vec_block)], axis=1)
        first_pieces = pieces_of_whole(first[None])

        def in_halves(w):
            return gathered(w).reshape(D, 2, -1).transpose(1, 0, 2)

        wide_all = jnp.concatenate([in_halves(w) for w in (gate_weight, out_weight, up_weight)], axis=2)
        pieces = in_two(pieces_of_whole(wide_all))
        down_all = gathered(down_weight).reshape(4, 2, 2, 192, D)
        down_pieces = [down_all[(4 - k) % 4, :, dc] for dc in range(2) for k in range(4)]

    q, k, kt, v, vt, w1, vecs = qkv_call(meta, rows, rows_other, cosine, sine, first_pieces)
    if fast:
        q, a0, by0, bx0, wide2, d0 = slot(q, a0, by0, bx0, wide2, d0)
        a1 = jnp.stack([wide2, wide3])
        q, a1 = slot(q, a1)
        by1, bx1, d1 = flip_y(a1), flip_x(a1), turn_z(d0, 1)
        ca0, cby0 = flip_c(a0), flip_c(by0)
    att_theirs, at_other, lse_other = attend_call(meta, q, k, vt, 1)
    if fast:
        q, att_theirs, by1, bx1, ca0, cby0, d1, by0, bx0, a1 = slot(
            q, att_theirs, by1, bx1, ca0, cby0, d1, by0, bx0, a1
        )
    att_got = flip_x(att_theirs)
    if fast:
        bxy0, bxy1, d2 = flip_x(by0), flip_y(bx1), turn_z(d1, 1)
        cbx0 = flip_c(bx0)
    att_mine, at_own, lse_own = attend_call(meta, q, k, vt, 0)
    if fast:
        att_mine, att_got, bxy0, bxy1, d2, cbx0, by1, a1, bx1 = slot(
            att_mine, att_got, bxy0, bxy1, d2, cbx0, by1, a1, bx1
        )
        cby1 = flip_c(by1)
        cbx1, cbxy0, cbxy1, ca1 = flip_c(bx1), flip_c(bxy0), flip_c(bxy1), flip_c(a1)
        att_mine, cbx1, cby1, cbxy0, cbxy1, ca1, d0, d1, d2 = slot(
            att_mine, cbx1, cby1, cbxy0, cbxy1, ca1, d0, d1, d2
        )
        d3, cd0, cd1, cd2 = turn_z(d2, 1), flip_c(d0), flip_c(d1), flip_c(d2)
        pieces = [a0, a1, bx0, bx1, by0, by1, bxy0, bxy1]
        pieces += [ca0, ca1, cbx0, cbx1, cby0, cby1, cbxy0, cbxy1]
    res, low_t, att_t, hid, part_a, part_b = hidden_call(
        meta, rows, att_mine, att_got, vecs, pieces
    )
    if fast:
        hid, d3, cd0, cd1, cd2 = slot(hid, d3, cd0, cd1, cd2)
        down_pieces = [d0, d1, d2, d3, cd0, cd1, cd2, flip_c(d3)]
    out, keep_d, send_d, gate_g, up_g, g_one, g_low, g_mine, g_theirs, vgrads = mlp_back_call(
        meta, res, cot, vecs, hid, part_a, part_b, pieces, down_pieces
    )

    if fast:
        keep_d, send_d, g_theirs, gate_g = slot(keep_d, send_d, g_theirs, gate_g)
        got_d = flip_c(send_d)
    keep_g, send_g = wide_grads_call(meta, low_t, gate_g, att_t, g_low)
    if fast:
        send_g, g_theirs, got_d, up_g = slot(send_g, g_theirs, got_d, up_g)
        got_g = flip_c(send_g)
    g_other = flip_x(g_theirs)
    keep_u, send_u = wide_grads_call(meta, low_t, up_g)
    if fast:
        send_u, got_g, got_d, g_other = slot(send_u, got_g, got_d, g_other)
        near_ga, sent_ga, near_gb, sent_gb, *part_d = fold(
            meta,
            (keep_g, got_g, keep_d, got_d),
            first_two(cut_core(48, GA, GW - GA))
            + [(dims, lambda spot, *refs, give=give: give(spot, *refs[2:])) for dims, give in cut_z(96, D)],
            "fold",
        )
        sent_ga, sent_gb, g_other, part_d, send_u = slot(sent_ga, sent_gb, g_other, part_d, send_u)
        got_ga, got_gb, got_u = flip_x(sent_ga), flip_y(sent_gb), flip_c(send_u)
        got_d = turn_z(part_d[3], 1)
    back_args = (q, k, kt, v, g_mine, g_other, at_own, at_other, lse_own, lse_other, cosine, sine)
    grads = attend_back_call(meta, *back_args, 0, 2)
    if fast:
        grads, got_ga, got_gb, got_u, got_d = slot(grads, got_ga, got_gb, got_u, got_d)
        near_ga, sent_ga, near_gb, sent_gb, near_ua, sent_ua, near_ub, sent_ub, sent_d = fold(
            meta,
            (keep_u, got_u, near_ga, got_ga, near_gb, got_gb, part_d[2], got_d),
            cut_plane(48, GA, GW - GA, 2) + first_two(cut_core(48, BLK, BLK)) + pair((2, 2, 96, D), 6),
            "fold",
        )
        grads, sent_ua, sent_ub, sent_ga, sent_gb, sent_d = slot(
            grads, sent_ua, sent_ub, sent_ga, sent_gb, sent_d
        )
        got_ua, got_ub, got_d = flip_x(sent_ua), flip_y(sent_ub), turn_z(sent_d, 1)
    grads = attend_back_call(meta, *back_args, 2, 1, grads)
    if fast:
        grads, got_ua, got_ub, got_d, sent_ga, sent_gb = slot(
            grads, got_ua, got_ub, got_d, sent_ga, sent_gb
        )
        near_ua, sent_ua, near_ub, sent_ub, sent_d = fold(
            meta,
            (near_ua, got_ua, near_ub, got_ub, part_d[1], got_d),
            cut_plane(48, BLK, BLK, 0) + pair((2, 2, 96, D), 4),
            "fold",
        )
        grads, sent_ga, sent_gb, sent_ua, sent_ub, sent_d = slot(
            grads, sent_ga, sent_gb, sent_ua, sent_ub, sent_d
        )
        got_ga, got_gb, got_ua, got_ub = flip_y(sent_ga), flip_x(sent_gb), flip_y(sent_ua), flip_x(sent_ub)
        got_d = turn_z(sent_d, 1)
    keep_q, send_q = first_grads_call(meta, rows, rows_other, grads, vgrads)
    if fast:
        keep_q, send_q, got_ga, got_gb, got_ua, got_ub, got_d, grads = slot(
            keep_q, send_q, got_ga, got_gb, got_ua, got_ub, got_d, grads
        )
        got_q = flip_c(send_q)
        near_g, *rest = fold(
            meta,
            (near_ga, got_ga, near_gb, got_gb, near_ua, got_ua, near_ub, got_ub, part_d[0], got_d),
            cut_line(48, GW, 0, 2)
            + cut_line(48, 2 * BLK, 4, 2)
            + [
                ((2, 96, D), lambda spot, *refs: add(refs[8][:, spot[2]], refs[9][:, spot[2]])),
                ((2, 96, D), lambda spot, *refs: add(refs[8][:, 1 - spot[2]], refs[9][:, 1 - spot[2]])),
            ],
            "fold",
        )
        sent_g, near_u, sent_u, near_d, sent_d = rest[:3], rest[3], rest[4:7], rest[7], rest[8]
        sent_g, grads = slot(sent_g, grads)
        got_g = turns(sent_g)
    theirs = tokens_part_call(grads, w1)
    if fast:
        got_q, theirs, sent_d = slot(got_q, theirs, sent_d)
        cut = (4, 2, 48, QW)
        near_q, sent_q = fold(
            meta,
            (keep_q.reshape(cut), got_q.reshape(cut)),
            [
                ((4, 48, QW), lambda spot, keep, got: add(keep[:, spot[2]], got[:, spot[2]])),
                ((4, 48, QW), lambda spot, keep, got: add(keep[:, 1 - spot[2]], got[:, 1 - spot[2]])),
            ],
            "fold",
        )
        sent_q, theirs = slot(sent_q, theirs)
        got_q, theirs = flip_y(sent_q), flip_x(theirs)
        got_q, got_g, sent_d = slot(got_q, got_g, sent_d)
        near_q, *rest = fold(
            meta,
            (near_q, got_q, near_g, *got_g),
            cut_line(48, QW, 0, 1) + total_of(48, GW, 2),
            "fold",
        )
        sent_q, total_g = rest[:3], rest[3]
        sent_q, total_g, theirs, sent_u, sent_d = slot(sent_q, total_g, theirs, sent_u, sent_d)
        got_q, got_d, other_g = turns(sent_q), flip_y(sent_d), flip_x(total_g)
        got_q, got_d, other_g, sent_u = slot(got_q, got_d, other_g, sent_u)
        total_q, total_d = fold(
            meta,
            (near_q, *got_q, near_d, got_d),
            total_of(48, QW, 0) + pair((2, 96, D), 4),
            "fold",
        )
        got_u, other_q, other_d = turns(sent_u), flip_x(total_q), flip_x(total_d)
    else:
        theirs = flip_x(theirs)
    grad_in = tokens_grad_call(g_one, theirs, grads, w1)
    if fast:
        got_u, grad_in, other_q, other_g, other_d = slot(got_u, grad_in, other_q, other_g, other_d)
        (total_u,) = fold(meta, (near_u, *got_u), total_of(48, 2 * BLK, 0), "fold")
        other_u = flip_x(total_u)

    def joined(part):
        n_rows = part.shape[1]
        part = part.reshape(2, n_rows, 3, 3, 128).transpose(1, 3, 0, 2, 4)
        return part.reshape(n_rows, 3 * D)

    if fast:
        grad_qkv = joined(halves(total_q[:, : 3 * HW], other_q[:, : 3 * HW], x))
        grad_g = halves(total_g, other_g, x)
        grad_gate = jnp.concatenate([grad_g[0, :, : 2 * BLK], grad_g[1, :, : 2 * BLK]], axis=1)
        grad_out = jnp.concatenate([grad_g[0, :, 2 * BLK :], grad_g[1, :, 2 * BLK :]], axis=1)
        grad_up = jnp.concatenate(list(halves(total_u, other_u, x)), axis=1)
        grad_down = add(total_d, other_d).reshape(-1, D)
        vec_own = add(total_q[:, 3 * HW : 3 * HW + 4], other_q[:, 3 * HW : 3 * HW + 4]).T
    else:

        def owned(a):
            part = lax.psum_scatter(a, "shard", scatter_dimension=0, tiled=True)
            return lax.psum(part, "seq").astype(f32)

        grad_g = whole_of_split(keep_g, send_g)
        grad_gate = owned(jnp.concatenate([grad_g[:, : 2 * BLK], grad_g[:, GW : GW + 2 * BLK]], axis=1))
        grad_out = owned(jnp.concatenate([grad_g[:, 2 * BLK : GW], grad_g[:, GW + 2 * BLK :]], axis=1))
        grad_up = owned(whole_of_split(keep_u, send_u))
        grad_down = owned(whole_of_down(keep_d, send_d))
        mine = jnp.stack([keep_q, send_q], axis=1).reshape(D, QW)[:, : 3 * HW]
        none = jnp.zeros_like(mine)
        both = jnp.stack([jnp.where(x == 0, mine, none), jnp.where(x == 0, none, mine)])
        grad_qkv = owned(joined(both))
        vec_grads = lax.psum(vgrads[:4], ("seq", "shard"))
        vec_own = lax.dynamic_slice_in_dim(vec_grads, shard * (D // n), D // n, 1)
    return (
        out[None],
        grad_in[None],
        grad_qkv,
        grad_out,
        grad_gate,
        grad_up,
        grad_down,
        vec_own[0],
        vec_own[1],
        vec_own[2],
        vec_own[3],
    )


def solution(mesh):
    placed = (
        P("shard", "seq", None),
        P(),
        P("shard", None),
        P("shard", None),
        P("shard", None),
        P("shard", None),
        P("shard", None),
        P("shard"),
        P("shard"),
        P("shard"),
        P("shard"),
        P("shard", "seq", None),
    )
    return jax.shard_map(
        local,
        mesh=mesh,
        in_specs=placed,
        out_specs=(
            P("shard", "seq", None),
            P("shard", "seq", None),
            P("shard", None),
            P("shard", None),
            P("shard", None),
            P("shard", None),
            P("shard", None),
            P("shard"),
            P("shard"),
            P("shard"),
            P("shard"),
        ),
        check_vma=False,
    )
```

```python
from functools import partial

import jax
import jax.numpy as jnp
from jax import lax
from jax.experimental import pallas as pl
from jax.experimental.pallas import tpu as pltpu
from jax.sharding import PartitionSpec as P

D = 768
H = 12
HD = 64
FF = 3072
HALF = 512
PAIRS = H // 2
BLK = 768
HW = D // 2
GW = 2 * BLK + HW
MW = GW + 2 * BLK
GA = 1024
QW = 3 * HW + 128
MIB = 1 << 20

rope_base = 1000.0
norm_eps = 1e-05
big_negative = -1e30

bf16 = jnp.bfloat16
f32 = jnp.float32
VM = pl.BlockSpec(memory_space=pltpu.VMEM)
SM = pl.BlockSpec(memory_space=pltpu.SMEM)
HBM = pl.BlockSpec(memory_space=pl.ANY)


def dot(a, b):
    return lax.dot_general(a, b, (((1,), (0,)), ((), ())), preferred_element_type=f32)


def dot_t(a, b):
    return lax.dot_general(a, b, (((1,), (1,)), ((), ())), preferred_element_type=f32)


def params(mib):
    return pltpu.CompilerParams(vmem_limit_bytes=mib * MIB)


def cost(flops, moved, trans=0):
    return pl.CostEstimate(flops=int(flops), bytes_accessed=int(moved), transcendentals=int(trans))


def shape(dims, kind):
    return jax.ShapeDtypeStruct(dims, kind)


def piece_copies(meta, pieces, dst, sems):
    x, z, y, c = meta[4], meta[1], meta[2], meta[3]
    copies = []
    for at in range(8):
        dc, dy, dh = at // 4, (at // 2) % 2, at % 2
        h = jnp.where(x == 0, dh, 1 - dh)
        yy = jnp.where(y == 0, dy, 1 - dy)
        cc = jnp.where(c == 0, dc, 1 - dc)
        for k in range(4):
            zz = lax.rem(z - k + 4, 4)
            row = pl.multiple_of(((zz * 2 + yy) * 2 + cc) * 48, 48)
            copies.append(
                pltpu.make_async_copy(
                    pieces[at * 2 + k // 2].at[k % 2], dst.at[h, pl.ds(row, 48)], sems.at[at * 4 + k]
                )
            )
    return copies


def spin(u, cosine, sine):
    lane = lax.broadcasted_iota(jnp.int32, u.shape, 1)
    swapped = jnp.where(lane % HD < HD // 2, pltpu.roll(u, 96, 1), pltpu.roll(u, 32, 1))
    return u * cosine + swapped * sine


def qkv_kernel(meta, own, other, cosine, sine, *rest):
    pieces = rest[:4]
    q_out, k_out, kt_out, v_out, vt_out, w_out, vecs, w, sems, out_sem = rest[4:]
    step = pl.program_id(0)

    @pl.when(step == 0)
    def _():
        z, y, c = meta[1], meta[2], meta[3]
        copies = []
        for at, piece in enumerate(pieces):
            yy = jnp.where(y == 0, at % 2, 1 - at % 2)
            cc = jnp.where(c == 0, at // 2, 1 - at // 2)
            for k in range(4):
                zz = lax.rem(z - k + 4, 4)
                row = pl.multiple_of(((zz * 2 + yy) * 2 + cc) * 48, 48)
                copies.append(
                    pltpu.make_async_copy(piece.at[k], w.at[pl.ds(row, 48)], sems.at[at * 4 + k])
                )
        for copy in copies:
            copy.start()
        for copy in copies:
            copy.wait()
        pltpu.make_async_copy(w, w_out, out_sem).start()
        vecs[...] = w[:, 3 * HW :].astype(f32).T[:8]

    part = w[:, pl.ds(pl.multiple_of(step * HW, HW), HW)]
    for half, rows in enumerate((own, other)):
        at = slice(half * HALF, (half + 1) * HALF)
        cs, sn = cosine[at, :], sine[at, :]
        qkv = dot(rows[...], part)
        q_out[at, :] = spin(qkv[:, :128], cs, sn).astype(bf16)
        kr = spin(qkv[:, 128:256], cs, sn).astype(bf16)
        vs = qkv[:, 256:].astype(bf16)
        k_out[at, :] = kr
        kt_out[:, at] = kr.T
        v_out[at, :] = vs
        vt_out[:, at] = vs.T

    @pl.when(step == 2)
    def _():
        pltpu.make_async_copy(w, w_out, out_sem).wait()


def qkv_call(meta, own, other, cosine, sine, pieces):
    rows = 2 * HALF
    full = pl.BlockSpec((rows, 128), lambda i: (0, 0))
    x_spec = pl.BlockSpec((HALF, D), lambda i: (0, 0))
    nat = pl.BlockSpec((rows, 128), lambda i: (0, i))
    tr = pl.BlockSpec((128, rows), lambda i: (i, 0))
    return pl.pallas_call(
        qkv_kernel,
        grid=(3,),
        in_specs=[SM, x_spec, x_spec, full, full] + [HBM] * 4,
        out_specs=[nat, nat, tr, nat, tr, HBM, pl.BlockSpec((8, D), lambda i: (0, 0))],
        out_shape=[
            shape((rows, HW), bf16),
            shape((rows, HW), bf16),
            shape((HW, rows), bf16),
            shape((rows, HW), bf16),
            shape((HW, rows), bf16),
            shape((D, QW), bf16),
            shape((8, D), f32),
        ],
        scratch_shapes=[
            pltpu.VMEM((D, QW), bf16),
            pltpu.SemaphoreType.DMA((16,)),
            pltpu.SemaphoreType.DMA,
        ],
        compiler_params=params(62),
        cost_estimate=cost(2 * rows * D * 3 * HW, 14e6),
        name="qkv",
    )(meta, own, other, cosine, sine, *pieces)


def segment_of(meta, pos):
    seg = jnp.zeros(pos.shape, jnp.int32)
    for d in range(8):
        seg = seg + jnp.where(pos >= meta[8 + d], 1, 0)
    return seg


def bias_of(meta, key_base, keys, query_base):
    row = lax.broadcasted_iota(jnp.int32, (keys, 128), 0)
    key_pos = jnp.where(row < HALF, row + key_base[0], row - HALF + key_base[1])
    key_seg = segment_of(meta, key_pos)[:, :1]
    key_pos = key_pos[:, :1]
    query_pos = lax.broadcasted_iota(jnp.int32, (8, HALF), 1) + query_base
    query_seg = segment_of(meta, query_pos)[:1]
    query_pos = query_pos[:1]
    near = jnp.abs(key_pos - query_pos) <= HALF
    return jnp.where((key_seg == query_seg) & near, 0.0, big_negative).astype(f32)


def head_part(block, hh, scale=None):
    lane = lax.broadcasted_iota(jnp.int32, block.shape, 1)
    kept = jnp.where((lane // HD) == hh, block, jnp.zeros_like(block))
    return kept if scale is None else kept * jnp.asarray(scale, block.dtype)


def bases(meta):
    return meta[0] * HALF, HALF - meta[0] * HALF


def attend_kernel(side, meta, q, k, vt, att, att_t, lse, bias):
    @pl.when(pl.program_id(0) == 0)
    def _():
        both = bases(meta)
        bias[...] = bias_of(meta, both, 2 * HALF, both[side])

    parts = []
    for hh in range(2):
        qz = head_part(q[...], hh, HD**-0.5)
        s = dot_t(k[...], qz) + bias[...]
        peak = jnp.max(s, axis=0, keepdims=True)
        e = jnp.exp(s - peak)
        total = jnp.sum(e, axis=0, keepdims=True)
        o = dot(vt[hh * HD : (hh + 1) * HD, :], e.astype(bf16)) * (1.0 / total)
        parts.append(o.astype(bf16))
        lse[0, hh : hh + 1, :] = peak + jnp.log(total)
    both = jnp.concatenate(parts, axis=0)
    att_t[...] = both
    att[...] = both.T


def attend_call(meta, q, k, vt, side):
    return pl.pallas_call(
        partial(attend_kernel, side),
        grid=(3,),
        in_specs=[
            SM,
            pl.BlockSpec((HALF, 128), lambda i: (side, i)),
            pl.BlockSpec((2 * HALF, 128), lambda i: (0, i)),
            pl.BlockSpec((128, 2 * HALF), lambda i: (i, 0)),
        ],
        out_specs=[
            pl.BlockSpec((HALF, 128), lambda i: (0, i)),
            pl.BlockSpec((128, HALF), lambda i: (i, 0)),
            pl.BlockSpec((1, 2, HALF), lambda i: (i, 0, 0)),
        ],
        out_shape=[
            shape((HALF, HW), bf16),
            shape((HW, HALF), bf16),
            shape((3, 2, HALF), f32),
        ],
        scratch_shapes=[pltpu.VMEM((2 * HALF, HALF), f32)],
        compiler_params=params(24),
        cost_estimate=cost(4 * 4 * 6 * 2 * HALF * HALF * HD, 4e6, 6 * 2 * HALF * HALF),
        name="attend",
    )(meta, q, k, vt)


def attend_back_kernel(
    meta, q, k, kt, v, g_own, g_other, at_own, at_other, lse_own, lse_other, cosine, sine, grads, bias,
):
    @pl.when(pl.program_id(0) == 0)
    def _():
        both = bases(meta)
        for side in range(2):
            bias[side] = bias_of(meta, both, 2 * HALF, both[side])

    dk = dv = None
    for side, (g, at, lse) in enumerate(((g_own, at_own, lse_own), (g_other, at_other, lse_other))):
        rows = slice(side * HALF, (side + 1) * HALF)
        prod = g[...].T.astype(f32) * at[...].astype(f32)
        parts = []
        for hh in range(2):
            qz = head_part(q[rows, :], hh, HD**-0.5)
            gz = head_part(g[...], hh)
            delta = jnp.sum(prod[hh * HD : (hh + 1) * HD, :], axis=0, keepdims=True)
            s = dot_t(k[...], qz) + bias[side]
            p = jnp.exp(s - lse[0, hh : hh + 1, :])
            dp = dot_t(v[...], gz)
            ds = (p * (dp - delta)).astype(bf16)
            parts.append(dot(kt[hh * HD : (hh + 1) * HD, :], ds) * HD**-0.5)
            gk, gv = dot(ds, qz), dot(p.astype(bf16), gz)
            dk, dv = (gk, gv) if dk is None else (dk + gk, dv + gv)
        dq = jnp.concatenate(parts, axis=0).T
        grads[rows, :128] = spin(dq, cosine[rows, :], -sine[rows, :]).astype(bf16)
    grads[:, 128:256] = spin(dk, cosine[...], -sine[...]).astype(bf16)
    grads[:, 256:] = dv.astype(bf16)


def attend_back_call(meta, q, k, kt, v, g_own, g_other, at_own, at_other, lse_own, lse_other, cosine, sine, begin, count, done=None):
    nat = pl.BlockSpec((HALF, 128), lambda i: (0, begin + i))
    wide = pl.BlockSpec((2 * HALF, 128), lambda i: (0, begin + i))
    tall = pl.BlockSpec((128, HALF), lambda i: (begin + i, 0))
    row = pl.BlockSpec((1, 2, HALF), lambda i: (begin + i, 0, 0))
    table = pl.BlockSpec((2 * HALF, 128), lambda i: (0, 0))
    extra = () if done is None else (done,)

    def kernel(*refs):
        attend_back_kernel(*refs[:13], *refs[13 + len(extra) :])

    return pl.pallas_call(
        kernel,
        grid=(count,),
        in_specs=[
            SM, wide, wide, pl.BlockSpec((128, 2 * HALF), lambda i: (begin + i, 0)), wide,
            nat, nat, tall, tall, row, row, table, table,
        ] + [HBM] * len(extra),
        out_specs=pl.BlockSpec((2 * HALF, HW), lambda i: (0, begin + i)),
        out_shape=shape((2 * HALF, 3 * HW), bf16),
        input_output_aliases={13: 0} if extra else {},
        scratch_shapes=[pltpu.VMEM((2, 2 * HALF, HALF), f32)],
        compiler_params=params(36),
        cost_estimate=cost(4 * 10 * 2 * count * 4 * HALF * HALF * HD, 12e6, 2 * count * 4 * HALF * HALF),
        name="attend_back",
    )(meta, q, k, kt, v, g_own, g_other, at_own, at_other, lse_own, lse_other, cosine, sine, *extra)


def norm_parts(r):
    centered = r - jnp.mean(r, axis=-1, keepdims=True)
    scale = lax.rsqrt(jnp.mean(centered * centered, axis=-1, keepdims=True) + norm_eps)
    return centered * scale, scale


def norm_back(c, z, scale, gain):
    e = c * gain
    return (e - jnp.mean(e, axis=-1, keepdims=True) - z * jnp.mean(e * z, axis=-1, keepdims=True)) * scale


def split_core(c, val):
    parts = val.astype(bf16).reshape(8, 2, 48, val.shape[1])
    return (
        jnp.where(c == 0, parts[:, 0], parts[:, 1]),
        jnp.where(c == 0, parts[:, 1], parts[:, 0]),
    )


def whole(dims):
    return pl.BlockSpec(dims, lambda i: (0,) * len(dims))


NAT = whole((HALF, D))
PART = pl.BlockSpec((1, HALF, BLK), lambda i: (i % 4, 0, 0))
WIDE = pl.BlockSpec((1, D, BLK), lambda i: ((i % 4) // 2, 0, i % 2))
DOWN = pl.BlockSpec((BLK, D), lambda i: (i % 4, 0))
HEADS = whole((HALF, HW))


def hidden_kernel(meta, rows, mine, theirs, vecs, *rest):
    res, low_t, att_t, hid, a_out, b_out, low, w, sems = rest[16:]
    step = pl.program_id(0)
    copies = piece_copies(meta, rest[:16], w, sems)

    @pl.when(step == 0)
    def _():
        for copy in copies:
            copy.start()
        first = meta[0] == 0
        m, t = mine[...], theirs[...]
        left, right = jnp.where(first, m, t), jnp.where(first, t, m)
        att_t[:HW, :] = left.T
        att_t[HW:, :] = right.T
        att = jnp.concatenate([left, right], axis=1)
        for copy in copies:
            copy.wait()
        branch = jnp.concatenate(
            [dot(att, w[0, :, 2 * BLK : GW]), dot(att, w[1, :, 2 * BLK : GW])], axis=1
        )
        r = rows[...].astype(f32) + branch
        res[...] = r
        z, _ = norm_parts(r)
        n1 = (z * vecs[0:1, :] + vecs[1:2, :]).astype(bf16)
        low[...] = n1
        low_t[...] = n1.T

    half = step // 2
    at = (step % 2) * BLK
    g = dot(low[...], w[half, :, pl.ds(pl.multiple_of(at, BLK), BLK)])
    u = dot(low[...], w[half, :, pl.ds(pl.multiple_of(GW + at, HW), BLK)])
    sig = 1.0 / (1.0 + jnp.exp(-g))
    gs = g * sig
    hid[0] = (gs * u).astype(bf16)
    a_out[0] = (u * (sig + gs * (1.0 - sig))).astype(bf16)
    b_out[0] = gs.astype(bf16)


def hidden_call(meta, rows, mine, theirs, vecs, pieces):
    part = shape((4, HALF, BLK), bf16)
    return pl.pallas_call(
        hidden_kernel,
        grid=(4,),
        in_specs=[SM, NAT, HEADS, HEADS, whole((8, D))] + [HBM] * 16,
        out_specs=[NAT, whole((D, HALF)), whole((D, HALF)), PART, PART, PART],
        out_shape=[
            shape((HALF, D), f32),
            shape((D, HALF), bf16),
            shape((D, HALF), bf16),
            part,
            part,
            part,
        ],
        scratch_shapes=[
            pltpu.VMEM((HALF, D), bf16),
            pltpu.VMEM((2, D, MW), bf16),
            pltpu.SemaphoreType.DMA((32,)),
        ],
        compiler_params=params(62),
        cost_estimate=cost(2 * HALF * D * (2 * FF + D), 30e6, HALF * FF),
        name="hidden",
    )(meta, rows, mine, theirs, vecs, *pieces)


def down_copies(meta, pieces, dst, sems):
    z, y, c = meta[1], meta[2], meta[3]
    copies = []
    for at, piece in enumerate(pieces):
        dc, k = at // 4, at % 4
        zz = lax.rem(z - k + 4, 4)
        cc = jnp.where(c == 0, dc, 1 - dc)
        for dy in range(2):
            yy = jnp.where(y == 0, dy, 1 - dy)
            row = pl.multiple_of(((zz * 2 + yy) * 2 + cc) * 192, 192)
            copies.append(
                pltpu.make_async_copy(piece.at[dy], dst.at[pl.ds(row, 192)], sems.at[at * 2 + dy])
            )
    return copies


def mlp_back_kernel(meta, res, cot, vecs, hid, a, b, *rest):
    pieces, downs = rest[:16], rest[16:24]
    out, keep, send, gate_g, up_g, g_one, low, mine, theirs, vgrads = rest[24:34]
    acc, held, m, w, wd, sems, down_sems = rest[34:]
    step = pl.program_id(0)
    copies = piece_copies(meta, pieces, w, sems)
    down = down_copies(meta, downs, wd, down_sems)

    @pl.when(step == 0)
    def _():
        for copy in down:
            copy.start()
        z, _ = norm_parts(res[...])
        acc[...] = z * vecs[0:1, :] + vecs[1:2, :]
        for copy in down:
            copy.wait()

    @pl.when(step == 1)
    def _():
        for copy in copies:
            copy.start()

    @pl.when(step < 4)
    def _():
        held[step] = hid[0]
        acc[...] += dot(hid[0], wd[pl.ds(pl.multiple_of(step * BLK, BLK), BLK), :])

    @pl.when(step == 3)
    def _():
        z, scale = norm_parts(acc[...])
        out[...] = (z * vecs[2:3, :] + vecs[3:4, :]).astype(bf16)
        c = cot[...].astype(f32)
        vgrads[2:3, :] = jnp.sum(c * z, axis=0, keepdims=True)
        vgrads[3:4, :] = jnp.sum(c, axis=0, keepdims=True)
        back = norm_back(c, z, scale, vecs[2:3, :])
        acc[...] = back
        m[...] = back.astype(bf16)

    @pl.when(step == 4)
    def _():
        for copy in copies:
            copy.wait()

    @pl.when(step >= 4)
    def _():
        j = step - 4
        half, at = j // 2, (j % 2) * BLK
        hg = dot_t(m[...], wd[pl.ds(pl.multiple_of(j * BLK, BLK), BLK), :])
        gg = (hg * a[0].astype(f32)).astype(bf16)
        ug = (hg * b[0].astype(f32)).astype(bf16)
        gate_g[0] = gg
        up_g[0] = ug
        acc[...] += dot_t(gg, w[half, :, pl.ds(pl.multiple_of(at, BLK), BLK)]) + dot_t(
            ug, w[half, :, pl.ds(pl.multiple_of(GW + at, HW), BLK)]
        )
        val = lax.dot_general(held[j], m[...], (((0,), (0,)), ((), ())), preferred_element_type=f32)
        c = meta[3]
        parts = val.astype(bf16).reshape(2, 2, 2, 96, D)
        for y in range(2):
            for h in range(2):
                keep[h, 0, y] = jnp.where(c == 0, parts[y, 0, h], parts[y, 1, h])
                send[h, 0, y] = jnp.where(c == 0, parts[y, 1, h], parts[y, 0, h])

    @pl.when(step == 7)
    def _():
        z, scale = norm_parts(res[...])
        c = acc[...]
        vgrads[0:1, :] = jnp.sum(c * z, axis=0, keepdims=True)
        vgrads[1:2, :] = jnp.sum(c, axis=0, keepdims=True)
        back = norm_back(c, z, scale, vecs[0:1, :])
        g_one[...] = back
        back = back.astype(bf16)
        low[...] = back
        ag = dot_t(back[:, :HW], w[0, :, 2 * BLK : GW]) + dot_t(back[:, HW:], w[1, :, 2 * BLK : GW])
        ag = ag.astype(bf16)
        first = meta[0] == 0
        mine[...] = jnp.where(first, ag[:, :HW], ag[:, HW:])
        theirs[...] = jnp.where(first, ag[:, HW:], ag[:, :HW])


def mlp_back_call(meta, res, cot, vecs, hid, a, b, pieces, downs):
    early = lambda i: jnp.minimum(i, 3)
    late = lambda i: jnp.maximum(i - 4, 0)
    part = pl.BlockSpec((1, HALF, BLK), lambda i: (late(i), 0, 0))
    grad = pl.BlockSpec((2, 1, 2, 96, D), lambda i: (0, late(i), 0, 0, 0))
    return pl.pallas_call(
        mlp_back_kernel,
        grid=(8,),
        in_specs=[
            SM, NAT, NAT, whole((8, D)), pl.BlockSpec((1, HALF, BLK), lambda i: (early(i), 0, 0)), part, part,
        ] + [HBM] * 24,
        out_specs=[NAT, grad, grad, part, part, NAT, NAT, HEADS, HEADS, whole((8, D))],
        out_shape=[
            shape((HALF, D), bf16),
            shape((2, 4, 2, 96, D), bf16),
            shape((2, 4, 2, 96, D), bf16),
            shape((4, HALF, BLK), bf16),
            shape((4, HALF, BLK), bf16),
            shape((HALF, D), f32),
            shape((HALF, D), bf16),
            shape((HALF, HW), bf16),
            shape((HALF, HW), bf16),
            shape((8, D), f32),
        ],
        scratch_shapes=[
            pltpu.VMEM((HALF, D), f32),
            pltpu.VMEM((4, HALF, BLK), bf16),
            pltpu.VMEM((HALF, D), bf16),
            pltpu.VMEM((2, D, MW), bf16),
            pltpu.VMEM((FF, D), bf16),
            pltpu.SemaphoreType.DMA((32,)),
            pltpu.SemaphoreType.DMA((16,)),
        ],
        compiler_params=params(62),
        cost_estimate=cost(2 * HALF * D * 5 * FF, 40e6),
        name="mlp_back",
    )(meta, res, cot, vecs, hid, a, b, *pieces, *downs)


def wide_grads_kernel(width, meta, low_t, grads, *rest):
    c = meta[3]
    keep, send = rest[-2:]

    def put(at, val):
        stay, leave = split_core(c, val)
        cols = slice(at, at + val.shape[1])
        for z in range(4):
            for y in range(2):
                keep[0, z, y, :, cols] = stay[2 * z + y]
                send[0, z, y, :, cols] = leave[2 * z + y]

    for i in range(2):
        put(i * BLK, dot(low_t[...], grads[i]))
    if width == GW:
        put(2 * BLK, dot(rest[0][...], rest[1][...]))


def wide_grads_call(meta, low_t, grads, *out_part):
    width = GW if out_part else 2 * BLK
    tall = whole((D, HALF))
    grad = pl.BlockSpec((1, 4, 2, 48, width), lambda i: (i, 0, 0, 0, 0))
    extra = [tall, pl.BlockSpec((HALF, HW), lambda i: (0, i))] if out_part else []
    return pl.pallas_call(
        partial(wide_grads_kernel, width),
        grid=(2,),
        in_specs=[SM, tall, pl.BlockSpec((2, HALF, BLK), lambda i: (i, 0, 0))] + extra,
        out_specs=[grad] * 2,
        out_shape=[shape((2, 4, 2, 48, width), bf16)] * 2,
        compiler_params=params(20),
        cost_estimate=cost(2 * HALF * D * FF, 9e6),
        name="wide_grads",
    )(meta, low_t, grads, *out_part)


def first_grads_kernel(meta, own, other, grads, vgrads, keep, send, rows_t):
    step = pl.program_id(0)

    @pl.when(step == 0)
    def _():
        rows_t[:, :HALF] = own[...].T
        rows_t[:, HALF:] = other[...].T
        row = lax.broadcasted_iota(jnp.int32, (8, D), 0)
        four = jnp.where(row < 4, vgrads[...], 0.0)
        four = jnp.concatenate([four, jnp.zeros((120, D), f32)], axis=0).T
        keep[:, :, 3 * HW :], send[:, :, 3 * HW :] = split_core(meta[3], four)

    for j in range(3):

        @pl.when(step == j)
        def _():
            at = slice(j * HW, (j + 1) * HW)
            keep[:, :, at], send[:, :, at] = split_core(meta[3], dot(rows_t[...], grads[...]))


def first_grads_call(meta, own, other, grads, vgrads):
    grad = whole((8, 48, QW))
    return pl.pallas_call(
        first_grads_kernel,
        grid=(3,),
        in_specs=[SM, NAT, NAT, pl.BlockSpec((2 * HALF, HW), lambda i: (0, i)), whole((8, D))],
        out_specs=[grad] * 2,
        out_shape=[shape((8, 48, QW), bf16)] * 2,
        scratch_shapes=[pltpu.VMEM((D, 2 * HALF), bf16)],
        compiler_params=params(24),
        cost_estimate=cost(2 * 2 * HALF * D * 3 * HW, 8e6),
        name="first_grads",
    )(meta, own, other, grads, vgrads)


def tokens_part_kernel(grads, w, out):
    out[...] = dot_t(grads[...], w[:, : 3 * HW]).astype(out.dtype)


def tokens_part_call(grads, w):
    return pl.pallas_call(
        tokens_part_kernel,
        grid=(2,),
        in_specs=[pl.BlockSpec((HALF // 2, 3 * HW), lambda i: (i + 2, 0)), whole((D, QW))],
        out_specs=pl.BlockSpec((HALF // 2, D), lambda i: (i, 0)),
        out_shape=shape((HALF, D), bf16),
        compiler_params=params(16),
        cost_estimate=cost(2 * HALF * D * 3 * HW, 5e6),
        name="tokens_part",
    )(grads, w)


def tokens_grad_kernel(g_one, theirs, grads, w, out):
    out[...] = g_one[...] + theirs[...].astype(f32) + dot_t(grads[...], w[:, : 3 * HW])


def tokens_grad_call(g_one, theirs, grads, w):
    part = pl.BlockSpec((HALF // 2, D), lambda i: (i, 0))
    return pl.pallas_call(
        tokens_grad_kernel,
        grid=(2,),
        in_specs=[part, part, pl.BlockSpec((HALF // 2, 3 * HW), lambda i: (i, 0)), whole((D, QW))],
        out_specs=part,
        out_shape=shape((HALF, D), f32),
        compiler_params=params(16),
        cost_estimate=cost(2 * HALF * D * 3 * HW, 8e6),
        name="tokens_grad",
    )(g_one, theirs, grads, w)


def pick(a, at, axis):
    return lax.dynamic_index_in_dim(a, at, axis, keepdims=False)


def flip_x(a):
    return lax.ppermute(a, "seq", [(0, 1), (1, 0)])


def flip(bit):
    def go(a):
        n = lax.axis_size("shard")
        return lax.ppermute(a, "shard", [(s, s ^ bit) for s in range(n)])

    return go


flip_c, flip_y, flip_z, flip_far = flip(1), flip(2), flip(4), flip(8)


def turn_z(a, k):
    return lax.ppermute(a, "shard", [(s, (s + 4 * k) % 16) for s in range(16)])


def after(a, *deps):
    return lax.optimization_barrier((a,) + deps)[0]


def slot(*arrays):
    return lax.optimization_barrier(arrays)


def around(mine):
    return [turn_z(mine, k) for k in (1, 2, 3)]


def pieces_of_whole(full):
    cut = full.reshape(full.shape[0], 4, 2, 2, 48, full.shape[2])
    order = jnp.array([0, 3, 2, 1])
    return [
        cut[dh, :, dy, dc][order]
        for dc in range(2)
        for dy in range(2)
        for dh in range(full.shape[0])
    ]


def in_two(pieces):
    return [part for piece in pieces for part in (piece[:2], piece[2:])]


def add(a, b):
    return a.astype(f32) + b.astype(f32)


def turns(sends):
    return [turn_z(send, k + 1) for k, send in enumerate(sends)]


def fold(meta, ins, outs, name):
    def kernel(*refs):
        spot = refs[0][0], refs[0][1], refs[0][2]
        for (_, give), out in zip(outs, refs[1 + len(ins) :]):
            out[...] = give(spot, *refs[1 : 1 + len(ins)]).astype(bf16)

    moved = 2 * sum(a.size for a in ins)
    return pl.pallas_call(
        kernel,
        grid=(1,),
        in_specs=[SM] + [whole(a.shape) for a in ins],
        out_specs=[whole(dims) for dims, _ in outs],
        out_shape=[shape(dims, bf16) for dims, _ in outs],
        compiler_params=params(32),
        cost_estimate=cost(moved, 2 * moved),
        name=name,
    )(meta, *ins)


def cut_core(rows, cols_x, cols_y):
    def along_x(flip):
        def give(spot, keep, got):
            at = spot[0] if flip == 0 else 1 - spot[0]
            return add(keep[at, :, :, :, :cols_x], got[at, :, :, :, :cols_x])

        return give

    def along_y(flip):
        def give(spot, keep, got):
            at = spot[2] if flip == 0 else 1 - spot[2]
            return add(keep[:, :, at, :, cols_x:], got[:, :, at, :, cols_x:])

        return give

    dims_x, dims_y = (4, 2, rows, cols_x), (2, 4, rows, cols_y)
    return [(dims_x, along_x(0)), (dims_x, along_x(1)), (dims_y, along_y(0)), (dims_y, along_y(1))]


def first_two(outs):
    return [(dims, lambda spot, *refs, give=give: give(spot, *refs[:2])) for dims, give in outs]


def cut_plane(rows, cols_x, cols_y, first):
    def along_y(flip):
        def give(spot, *refs):
            at = spot[2] if flip == 0 else 1 - spot[2]
            return add(refs[first][:, at], refs[first + 1][:, at])

        return give

    def along_x(flip):
        def give(spot, *refs):
            at = spot[0] if flip == 0 else 1 - spot[0]
            return add(refs[first + 2][at], refs[first + 3][at])

        return give

    dims_a, dims_b = (4, rows, cols_x), (4, rows, cols_y)
    return [(dims_a, along_y(0)), (dims_a, along_y(1)), (dims_b, along_x(0)), (dims_b, along_x(1))]


def cut_line(rows, cols, first, count):
    def part(k):
        def give(spot, *refs):
            at = lax.rem(spot[1] + k, 4)
            sums = [
                add(refs[first + 2 * i][at], refs[first + 2 * i + 1][at]) for i in range(count)
            ]
            return sums[0] if count == 1 else jnp.concatenate(sums, axis=-1)

        return give

    return [((rows, cols), part(k)) for k in range(4)]


def cut_near(rows, cols, first, count):
    def part(flip):
        def give(spot, *refs):
            odd = lax.rem(spot[1] + flip, 2)
            return jnp.stack(
                [
                    jnp.concatenate(
                        [
                            add(refs[first + 2 * i][odd + 2 * b], refs[first + 2 * i + 1][odd + 2 * b])
                            for i in range(count)
                        ],
                        axis=-1,
                    )
                    for b in range(2)
                ]
            )

        return give

    return [((2, rows, cols), part(0)), ((2, rows, cols), part(1))]


def cut_far(rows, cols, first):
    def part(flip):
        def give(spot, *refs):
            at = lax.rem(spot[1] // 2 + flip, 2)
            return add(refs[first][at], refs[first + 1][at])

        return give

    return [((rows, cols), part(0)), ((rows, cols), part(1))]


def cut_z(rows, cols):
    def part(k):
        def give(spot, keep, got, *_):
            at = lax.rem(spot[1] + k, 4)
            return add(keep[:, at], got[:, at])

        return give

    return [((2, 2, rows, cols), part(k)) for k in range(4)]


def pair(dims, first):
    return [(dims, lambda spot, *refs: add(refs[first][...], refs[first + 1][...]))]


def total_of(rows, cols, first):
    def give(spot, *refs):
        near, *gots = [refs[first + i][...].astype(f32) for i in range(4)]
        return near + gots[0] + gots[1] + gots[2]

    return [((rows, cols), give)]


def halves(mine, other, x):
    return jnp.where(x == 0, jnp.stack([mine, other]), jnp.stack([other, mine])).astype(f32)


def whole_of_split(keep, send):
    both = jnp.stack([keep, send], axis=3)
    return both.transpose(1, 2, 3, 4, 0, 5).reshape(D, -1)


def whole_of_down(keep, send):
    return jnp.stack([keep, send], axis=3).transpose(1, 2, 3, 0, 4, 5).reshape(FF, D)


def local(
    tokens,
    doc_lengths,
    qkv_weight,
    out_weight,
    gate_weight,
    up_weight,
    down_weight,
    norm1_gain,
    norm1_bias,
    norm2_gain,
    norm2_bias,
    cotangent,
):
    n = lax.axis_size("shard")
    fast = n == 16
    x = lax.axis_index("seq").astype(jnp.int32)
    shard = lax.axis_index("shard").astype(jnp.int32)
    zero = jnp.zeros((), jnp.int32)
    z, y, c = (shard // 4, (shard // 2) % 2, shard % 2) if fast else (zero, zero, zero)

    rows = tokens[0]
    cot = cotangent[0]
    lengths = lax.dynamic_slice_in_dim(doc_lengths, shard, 1, 0)[0]
    ends = jnp.cumsum(lengths).astype(jnp.int32)
    hx = x if fast else zero
    meta = jnp.concatenate([jnp.stack([x, z, y, c, hx]), jnp.zeros((3,), jnp.int32), ends])
    spots = jnp.arange(2 * HALF, dtype=jnp.int32)
    spots = jnp.where(spots < HALF, spots + x * HALF, spots - x * HALF)
    passed = spots[:, None] >= ends[None, :]
    place = spots - jnp.sum(jnp.where(passed, lengths[None, :], 0), axis=1)
    frequency = rope_base ** (-jnp.arange(HD // 2, dtype=f32) * 2.0 / HD)
    angles = place.astype(f32)[:, None] * frequency[None, :]
    cosine = jnp.tile(jnp.cos(angles), (1, 4))
    sine = jnp.sin(angles)
    sine = jnp.concatenate([-sine, sine, -sine, sine], axis=1)

    vec_block = jnp.stack([norm1_gain, norm1_bias, norm2_gain, norm2_bias], axis=1)
    vec_block = jnp.pad(vec_block, ((0, 0), (0, 124)))

    def my_heads(w):
        mine = lax.dynamic_slice_in_dim(w.reshape(w.shape[0], 3, 2, HW), x, 1, 2)
        mine = mine.reshape(w.shape[0], 3, 3, 128).transpose(0, 2, 1, 3)
        return mine.reshape(w.shape[0], 3 * HW)

    def half_of(w, at):
        cols = w.shape[1] // 2
        return jnp.where(at == 0, w[:, :cols], w[:, cols:])

    if fast:
        first = jnp.concatenate([my_heads(qkv_weight), vec_block], axis=1)
        wide, wide_o = [
            jnp.concatenate([half_of(w, at) for w in (gate_weight, out_weight, up_weight)], axis=1)
            for at in (x, 1 - x)
        ]
        zq, yd, yo = around(first), flip_y(down_weight), flip_y(wide_o)
        first, zq, wide, cosine, sine, rows_late, yd = slot(
            first, zq, wide, cosine, sine, rows, yd
        )
        wide_late, wide1 = wide, turn_z(wide, 1)
        aq = jnp.stack([first] + zq)
        byq, rows_other = flip_y(aq), flip_x(rows_late)
        wide2, wide3 = turn_z(wide_late, 2), turn_z(wide_late, 3)
        aq, byq, wide, wide1, wide3, down, yd, yo = slot(aq, byq, wide, wide1, wide3, down_weight, yd, yo)
        a0 = jnp.stack([wide, wide1])
        d0 = jnp.stack([down, yd])
        caq, cbyq = flip_c(aq), flip_c(byq)
        caq, cbyq, a0, rows_other, d0 = slot(caq, cbyq, a0, rows_other, d0)
        by0, bx0 = flip_y(a0), flip_x(a0)
        first_pieces = [aq, byq, caq, cbyq]
    else:
        rows_other = flip_x(rows)

        def gathered(w):
            return lax.all_gather(w, "shard", axis=0, tiled=True)

        first = jnp.concatenate([my_heads(gathered(qkv_weight)), gathered(vec_block)], axis=1)
        first_pieces = pieces_of_whole(first[None])

        def in_halves(w):
            return gathered(w).reshape(D, 2, -1).transpose(1, 0, 2)

        wide_all = jnp.concatenate([in_halves(w) for w in (gate_weight, out_weight, up_weight)], axis=2)
        pieces = in_two(pieces_of_whole(wide_all))
        down_all = gathered(down_weight).reshape(4, 2, 2, 192, D)
        down_pieces = [down_all[(4 - k) % 4, :, dc] for dc in range(2) for k in range(4)]

    q, k, kt, v, vt, w1, vecs = qkv_call(meta, rows, rows_other, cosine, sine, first_pieces)
    if fast:
        q, a0, by0, bx0, wide2, d0 = slot(q, a0, by0, bx0, wide2, d0)
        a1 = jnp.stack([wide2, wide3])
        q, a1 = slot(q, a1)
        by1, bx1, d1 = flip_y(a1), flip_x(a1), turn_z(d0, 1)
        ca0, cby0 = flip_c(a0), flip_c(by0)
    att_theirs, at_other, lse_other = attend_call(meta, q, k, vt, 1)
    if fast:
        q, att_theirs, by1, bx1, ca0, cby0, d1, by0, bx0, a1 = slot(
            q, att_theirs, by1, bx1, ca0, cby0, d1, by0, bx0, a1
        )
    att_got = flip_x(att_theirs)
    if fast:
        bxy0, bxy1, d2 = flip_x(by0[1]), flip_y(bx1), turn_z(d1, 1)
        cbx0 = flip_c(bx0)
    att_mine, at_own, lse_own = attend_call(meta, q, k, vt, 0)
    if fast:
        att_mine, att_got, bxy0, bxy1, d2, cbx0, by1, a1, bx1 = slot(
            att_mine, att_got, bxy0, bxy1, d2, cbx0, by1, a1, bx1
        )
        bxy0 = jnp.stack([yo, bxy0])
        cby1 = flip_c(by1)
        cbx1, cbxy0, cbxy1, ca1 = flip_c(bx1), flip_c(bxy0), flip_c(bxy1), flip_c(a1)
        att_mine, cbx1, cby1, cbxy0, cbxy1, ca1, d0, d1, d2 = slot(
            att_mine, cbx1, cby1, cbxy0, cbxy1, ca1, d0, d1, d2
        )
        d3, cd0, cd1, cd2 = turn_z(d2, 1), flip_c(d0), flip_c(d1), flip_c(d2)
        pieces = [a0, a1, bx0, bx1, by0, by1, bxy0, bxy1]
        pieces += [ca0, ca1, cbx0, cbx1, cby0, cby1, cbxy0, cbxy1]
    res, low_t, att_t, hid, part_a, part_b = hidden_call(
        meta, rows, att_mine, att_got, vecs, pieces
    )
    if fast:
        hid, d3, cd0, cd1, cd2 = slot(hid, d3, cd0, cd1, cd2)
        down_pieces = [d0, d1, d2, d3, cd0, cd1, cd2, flip_c(d3)]
    out, keep_d, send_d, gate_g, up_g, g_one, g_low, g_mine, g_theirs, vgrads = mlp_back_call(
        meta, res, cot, vecs, hid, part_a, part_b, pieces, down_pieces
    )

    if fast:
        keep_d, send_d, g_theirs, gate_g = slot(keep_d, send_d, g_theirs, gate_g)
        got_d = flip_c(send_d)
    keep_g, send_g = wide_grads_call(meta, low_t, gate_g, att_t, g_low)
    if fast:
        send_g, g_theirs, got_d, up_g = slot(send_g, g_theirs, got_d, up_g)
        got_g = flip_c(send_g)
    g_other = flip_x(g_theirs)
    keep_u, send_u = wide_grads_call(meta, low_t, up_g)
    if fast:
        send_u, got_g, got_d, g_other = slot(send_u, got_g, got_d, g_other)
        near_ga, sent_ga, near_gb, sent_gb, *part_d = fold(
            meta,
            (keep_g, got_g, keep_d, got_d),
            first_two(cut_core(48, GA, GW - GA))
            + [(dims, lambda spot, *refs, give=give: give(spot, *refs[2:])) for dims, give in cut_z(96, D)],
            "fold",
        )
        sent_ga, sent_gb, g_other, part_d, send_u = slot(sent_ga, sent_gb, g_other, part_d, send_u)
        got_ga, got_gb, got_u = flip_x(sent_ga), flip_y(sent_gb), flip_c(send_u)
        got_d = turn_z(part_d[3], 1)
    back_args = (q, k, kt, v, g_mine, g_other, at_own, at_other, lse_own, lse_other, cosine, sine)
    grads = attend_back_call(meta, *back_args, 0, 2)
    if fast:
        grads, got_ga, got_gb, got_u, got_d = slot(grads, got_ga, got_gb, got_u, got_d)
        near_ga, sent_ga, near_gb, sent_gb, near_ua, sent_ua, near_ub, sent_ub, sent_d = fold(
            meta,
            (keep_u, got_u, near_ga, got_ga, near_gb, got_gb, part_d[2], got_d),
            cut_plane(48, GA, GW - GA, 2) + first_two(cut_core(48, BLK, BLK)) + pair((2, 2, 96, D), 6),
            "fold",
        )
        grads, sent_ua, sent_ub, sent_ga, sent_gb, sent_d = slot(
            grads, sent_ua, sent_ub, sent_ga, sent_gb, sent_d
        )
        got_ua, got_ub, got_d = flip_x(sent_ua), flip_y(sent_ub), turn_z(sent_d, 1)
    grads = attend_back_call(meta, *back_args, 2, 1, grads)
    if fast:
        grads, got_ua, got_ub, got_d, sent_ga, sent_gb = slot(
            grads, got_ua, got_ub, got_d, sent_ga, sent_gb
        )

        def joined_sends(spot, *refs):
            return jnp.concatenate(
                [refs[6][...].astype(f32), add(refs[0][:, 1 - spot[2]], refs[1][:, 1 - spot[2]])], axis=-1
            )

        def joined_sends_x(spot, *refs):
            return jnp.concatenate(
                [refs[7][...].astype(f32), add(refs[2][1 - spot[0]], refs[3][1 - spot[0]])], axis=-1
            )

        plane = cut_plane(48, BLK, BLK, 0)
        near_ua, near_ub, sent_y, sent_x, sent_d = fold(
            meta,
            (near_ua, got_ua, near_ub, got_ub, part_d[1], got_d, sent_ga, sent_gb),
            [
                plane[0],
                plane[2],
                ((4, 48, GA + BLK), joined_sends),
                ((4, 48, GW - GA + BLK), joined_sends_x),
            ]
            + pair((2, 2, 96, D), 4),
            "fold",
        )
        grads, sent_y, sent_x, sent_d = slot(grads, sent_y, sent_x, sent_d)
        got_y, got_x, got_d = flip_y(sent_y), flip_x(sent_x), turn_z(sent_d, 1)
    keep_q, send_q = first_grads_call(meta, rows, rows_other, grads, vgrads)
    if fast:
        keep_q, send_q, got_y, got_x, got_d, grads = slot(keep_q, send_q, got_y, got_x, got_d, grads)
        got_q = flip_c(send_q)

        def line(flip):
            def give(spot, ga, gb, ua, ub, gy, gx, *_):
                odd = lax.rem(spot[1] + flip, 2)
                parts = []
                for b in range(2):
                    at = odd + 2 * b
                    parts.append(
                        jnp.concatenate(
                            [
                                add(ga[at], gy[at, :, :GA]),
                                add(gb[at], gx[at, :, : GW - GA]),
                                add(ua[at], gy[at, :, GA:]),
                                add(ub[at], gx[at, :, GW - GA :]),
                            ],
                            axis=-1,
                        )
                    )
                return jnp.stack(parts)

            return give

        cut = (4, 2, 48, QW)
        near_w, sent_w, near_d, sent_d = fold(
            meta,
            (near_ga, near_gb, near_ua, near_ub, got_y, got_x, part_d[0], got_d),
            [
                ((2, 48, MW), line(0)),
                ((2, 48, MW), line(1)),
                ((2, 96, D), lambda spot, *refs: add(refs[6][:, spot[2]], refs[7][:, spot[2]])),
                ((2, 96, D), lambda spot, *refs: add(refs[6][:, 1 - spot[2]], refs[7][:, 1 - spot[2]])),
            ],
            "fold",
        )
        sent_w, sent_d, grads = slot(sent_w, sent_d, grads)
        got_w, got_d = flip_z(sent_w), flip_y(sent_d)
    theirs = tokens_part_call(grads, w1)
    if fast:
        got_q, theirs = slot(got_q, theirs)
        near_q, sent_q = fold(
            meta,
            (keep_q.reshape(cut), got_q.reshape(cut)),
            [
                ((4, 48, QW), lambda spot, keep, got: add(keep[:, spot[2]], got[:, spot[2]])),
                ((4, 48, QW), lambda spot, keep, got: add(keep[:, 1 - spot[2]], got[:, 1 - spot[2]])),
            ],
            "fold",
        )
        sent_q, theirs = slot(sent_q, theirs)
        got_q, theirs = flip_y(sent_q), flip_x(theirs)
        got_q, got_w, got_d = slot(got_q, got_w, got_d)
        near_q, sent_q, near_w, sent_w, total_d = fold(
            meta,
            (near_q, got_q, near_w, got_w, near_d, got_d),
            cut_near(48, QW, 0, 1) + cut_far(48, MW, 2) + pair((2, 96, D), 4),
            "fold",
        )
        sent_q, sent_w, total_d, theirs = slot(sent_q, sent_w, total_d, theirs)
        got_q, got_w, other_d = flip_z(sent_q), flip_far(sent_w), flip_x(total_d)
        got_q, got_w, theirs = slot(got_q, got_w, theirs)
        near_q, sent_q, total_w = fold(
            meta,
            (near_q, got_q, near_w, got_w),
            cut_far(48, QW, 0) + pair((48, MW), 2),
            "fold",
        )
        sent_q, total_w, theirs = slot(sent_q, total_w, theirs)
        got_q, other_w = flip_far(sent_q), flip_x(total_w)
    else:
        theirs = flip_x(theirs)
    grad_in = tokens_grad_call(g_one, theirs, grads, w1)
    if fast:
        got_q, grad_in, other_w, other_d = slot(got_q, grad_in, other_w, other_d)
        (total_q,) = fold(meta, (near_q, got_q), pair((48, QW), 0), "fold")
        other_q = flip_x(total_q)

    def joined(part):
        n_rows = part.shape[1]
        part = part.reshape(2, n_rows, 3, 3, 128).transpose(1, 3, 0, 2, 4)
        return part.reshape(n_rows, 3 * D)

    if fast:
        grad_qkv = joined(halves(total_q[:, : 3 * HW], other_q[:, : 3 * HW], x))
        grad_w = halves(total_w, other_w, x)
        grad_gate = jnp.concatenate([grad_w[0, :, : 2 * BLK], grad_w[1, :, : 2 * BLK]], axis=1)
        grad_out = jnp.concatenate([grad_w[0, :, 2 * BLK : GW], grad_w[1, :, 2 * BLK : GW]], axis=1)
        grad_up = jnp.concatenate([grad_w[0, :, GW:], grad_w[1, :, GW:]], axis=1)
        grad_down = add(total_d, other_d).reshape(-1, D)
        vec_own = add(total_q[:, 3 * HW : 3 * HW + 4], other_q[:, 3 * HW : 3 * HW + 4]).T
    else:

        def owned(a):
            part = lax.psum_scatter(a, "shard", scatter_dimension=0, tiled=True)
            return lax.psum(part, "seq").astype(f32)

        grad_g = whole_of_split(keep_g, send_g)
        grad_gate = owned(jnp.concatenate([grad_g[:, : 2 * BLK], grad_g[:, GW : GW + 2 * BLK]], axis=1))
        grad_out = owned(jnp.concatenate([grad_g[:, 2 * BLK : GW], grad_g[:, GW + 2 * BLK :]], axis=1))
        grad_up = owned(whole_of_split(keep_u, send_u))
        grad_down = owned(whole_of_down(keep_d, send_d))
        mine = jnp.stack([keep_q, send_q], axis=1).reshape(D, QW)[:, : 3 * HW]
        none = jnp.zeros_like(mine)
        both = jnp.stack([jnp.where(x == 0, mine, none), jnp.where(x == 0, none, mine)])
        grad_qkv = owned(joined(both))
        vec_grads = lax.psum(vgrads[:4], ("seq", "shard"))
        vec_own = lax.dynamic_slice_in_dim(vec_grads, shard * (D // n), D // n, 1)
    return (
        out[None],
        grad_in[None],
        grad_qkv,
        grad_out,
        grad_gate,
        grad_up,
        grad_down,
        vec_own[0],
        vec_own[1],
        vec_own[2],
        vec_own[3],
    )


def solution(mesh):
    placed = (
        P("shard", "seq", None),
        P(),
        P("shard", None),
        P("shard", None),
        P("shard", None),
        P("shard", None),
        P("shard", None),
        P("shard"),
        P("shard"),
        P("shard"),
        P("shard"),
        P("shard", "seq", None),
    )
    return jax.shard_map(
        local,
        mesh=mesh,
        in_specs=placed,
        out_specs=(
            P("shard", "seq", None),
            P("shard", "seq", None),
            P("shard", None),
            P("shard", None),
            P("shard", None),
            P("shard", None),
            P("shard", None),
            P("shard"),
            P("shard"),
            P("shard"),
            P("shard"),
        ),
        check_vma=False,
    )
```

```python
from functools import partial

import jax
import jax.numpy as jnp
from jax import lax
from jax.experimental import pallas as pl
from jax.experimental.pallas import tpu as pltpu
from jax.sharding import PartitionSpec as P

D = 768
H = 12
HD = 64
FF = 3072
HALF = 512
PAIRS = H // 2
BLK = 768
HW = D // 2
GW = 2 * BLK + HW
MW = GW + 2 * BLK
GA = 1024
QW = 3 * HW + 128
MIB = 1 << 20

rope_base = 1000.0
norm_eps = 1e-05
big_negative = -1e30

bf16 = jnp.bfloat16
f32 = jnp.float32
VM = pl.BlockSpec(memory_space=pltpu.VMEM)
SM = pl.BlockSpec(memory_space=pltpu.SMEM)
HBM = pl.BlockSpec(memory_space=pl.ANY)


def dot(a, b):
    return lax.dot_general(a, b, (((1,), (0,)), ((), ())), preferred_element_type=f32)


def dot_t(a, b):
    return lax.dot_general(a, b, (((1,), (1,)), ((), ())), preferred_element_type=f32)


def params(mib):
    return pltpu.CompilerParams(vmem_limit_bytes=mib * MIB)


def cost(flops, moved, trans=0):
    return pl.CostEstimate(flops=int(flops), bytes_accessed=int(moved), transcendentals=int(trans))


def shape(dims, kind):
    return jax.ShapeDtypeStruct(dims, kind)


def piece_copies(meta, pieces, dst, sems):
    x, z, y, c = meta[4], meta[1], meta[2], meta[3]
    copies = []
    for at in range(8):
        dc, dy, dh = at // 4, (at // 2) % 2, at % 2
        h = jnp.where(x == 0, dh, 1 - dh)
        yy = jnp.where(y == 0, dy, 1 - dy)
        cc = jnp.where(c == 0, dc, 1 - dc)
        for k in range(4):
            zz = lax.rem(z - k + 4, 4)
            row = pl.multiple_of(((zz * 2 + yy) * 2 + cc) * 48, 48)
            copies.append(
                pltpu.make_async_copy(
                    pieces[at * 2 + k // 2].at[k % 2], dst.at[h, pl.ds(row, 48)], sems.at[at * 4 + k]
                )
            )
    return copies


def spin(u, cosine, sine):
    lane = lax.broadcasted_iota(jnp.int32, u.shape, 1)
    swapped = jnp.where(lane % HD < HD // 2, pltpu.roll(u, 96, 1), pltpu.roll(u, 32, 1))
    return u * cosine + swapped * sine


def qkv_kernel(meta, own, other, cosine, sine, *rest):
    pieces = rest[:4]
    q_out, k_out, kt_out, v_out, vt_out, w_out, vecs, w, sems, out_sem = rest[4:]
    step = pl.program_id(0)

    @pl.when(step == 0)
    def _():
        z, y, c = meta[1], meta[2], meta[3]
        copies = []
        for at, piece in enumerate(pieces):
            yy = jnp.where(y == 0, at % 2, 1 - at % 2)
            cc = jnp.where(c == 0, at // 2, 1 - at // 2)
            for k in range(4):
                zz = lax.rem(z - k + 4, 4)
                row = pl.multiple_of(((zz * 2 + yy) * 2 + cc) * 48, 48)
                copies.append(
                    pltpu.make_async_copy(piece.at[k], w.at[pl.ds(row, 48)], sems.at[at * 4 + k])
                )
        for copy in copies:
            copy.start()
        for copy in copies:
            copy.wait()
        pltpu.make_async_copy(w, w_out, out_sem).start()
        vecs[...] = w[:, 3 * HW :].astype(f32).T[:8]

    part = w[:, pl.ds(pl.multiple_of(step * HW, HW), HW)]
    for half, rows in enumerate((own, other)):
        at = slice(half * HALF, (half + 1) * HALF)
        cs, sn = cosine[at, :], sine[at, :]
        qkv = dot(rows[...], part)
        q_out[at, :] = spin(qkv[:, :128], cs, sn).astype(bf16)
        kr = spin(qkv[:, 128:256], cs, sn).astype(bf16)
        vs = qkv[:, 256:].astype(bf16)
        k_out[at, :] = kr
        kt_out[:, at] = kr.T
        v_out[at, :] = vs
        vt_out[:, at] = vs.T

    @pl.when(step == 2)
    def _():
        pltpu.make_async_copy(w, w_out, out_sem).wait()


def qkv_call(meta, own, other, cosine, sine, pieces):
    rows = 2 * HALF
    full = pl.BlockSpec((rows, 128), lambda i: (0, 0))
    x_spec = pl.BlockSpec((HALF, D), lambda i: (0, 0))
    nat = pl.BlockSpec((rows, 128), lambda i: (0, i))
    tr = pl.BlockSpec((128, rows), lambda i: (i, 0))
    return pl.pallas_call(
        qkv_kernel,
        grid=(3,),
        in_specs=[SM, x_spec, x_spec, full, full] + [HBM] * 4,
        out_specs=[nat, nat, tr, nat, tr, HBM, pl.BlockSpec((8, D), lambda i: (0, 0))],
        out_shape=[
            shape((rows, HW), bf16),
            shape((rows, HW), bf16),
            shape((HW, rows), bf16),
            shape((rows, HW), bf16),
            shape((HW, rows), bf16),
            shape((D, QW), bf16),
            shape((8, D), f32),
        ],
        scratch_shapes=[
            pltpu.VMEM((D, QW), bf16),
            pltpu.SemaphoreType.DMA((16,)),
            pltpu.SemaphoreType.DMA,
        ],
        compiler_params=params(62),
        cost_estimate=cost(2 * rows * D * 3 * HW, 14e6),
        name="qkv",
    )(meta, own, other, cosine, sine, *pieces)


def segment_of(meta, pos):
    seg = jnp.zeros(pos.shape, jnp.int32)
    for d in range(8):
        seg = seg + jnp.where(pos >= meta[8 + d], 1, 0)
    return seg


def bias_of(meta, key_base, keys, query_base):
    row = lax.broadcasted_iota(jnp.int32, (keys, 128), 0)
    key_pos = jnp.where(row < HALF, row + key_base[0], row - HALF + key_base[1])
    key_seg = segment_of(meta, key_pos)[:, :1]
    key_pos = key_pos[:, :1]
    query_pos = lax.broadcasted_iota(jnp.int32, (8, HALF), 1) + query_base
    query_seg = segment_of(meta, query_pos)[:1]
    query_pos = query_pos[:1]
    near = jnp.abs(key_pos - query_pos) <= HALF
    return jnp.where((key_seg == query_seg) & near, 0.0, big_negative).astype(f32)


def head_part(block, hh, scale=None):
    lane = lax.broadcasted_iota(jnp.int32, block.shape, 1)
    kept = jnp.where((lane // HD) == hh, block, jnp.zeros_like(block))
    return kept if scale is None else kept * jnp.asarray(scale, block.dtype)


def bases(meta):
    return meta[0] * HALF, HALF - meta[0] * HALF


def attend_kernel(side, meta, q, k, vt, att, att_t, lse, bias):
    @pl.when(pl.program_id(0) == 0)
    def _():
        both = bases(meta)
        bias[...] = bias_of(meta, both, 2 * HALF, both[side])

    parts = []
    for hh in range(2):
        qz = head_part(q[...], hh, HD**-0.5)
        s = dot_t(k[...], qz) + bias[...]
        peak = jnp.max(s, axis=0, keepdims=True)
        e = jnp.exp(s - peak)
        total = jnp.sum(e, axis=0, keepdims=True)
        o = dot(vt[hh * HD : (hh + 1) * HD, :], e.astype(bf16)) * (1.0 / total)
        parts.append(o.astype(bf16))
        lse[0, hh : hh + 1, :] = peak + jnp.log(total)
    both = jnp.concatenate(parts, axis=0)
    att_t[...] = both
    att[...] = both.T


def attend_call(meta, q, k, vt, side):
    return pl.pallas_call(
        partial(attend_kernel, side),
        grid=(3,),
        in_specs=[
            SM,
            pl.BlockSpec((HALF, 128), lambda i: (side, i)),
            pl.BlockSpec((2 * HALF, 128), lambda i: (0, i)),
            pl.BlockSpec((128, 2 * HALF), lambda i: (i, 0)),
        ],
        out_specs=[
            pl.BlockSpec((HALF, 128), lambda i: (0, i)),
            pl.BlockSpec((128, HALF), lambda i: (i, 0)),
            pl.BlockSpec((1, 2, HALF), lambda i: (i, 0, 0)),
        ],
        out_shape=[
            shape((HALF, HW), bf16),
            shape((HW, HALF), bf16),
            shape((3, 2, HALF), f32),
        ],
        scratch_shapes=[pltpu.VMEM((2 * HALF, HALF), f32)],
        compiler_params=params(24),
        cost_estimate=cost(4 * 4 * 6 * 2 * HALF * HALF * HD, 4e6, 6 * 2 * HALF * HALF),
        name="attend",
    )(meta, q, k, vt)


def attend_back_kernel(
    meta, q, k, kt, v, g_own, g_other, at_own, at_other, lse_own, lse_other, cosine, sine, grads, bias,
):
    @pl.when(pl.program_id(0) == 0)
    def _():
        both = bases(meta)
        for side in range(2):
            bias[side] = bias_of(meta, both, 2 * HALF, both[side])

    dk = dv = None
    for side, (g, at, lse) in enumerate(((g_own, at_own, lse_own), (g_other, at_other, lse_other))):
        rows = slice(side * HALF, (side + 1) * HALF)
        prod = g[...].T.astype(f32) * at[...].astype(f32)
        parts = []
        for hh in range(2):
            qz = head_part(q[rows, :], hh, HD**-0.5)
            gz = head_part(g[...], hh)
            delta = jnp.sum(prod[hh * HD : (hh + 1) * HD, :], axis=0, keepdims=True)
            s = dot_t(k[...], qz) + bias[side]
            p = jnp.exp(s - lse[0, hh : hh + 1, :])
            dp = dot_t(v[...], gz)
            ds = (p * (dp - delta)).astype(bf16)
            parts.append(dot(kt[hh * HD : (hh + 1) * HD, :], ds) * HD**-0.5)
            gk, gv = dot(ds, qz), dot(p.astype(bf16), gz)
            dk, dv = (gk, gv) if dk is None else (dk + gk, dv + gv)
        dq = jnp.concatenate(parts, axis=0).T
        grads[rows, :128] = spin(dq, cosine[rows, :], -sine[rows, :]).astype(bf16)
    grads[:, 128:256] = spin(dk, cosine[...], -sine[...]).astype(bf16)
    grads[:, 256:] = dv.astype(bf16)


def attend_back_call(meta, q, k, kt, v, g_own, g_other, at_own, at_other, lse_own, lse_other, cosine, sine, begin, count, done=None):
    nat = pl.BlockSpec((HALF, 128), lambda i: (0, begin + i))
    wide = pl.BlockSpec((2 * HALF, 128), lambda i: (0, begin + i))
    tall = pl.BlockSpec((128, HALF), lambda i: (begin + i, 0))
    row = pl.BlockSpec((1, 2, HALF), lambda i: (begin + i, 0, 0))
    table = pl.BlockSpec((2 * HALF, 128), lambda i: (0, 0))
    extra = () if done is None else (done,)

    def kernel(*refs):
        attend_back_kernel(*refs[:13], *refs[13 + len(extra) :])

    return pl.pallas_call(
        kernel,
        grid=(count,),
        in_specs=[
            SM, wide, wide, pl.BlockSpec((128, 2 * HALF), lambda i: (begin + i, 0)), wide,
            nat, nat, tall, tall, row, row, table, table,
        ] + [HBM] * len(extra),
        out_specs=pl.BlockSpec((2 * HALF, HW), lambda i: (0, begin + i)),
        out_shape=shape((2 * HALF, 3 * HW), bf16),
        input_output_aliases={13: 0} if extra else {},
        scratch_shapes=[pltpu.VMEM((2, 2 * HALF, HALF), f32)],
        compiler_params=params(36),
        cost_estimate=cost(4 * 10 * 2 * count * 4 * HALF * HALF * HD, 12e6, 2 * count * 4 * HALF * HALF),
        name="attend_back",
    )(meta, q, k, kt, v, g_own, g_other, at_own, at_other, lse_own, lse_other, cosine, sine, *extra)


def norm_parts(r):
    centered = r - jnp.mean(r, axis=-1, keepdims=True)
    scale = lax.rsqrt(jnp.mean(centered * centered, axis=-1, keepdims=True) + norm_eps)
    return centered * scale, scale


def norm_back(c, z, scale, gain):
    e = c * gain
    return (e - jnp.mean(e, axis=-1, keepdims=True) - z * jnp.mean(e * z, axis=-1, keepdims=True)) * scale


def split_core(c, val):
    parts = val.astype(bf16).reshape(8, 2, 48, val.shape[1])
    return (
        jnp.where(c == 0, parts[:, 0], parts[:, 1]),
        jnp.where(c == 0, parts[:, 1], parts[:, 0]),
    )


def whole(dims):
    return pl.BlockSpec(dims, lambda i: (0,) * len(dims))


NAT = whole((HALF, D))
PART = pl.BlockSpec((1, HALF, BLK), lambda i: (i % 4, 0, 0))
WIDE = pl.BlockSpec((1, D, BLK), lambda i: ((i % 4) // 2, 0, i % 2))
DOWN = pl.BlockSpec((BLK, D), lambda i: (i % 4, 0))
HEADS = whole((HALF, HW))


def hidden_kernel(meta, rows, mine, theirs, vecs, *rest):
    res, low_t, att_t, hid, a_out, b_out, low, w, sems = rest[16:]
    step = pl.program_id(0)
    copies = piece_copies(meta, rest[:16], w, sems)

    @pl.when(step == 0)
    def _():
        for copy in copies:
            copy.start()
        first = meta[0] == 0
        m, t = mine[...], theirs[...]
        left, right = jnp.where(first, m, t), jnp.where(first, t, m)
        att_t[:HW, :] = left.T
        att_t[HW:, :] = right.T
        att = jnp.concatenate([left, right], axis=1)
        for copy in copies:
            copy.wait()
        branch = jnp.concatenate(
            [dot(att, w[0, :, 2 * BLK : GW]), dot(att, w[1, :, 2 * BLK : GW])], axis=1
        )
        r = rows[...].astype(f32) + branch
        res[...] = r
        z, _ = norm_parts(r)
        n1 = (z * vecs[0:1, :] + vecs[1:2, :]).astype(bf16)
        low[...] = n1
        low_t[...] = n1.T

    half = step // 2
    at = (step % 2) * BLK
    g = dot(low[...], w[half, :, pl.ds(pl.multiple_of(at, BLK), BLK)])
    u = dot(low[...], w[half, :, pl.ds(pl.multiple_of(GW + at, HW), BLK)])
    sig = 1.0 / (1.0 + jnp.exp(-g))
    gs = g * sig
    hid[0] = (gs * u).astype(bf16)
    a_out[0] = (u * (sig + gs * (1.0 - sig))).astype(bf16)
    b_out[0] = gs.astype(bf16)


def hidden_call(meta, rows, mine, theirs, vecs, pieces):
    part = shape((4, HALF, BLK), bf16)
    return pl.pallas_call(
        hidden_kernel,
        grid=(4,),
        in_specs=[SM, NAT, HEADS, HEADS, whole((8, D))] + [HBM] * 16,
        out_specs=[NAT, whole((D, HALF)), whole((D, HALF)), PART, PART, PART],
        out_shape=[
            shape((HALF, D), f32),
            shape((D, HALF), bf16),
            shape((D, HALF), bf16),
            part,
            part,
            part,
        ],
        scratch_shapes=[
            pltpu.VMEM((HALF, D), bf16),
            pltpu.VMEM((2, D, MW), bf16),
            pltpu.SemaphoreType.DMA((32,)),
        ],
        compiler_params=params(62),
        cost_estimate=cost(2 * HALF * D * (2 * FF + D), 30e6, HALF * FF),
        name="hidden",
    )(meta, rows, mine, theirs, vecs, *pieces)


def down_copies(meta, pieces, dst, sems):
    z, y, c = meta[1], meta[2], meta[3]
    copies = []
    for at, piece in enumerate(pieces):
        dc, k = at // 4, at % 4
        zz = lax.rem(z - k + 4, 4)
        cc = jnp.where(c == 0, dc, 1 - dc)
        for dy in range(2):
            yy = jnp.where(y == 0, dy, 1 - dy)
            row = pl.multiple_of(((zz * 2 + yy) * 2 + cc) * 192, 192)
            copies.append(
                pltpu.make_async_copy(piece.at[dy], dst.at[pl.ds(row, 192)], sems.at[at * 2 + dy])
            )
    return copies


def mlp_back_kernel(meta, res, cot, vecs, hid, a, b, *rest):
    pieces, downs = rest[:16], rest[16:24]
    out, keep, send, gate_g, up_g, g_one, low, mine, theirs, vgrads = rest[24:34]
    acc, held, m, w, wd, sems, down_sems = rest[34:]
    step = pl.program_id(0)
    copies = piece_copies(meta, pieces, w, sems)
    down = down_copies(meta, downs, wd, down_sems)

    @pl.when(step == 0)
    def _():
        for copy in down:
            copy.start()
        z, _ = norm_parts(res[...])
        acc[...] = z * vecs[0:1, :] + vecs[1:2, :]
        for copy in down:
            copy.wait()

    @pl.when(step == 1)
    def _():
        for copy in copies:
            copy.start()

    @pl.when(step < 4)
    def _():
        held[step] = hid[0]
        acc[...] += dot(hid[0], wd[pl.ds(pl.multiple_of(step * BLK, BLK), BLK), :])

    @pl.when(step == 3)
    def _():
        z, scale = norm_parts(acc[...])
        out[...] = (z * vecs[2:3, :] + vecs[3:4, :]).astype(bf16)
        c = cot[...].astype(f32)
        vgrads[2:3, :] = jnp.sum(c * z, axis=0, keepdims=True)
        vgrads[3:4, :] = jnp.sum(c, axis=0, keepdims=True)
        back = norm_back(c, z, scale, vecs[2:3, :])
        acc[...] = back
        m[...] = back.astype(bf16)

    @pl.when(step == 4)
    def _():
        for copy in copies:
            copy.wait()

    @pl.when(step >= 4)
    def _():
        j = step - 4
        half, at = j // 2, (j % 2) * BLK
        hg = dot_t(m[...], wd[pl.ds(pl.multiple_of(j * BLK, BLK), BLK), :])
        gg = (hg * a[0].astype(f32)).astype(bf16)
        ug = (hg * b[0].astype(f32)).astype(bf16)
        gate_g[0] = gg
        up_g[0] = ug
        acc[...] += dot_t(gg, w[half, :, pl.ds(pl.multiple_of(at, BLK), BLK)]) + dot_t(
            ug, w[half, :, pl.ds(pl.multiple_of(GW + at, HW), BLK)]
        )
        val = lax.dot_general(held[j], m[...], (((0,), (0,)), ((), ())), preferred_element_type=f32)
        c = meta[3]
        parts = val.astype(bf16).reshape(2, 2, 2, 96, D)
        for y in range(2):
            for h in range(2):
                keep[h, 0, y] = jnp.where(c == 0, parts[y, 0, h], parts[y, 1, h])
                send[h, 0, y] = jnp.where(c == 0, parts[y, 1, h], parts[y, 0, h])

    @pl.when(step == 7)
    def _():
        z, scale = norm_parts(res[...])
        c = acc[...]
        vgrads[0:1, :] = jnp.sum(c * z, axis=0, keepdims=True)
        vgrads[1:2, :] = jnp.sum(c, axis=0, keepdims=True)
        back = norm_back(c, z, scale, vecs[0:1, :])
        g_one[...] = back
        back = back.astype(bf16)
        low[...] = back
        ag = dot_t(back[:, :HW], w[0, :, 2 * BLK : GW]) + dot_t(back[:, HW:], w[1, :, 2 * BLK : GW])
        ag = ag.astype(bf16)
        first = meta[0] == 0
        mine[...] = jnp.where(first, ag[:, :HW], ag[:, HW:])
        theirs[...] = jnp.where(first, ag[:, HW:], ag[:, :HW])


def mlp_back_call(meta, res, cot, vecs, hid, a, b, pieces, downs):
    early = lambda i: jnp.minimum(i, 3)
    late = lambda i: jnp.maximum(i - 4, 0)
    part = pl.BlockSpec((1, HALF, BLK), lambda i: (late(i), 0, 0))
    grad = pl.BlockSpec((2, 1, 2, 96, D), lambda i: (0, late(i), 0, 0, 0))
    return pl.pallas_call(
        mlp_back_kernel,
        grid=(8,),
        in_specs=[
            SM, NAT, NAT, whole((8, D)), pl.BlockSpec((1, HALF, BLK), lambda i: (early(i), 0, 0)), part, part,
        ] + [HBM] * 24,
        out_specs=[NAT, grad, grad, part, part, NAT, NAT, HEADS, HEADS, whole((8, D))],
        out_shape=[
            shape((HALF, D), bf16),
            shape((2, 4, 2, 96, D), bf16),
            shape((2, 4, 2, 96, D), bf16),
            shape((4, HALF, BLK), bf16),
            shape((4, HALF, BLK), bf16),
            shape((HALF, D), f32),
            shape((HALF, D), bf16),
            shape((HALF, HW), bf16),
            shape((HALF, HW), bf16),
            shape((8, D), f32),
        ],
        scratch_shapes=[
            pltpu.VMEM((HALF, D), f32),
            pltpu.VMEM((4, HALF, BLK), bf16),
            pltpu.VMEM((HALF, D), bf16),
            pltpu.VMEM((2, D, MW), bf16),
            pltpu.VMEM((FF, D), bf16),
            pltpu.SemaphoreType.DMA((32,)),
            pltpu.SemaphoreType.DMA((16,)),
        ],
        compiler_params=params(62),
        cost_estimate=cost(2 * HALF * D * 5 * FF, 40e6),
        name="mlp_back",
    )(meta, res, cot, vecs, hid, a, b, *pieces, *downs)


def wide_grads_kernel(width, meta, low_t, grads, *rest):
    c = meta[3]
    keep, send = rest[-2:]

    def put(at, val):
        stay, leave = split_core(c, val)
        cols = slice(at, at + val.shape[1])
        for z in range(4):
            for y in range(2):
                keep[0, z, y, :, cols] = stay[2 * z + y]
                send[0, z, y, :, cols] = leave[2 * z + y]

    for i in range(2):
        put(i * BLK, dot(low_t[...], grads[i]))
    if width == GW:
        put(2 * BLK, dot(rest[0][...], rest[1][...]))


def wide_grads_call(meta, low_t, grads, *out_part):
    width = GW if out_part else 2 * BLK
    tall = whole((D, HALF))
    grad = pl.BlockSpec((1, 4, 2, 48, width), lambda i: (i, 0, 0, 0, 0))
    extra = [tall, pl.BlockSpec((HALF, HW), lambda i: (0, i))] if out_part else []
    return pl.pallas_call(
        partial(wide_grads_kernel, width),
        grid=(2,),
        in_specs=[SM, tall, pl.BlockSpec((2, HALF, BLK), lambda i: (i, 0, 0))] + extra,
        out_specs=[grad] * 2,
        out_shape=[shape((2, 4, 2, 48, width), bf16)] * 2,
        compiler_params=params(20),
        cost_estimate=cost(2 * HALF * D * FF, 9e6),
        name="wide_grads",
    )(meta, low_t, grads, *out_part)


def first_grads_kernel(meta, own, other, grads, vgrads, keep, send, rows_t):
    step = pl.program_id(0)

    @pl.when(step == 0)
    def _():
        rows_t[:, :HALF] = own[...].T
        rows_t[:, HALF:] = other[...].T
        row = lax.broadcasted_iota(jnp.int32, (8, D), 0)
        four = jnp.where(row < 4, vgrads[...], 0.0)
        four = jnp.concatenate([four, jnp.zeros((120, D), f32)], axis=0).T
        keep[:, :, 3 * HW :], send[:, :, 3 * HW :] = split_core(meta[3], four)

    for j in range(3):

        @pl.when(step == j)
        def _():
            at = slice(j * HW, (j + 1) * HW)
            keep[:, :, at], send[:, :, at] = split_core(meta[3], dot(rows_t[...], grads[...]))


def first_grads_call(meta, own, other, grads, vgrads):
    grad = whole((8, 48, QW))
    return pl.pallas_call(
        first_grads_kernel,
        grid=(3,),
        in_specs=[SM, NAT, NAT, pl.BlockSpec((2 * HALF, HW), lambda i: (0, i)), whole((8, D))],
        out_specs=[grad] * 2,
        out_shape=[shape((8, 48, QW), bf16)] * 2,
        scratch_shapes=[pltpu.VMEM((D, 2 * HALF), bf16)],
        compiler_params=params(24),
        cost_estimate=cost(2 * 2 * HALF * D * 3 * HW, 8e6),
        name="first_grads",
    )(meta, own, other, grads, vgrads)


def tokens_part_kernel(grads, w, out):
    out[...] = dot_t(grads[...], w[:, : 3 * HW]).astype(out.dtype)


def tokens_part_call(grads, w):
    return pl.pallas_call(
        tokens_part_kernel,
        grid=(2,),
        in_specs=[pl.BlockSpec((HALF // 2, 3 * HW), lambda i: (i + 2, 0)), whole((D, QW))],
        out_specs=pl.BlockSpec((HALF // 2, D), lambda i: (i, 0)),
        out_shape=shape((HALF, D), bf16),
        compiler_params=params(16),
        cost_estimate=cost(2 * HALF * D * 3 * HW, 5e6),
        name="tokens_part",
    )(grads, w)


def tokens_grad_kernel(g_one, theirs, grads, w, out):
    out[...] = g_one[...] + theirs[...].astype(f32) + dot_t(grads[...], w[:, : 3 * HW])


def tokens_grad_call(g_one, theirs, grads, w):
    part = pl.BlockSpec((HALF // 2, D), lambda i: (i, 0))
    return pl.pallas_call(
        tokens_grad_kernel,
        grid=(2,),
        in_specs=[part, part, pl.BlockSpec((HALF // 2, 3 * HW), lambda i: (i, 0)), whole((D, QW))],
        out_specs=part,
        out_shape=shape((HALF, D), f32),
        compiler_params=params(16),
        cost_estimate=cost(2 * HALF * D * 3 * HW, 8e6),
        name="tokens_grad",
    )(g_one, theirs, grads, w)


def pick(a, at, axis):
    return lax.dynamic_index_in_dim(a, at, axis, keepdims=False)


def flip_x(a):
    return lax.ppermute(a, "seq", [(0, 1), (1, 0)])


def flip(bit):
    def go(a):
        n = lax.axis_size("shard")
        return lax.ppermute(a, "shard", [(s, s ^ bit) for s in range(n)])

    return go


flip_c, flip_y, flip_z, flip_far = flip(1), flip(2), flip(4), flip(8)


def turn_z(a, k):
    return lax.ppermute(a, "shard", [(s, (s + 4 * k) % 16) for s in range(16)])


def after(a, *deps):
    return lax.optimization_barrier((a,) + deps)[0]


def slot(*arrays):
    return lax.optimization_barrier(arrays)


def around(mine):
    return [turn_z(mine, k) for k in (1, 2, 3)]


def pieces_of_whole(full):
    cut = full.reshape(full.shape[0], 4, 2, 2, 48, full.shape[2])
    order = jnp.array([0, 3, 2, 1])
    return [
        cut[dh, :, dy, dc][order]
        for dc in range(2)
        for dy in range(2)
        for dh in range(full.shape[0])
    ]


def in_two(pieces):
    return [part for piece in pieces for part in (piece[:2], piece[2:])]


def add(a, b):
    return a.astype(f32) + b.astype(f32)


def turns(sends):
    return [turn_z(send, k + 1) for k, send in enumerate(sends)]


def fold(meta, ins, outs, name):
    def kernel(*refs):
        spot = refs[0][0], refs[0][1], refs[0][2]
        for (_, give), out in zip(outs, refs[1 + len(ins) :]):
            out[...] = give(spot, *refs[1 : 1 + len(ins)]).astype(bf16)

    moved = 2 * sum(a.size for a in ins)
    return pl.pallas_call(
        kernel,
        grid=(1,),
        in_specs=[SM] + [whole(a.shape) for a in ins],
        out_specs=[whole(dims) for dims, _ in outs],
        out_shape=[shape(dims, bf16) for dims, _ in outs],
        compiler_params=params(32),
        cost_estimate=cost(moved, 2 * moved),
        name=name,
    )(meta, *ins)


def cut_core(rows, cols_x, cols_y):
    def along_x(flip):
        def give(spot, keep, got):
            at = spot[0] if flip == 0 else 1 - spot[0]
            return add(keep[at, :, :, :, :cols_x], got[at, :, :, :, :cols_x])

        return give

    def along_y(flip):
        def give(spot, keep, got):
            at = spot[2] if flip == 0 else 1 - spot[2]
            return add(keep[:, :, at, :, cols_x:], got[:, :, at, :, cols_x:])

        return give

    dims_x, dims_y = (4, 2, rows, cols_x), (2, 4, rows, cols_y)
    return [(dims_x, along_x(0)), (dims_x, along_x(1)), (dims_y, along_y(0)), (dims_y, along_y(1))]


def first_two(outs):
    return [(dims, lambda spot, *refs, give=give: give(spot, *refs[:2])) for dims, give in outs]


def cut_plane(rows, cols_x, cols_y, first):
    def along_y(flip):
        def give(spot, *refs):
            at = spot[2] if flip == 0 else 1 - spot[2]
            return add(refs[first][:, at], refs[first + 1][:, at])

        return give

    def along_x(flip):
        def give(spot, *refs):
            at = spot[0] if flip == 0 else 1 - spot[0]
            return add(refs[first + 2][at], refs[first + 3][at])

        return give

    dims_a, dims_b = (4, rows, cols_x), (4, rows, cols_y)
    return [(dims_a, along_y(0)), (dims_a, along_y(1)), (dims_b, along_x(0)), (dims_b, along_x(1))]


def cut_line(rows, cols, first, count):
    def part(k):
        def give(spot, *refs):
            at = lax.rem(spot[1] + k, 4)
            sums = [
                add(refs[first + 2 * i][at], refs[first + 2 * i + 1][at]) for i in range(count)
            ]
            return sums[0] if count == 1 else jnp.concatenate(sums, axis=-1)

        return give

    return [((rows, cols), part(k)) for k in range(4)]


def cut_near(rows, cols, first, count):
    def part(flip):
        def give(spot, *refs):
            odd = lax.rem(spot[1] + flip, 2)
            return jnp.stack(
                [
                    jnp.concatenate(
                        [
                            add(refs[first + 2 * i][odd + 2 * b], refs[first + 2 * i + 1][odd + 2 * b])
                            for i in range(count)
                        ],
                        axis=-1,
                    )
                    for b in range(2)
                ]
            )

        return give

    return [((2, rows, cols), part(0)), ((2, rows, cols), part(1))]


def cut_far(rows, cols, first):
    def part(flip):
        def give(spot, *refs):
            at = lax.rem(spot[1] // 2 + flip, 2)
            return add(refs[first][at], refs[first + 1][at])

        return give

    return [((rows, cols), part(0)), ((rows, cols), part(1))]


def cut_z(rows, cols):
    def part(k):
        def give(spot, keep, got, *_):
            at = lax.rem(spot[1] + k, 4)
            return add(keep[:, at], got[:, at])

        return give

    return [((2, 2, rows, cols), part(k)) for k in range(4)]


def pair(dims, first):
    return [(dims, lambda spot, *refs: add(refs[first][...], refs[first + 1][...]))]


def total_of(rows, cols, first):
    def give(spot, *refs):
        near, *gots = [refs[first + i][...].astype(f32) for i in range(4)]
        return near + gots[0] + gots[1] + gots[2]

    return [((rows, cols), give)]


def halves(mine, other, x):
    return jnp.where(x == 0, jnp.stack([mine, other]), jnp.stack([other, mine])).astype(f32)


def whole_of_split(keep, send):
    both = jnp.stack([keep, send], axis=3)
    return both.transpose(1, 2, 3, 4, 0, 5).reshape(D, -1)


def whole_of_down(keep, send):
    return jnp.stack([keep, send], axis=3).transpose(1, 2, 3, 0, 4, 5).reshape(FF, D)


def local(
    tokens,
    doc_lengths,
    qkv_weight,
    out_weight,
    gate_weight,
    up_weight,
    down_weight,
    norm1_gain,
    norm1_bias,
    norm2_gain,
    norm2_bias,
    cotangent,
):
    n = lax.axis_size("shard")
    fast = n == 16
    x = lax.axis_index("seq").astype(jnp.int32)
    shard = lax.axis_index("shard").astype(jnp.int32)
    zero = jnp.zeros((), jnp.int32)
    z, y, c = (shard // 4, (shard // 2) % 2, shard % 2) if fast else (zero, zero, zero)

    rows = tokens[0]
    cot = cotangent[0]
    lengths = lax.dynamic_slice_in_dim(doc_lengths, shard, 1, 0)[0]
    ends = jnp.cumsum(lengths).astype(jnp.int32)
    hx = x if fast else zero
    meta = jnp.concatenate([jnp.stack([x, z, y, c, hx]), jnp.zeros((3,), jnp.int32), ends])
    spots = jnp.arange(2 * HALF, dtype=jnp.int32)
    spots = jnp.where(spots < HALF, spots + x * HALF, spots - x * HALF)
    passed = spots[:, None] >= ends[None, :]
    place = spots - jnp.sum(jnp.where(passed, lengths[None, :], 0), axis=1)
    frequency = rope_base ** (-jnp.arange(HD // 2, dtype=f32) * 2.0 / HD)
    angles = place.astype(f32)[:, None] * frequency[None, :]
    cosine = jnp.tile(jnp.cos(angles), (1, 4))
    sine = jnp.sin(angles)
    sine = jnp.concatenate([-sine, sine, -sine, sine], axis=1)

    vec_block = jnp.stack([norm1_gain, norm1_bias, norm2_gain, norm2_bias], axis=1)
    vec_block = jnp.pad(vec_block, ((0, 0), (0, 124)))

    def my_heads(w):
        mine = lax.dynamic_slice_in_dim(w.reshape(w.shape[0], 3, 2, HW), x, 1, 2)
        mine = mine.reshape(w.shape[0], 3, 3, 128).transpose(0, 2, 1, 3)
        return mine.reshape(w.shape[0], 3 * HW)

    def half_of(w, at):
        cols = w.shape[1] // 2
        return jnp.where(at == 0, w[:, :cols], w[:, cols:])

    if fast:
        first = jnp.concatenate([my_heads(qkv_weight), vec_block], axis=1)
        wide, wide_o = [
            jnp.concatenate([half_of(w, at) for w in (gate_weight, out_weight, up_weight)], axis=1)
            for at in (x, 1 - x)
        ]
        zq, yd, yo = around(first), flip_y(down_weight), flip_y(wide_o)
        first, zq, wide, cosine, sine, rows_late, yd = slot(
            first, zq, wide, cosine, sine, rows, yd
        )
        wide_late, wide1 = wide, turn_z(wide, 1)
        aq = jnp.stack([first] + zq)
        byq, rows_other = flip_y(aq), flip_x(rows_late)
        wide2, wide3 = turn_z(wide_late, 2), turn_z(wide_late, 3)
        aq, byq, wide, wide1, wide3, down, yd, yo = slot(aq, byq, wide, wide1, wide3, down_weight, yd, yo)
        a0 = jnp.stack([wide, wide1])
        d0 = jnp.stack([down, yd])
        caq, cbyq = flip_c(aq), flip_c(byq)
        caq, cbyq, a0, rows_other, d0 = slot(caq, cbyq, a0, rows_other, d0)
        by0, bx0 = flip_y(a0), flip_x(a0)
        first_pieces = [aq, byq, caq, cbyq]
    else:
        rows_other = flip_x(rows)

        def gathered(w):
            return lax.all_gather(w, "shard", axis=0, tiled=True)

        first = jnp.concatenate([my_heads(gathered(qkv_weight)), gathered(vec_block)], axis=1)
        first_pieces = pieces_of_whole(first[None])

        def in_halves(w):
            return gathered(w).reshape(D, 2, -1).transpose(1, 0, 2)

        wide_all = jnp.concatenate([in_halves(w) for w in (gate_weight, out_weight, up_weight)], axis=2)
        pieces = in_two(pieces_of_whole(wide_all))
        down_all = gathered(down_weight).reshape(4, 2, 2, 192, D)
        down_pieces = [down_all[(4 - k) % 4, :, dc] for dc in range(2) for k in range(4)]

    q, k, kt, v, vt, w1, vecs = qkv_call(meta, rows, rows_other, cosine, sine, first_pieces)
    if fast:
        q, a0, by0, bx0, wide2, d0 = slot(q, a0, by0, bx0, wide2, d0)
        a1 = jnp.stack([wide2, wide3])
        q, a1 = slot(q, a1)
        by1, bx1, d1 = flip_y(a1), flip_x(a1), turn_z(d0, 1)
        ca0, cby0 = flip_c(a0), flip_c(by0)
    att_theirs, at_other, lse_other = attend_call(meta, q, k, vt, 1)
    if fast:
        q, att_theirs, by1, bx1, ca0, cby0, d1, by0, bx0, a1 = slot(
            q, att_theirs, by1, bx1, ca0, cby0, d1, by0, bx0, a1
        )
    att_got = flip_x(att_theirs)
    if fast:
        bxy0, bxy1, d2 = flip_x(by0[1]), flip_y(bx1), turn_z(d1, 1)
        cbx0 = flip_c(bx0)
    att_mine, at_own, lse_own = attend_call(meta, q, k, vt, 0)
    if fast:
        att_mine, att_got, bxy0, bxy1, d2, cbx0, by1, a1, bx1 = slot(
            att_mine, att_got, bxy0, bxy1, d2, cbx0, by1, a1, bx1
        )
        bxy0 = jnp.stack([yo, bxy0])
        cby1 = flip_c(by1)
        cbx1, cbxy0, cbxy1, ca1 = flip_c(bx1), flip_c(bxy0), flip_c(bxy1), flip_c(a1)
        att_mine, cbx1, cby1, cbxy0, cbxy1, ca1, d0, d1, d2 = slot(
            att_mine, cbx1, cby1, cbxy0, cbxy1, ca1, d0, d1, d2
        )
        d3, cd0, cd1, cd2 = turn_z(d2, 1), flip_c(d0), flip_c(d1), flip_c(d2)
        pieces = [a0, a1, bx0, bx1, by0, by1, bxy0, bxy1]
        pieces += [ca0, ca1, cbx0, cbx1, cby0, cby1, cbxy0, cbxy1]
    res, low_t, att_t, hid, part_a, part_b = hidden_call(
        meta, rows, att_mine, att_got, vecs, pieces
    )
    if fast:
        hid, d3, cd0, cd1, cd2 = slot(hid, d3, cd0, cd1, cd2)
        down_pieces = [d0, d1, d2, d3, cd0, cd1, cd2, flip_c(d3)]
    out, keep_d, send_d, gate_g, up_g, g_one, g_low, g_mine, g_theirs, vgrads = mlp_back_call(
        meta, res, cot, vecs, hid, part_a, part_b, pieces, down_pieces
    )

    if fast:
        keep_d, send_d, g_theirs, gate_g = slot(keep_d, send_d, g_theirs, gate_g)
        got_d = flip_c(send_d)
    keep_g, send_g = wide_grads_call(meta, low_t, gate_g, att_t, g_low)
    if fast:
        send_g, g_theirs, got_d, up_g = slot(send_g, g_theirs, got_d, up_g)
        got_g = flip_c(send_g)
    g_other = flip_x(g_theirs)
    keep_u, send_u = wide_grads_call(meta, low_t, up_g)
    if fast:
        send_u, got_g, got_d, g_other = slot(send_u, got_g, got_d, g_other)
        near_ga, sent_ga, near_gb, sent_gb, *part_d = fold(
            meta,
            (keep_g, got_g, keep_d, got_d),
            first_two(cut_core(48, GA, GW - GA))
            + [(dims, lambda spot, *refs, give=give: give(spot, *refs[2:])) for dims, give in cut_z(96, D)],
            "fold",
        )
        sent_ga, sent_gb, g_other, part_d, send_u = slot(sent_ga, sent_gb, g_other, part_d, send_u)
        got_ga, got_gb, got_u = flip_x(sent_ga), flip_y(sent_gb), flip_c(send_u)
        got_d = turn_z(part_d[3], 1)
    back_args = (q, k, kt, v, g_mine, g_other, at_own, at_other, lse_own, lse_other, cosine, sine)
    grads = attend_back_call(meta, *back_args, 0, 2)
    if fast:
        grads, got_ga, got_gb, got_u, got_d = slot(grads, got_ga, got_gb, got_u, got_d)
        near_ga, sent_ga, near_gb, sent_gb, near_ua, sent_ua, near_ub, sent_ub, sent_d = fold(
            meta,
            (keep_u, got_u, near_ga, got_ga, near_gb, got_gb, part_d[2], got_d),
            cut_plane(48, GA, GW - GA, 2) + first_two(cut_core(48, BLK, BLK)) + pair((2, 2, 96, D), 6),
            "fold",
        )
        grads, sent_ua, sent_ub, sent_ga, sent_gb, sent_d = slot(
            grads, sent_ua, sent_ub, sent_ga, sent_gb, sent_d
        )
        got_ua, got_ub, got_d = flip_x(sent_ua), flip_y(sent_ub), turn_z(sent_d, 1)
    grads = attend_back_call(meta, *back_args, 2, 1, grads)
    if fast:
        grads, got_ua, got_ub, got_d, sent_ga, sent_gb = slot(
            grads, got_ua, got_ub, got_d, sent_ga, sent_gb
        )
        near_ua, sent_ua, near_ub, sent_ub, sent_d = fold(
            meta,
            (near_ua, got_ua, near_ub, got_ub, part_d[1], got_d),
            cut_plane(48, BLK, BLK, 0) + pair((2, 2, 96, D), 4),
            "fold",
        )
        grads, sent_ga, sent_gb, sent_ua, sent_ub, sent_d = slot(
            grads, sent_ga, sent_gb, sent_ua, sent_ub, sent_d
        )
        got_ga, got_gb, got_ua, got_ub = flip_y(sent_ga), flip_x(sent_gb), flip_y(sent_ua), flip_x(sent_ub)
        got_d = turn_z(sent_d, 1)
    keep_q, send_q = first_grads_call(meta, rows, rows_other, grads, vgrads)
    if fast:
        keep_q, send_q, got_ga, got_gb, grads = slot(keep_q, send_q, got_ga, got_gb, grads)
        near_g, sent_g = fold(
            meta, (near_ga, got_ga, near_gb, got_gb), cut_near(48, GW, 0, 2), "fold"
        )
        got_g = flip_z(sent_g)
        got_g, got_ua, got_ub, got_d, send_q, grads = slot(
            got_g, got_ua, got_ub, got_d, send_q, grads
        )
        near_u, sent_u, near_g, sent_g, near_d, sent_d = fold(
            meta,
            (near_ua, got_ua, near_ub, got_ub, near_g, got_g, part_d[0], got_d),
            cut_near(48, 2 * BLK, 0, 2)
            + cut_far(48, GW, 4)
            + [
                ((2, 96, D), lambda spot, *refs: add(refs[6][:, spot[2]], refs[7][:, spot[2]])),
                ((2, 96, D), lambda spot, *refs: add(refs[6][:, 1 - spot[2]], refs[7][:, 1 - spot[2]])),
            ],
            "fold",
        )
        sent_u, sent_g, sent_d, send_q, grads = slot(sent_u, sent_g, sent_d, send_q, grads)
        got_q, got_u, got_d, got_g = flip_c(send_q), flip_z(sent_u), flip_y(sent_d), flip_far(sent_g)
    theirs = tokens_part_call(grads, w1)
    if fast:
        got_q, theirs = slot(got_q, theirs)
        cut = (4, 2, 48, QW)
        near_q, sent_q = fold(
            meta,
            (keep_q.reshape(cut), got_q.reshape(cut)),
            [
                ((4, 48, QW), lambda spot, keep, got: add(keep[:, spot[2]], got[:, spot[2]])),
                ((4, 48, QW), lambda spot, keep, got: add(keep[:, 1 - spot[2]], got[:, 1 - spot[2]])),
            ],
            "fold",
        )
        sent_q, theirs = slot(sent_q, theirs)
        got_q, theirs = flip_y(sent_q), flip_x(theirs)
        got_q, got_u, got_d, got_g = slot(got_q, got_u, got_d, got_g)
        near_q, sent_q, near_u, sent_u, total_d, total_g = fold(
            meta,
            (near_q, got_q, near_u, got_u, near_d, got_d, near_g, got_g),
            cut_near(48, QW, 0, 1) + cut_far(48, 2 * BLK, 2) + pair((2, 96, D), 4) + pair((48, GW), 6),
            "fold",
        )
        sent_q, sent_u, total_d, total_g, theirs = slot(sent_q, sent_u, total_d, total_g, theirs)
        got_q, got_u, other_d, other_g = flip_z(sent_q), flip_far(sent_u), flip_x(total_d), flip_x(total_g)
        got_q, got_u = slot(got_q, got_u)
        near_q, sent_q, total_u = fold(
            meta,
            (near_q, got_q, near_u, got_u),
            cut_far(48, QW, 0) + pair((48, 2 * BLK), 2),
            "fold",
        )
        sent_q, total_u = slot(sent_q, total_u)
        got_q, other_u = flip_far(sent_q), flip_x(total_u)
    else:
        theirs = flip_x(theirs)
    grad_in = tokens_grad_call(g_one, theirs, grads, w1)
    if fast:
        got_q, grad_in, other_u, other_d, other_g = slot(got_q, grad_in, other_u, other_d, other_g)
        (total_q,) = fold(meta, (near_q, got_q), pair((48, QW), 0), "fold")
        other_q = flip_x(total_q)

    def joined(part):
        n_rows = part.shape[1]
        part = part.reshape(2, n_rows, 3, 3, 128).transpose(1, 3, 0, 2, 4)
        return part.reshape(n_rows, 3 * D)

    if fast:
        grad_qkv = joined(halves(total_q[:, : 3 * HW], other_q[:, : 3 * HW], x))
        grad_g = halves(total_g, other_g, x)
        grad_gate = jnp.concatenate([grad_g[0, :, : 2 * BLK], grad_g[1, :, : 2 * BLK]], axis=1)
        grad_out = jnp.concatenate([grad_g[0, :, 2 * BLK :], grad_g[1, :, 2 * BLK :]], axis=1)
        grad_up = jnp.concatenate(list(halves(total_u, other_u, x)), axis=1)
        grad_down = add(total_d, other_d).reshape(-1, D)
        vec_own = add(total_q[:, 3 * HW : 3 * HW + 4], other_q[:, 3 * HW : 3 * HW + 4]).T
    else:

        def owned(a):
            part = lax.psum_scatter(a, "shard", scatter_dimension=0, tiled=True)
            return lax.psum(part, "seq").astype(f32)

        grad_g = whole_of_split(keep_g, send_g)
        grad_gate = owned(jnp.concatenate([grad_g[:, : 2 * BLK], grad_g[:, GW : GW + 2 * BLK]], axis=1))
        grad_out = owned(jnp.concatenate([grad_g[:, 2 * BLK : GW], grad_g[:, GW + 2 * BLK :]], axis=1))
        grad_up = owned(whole_of_split(keep_u, send_u))
        grad_down = owned(whole_of_down(keep_d, send_d))
        mine = jnp.stack([keep_q, send_q], axis=1).reshape(D, QW)[:, : 3 * HW]
        none = jnp.zeros_like(mine)
        both = jnp.stack([jnp.where(x == 0, mine, none), jnp.where(x == 0, none, mine)])
        grad_qkv = owned(joined(both))
        vec_grads = lax.psum(vgrads[:4], ("seq", "shard"))
        vec_own = lax.dynamic_slice_in_dim(vec_grads, shard * (D // n), D // n, 1)
    return (
        out[None],
        grad_in[None],
        grad_qkv,
        grad_out,
        grad_gate,
        grad_up,
        grad_down,
        vec_own[0],
        vec_own[1],
        vec_own[2],
        vec_own[3],
    )


def solution(mesh):
    placed = (
        P("shard", "seq", None),
        P(),
        P("shard", None),
        P("shard", None),
        P("shard", None),
        P("shard", None),
        P("shard", None),
        P("shard"),
        P("shard"),
        P("shard"),
        P("shard"),
        P("shard", "seq", None),
    )
    return jax.shard_map(
        local,
        mesh=mesh,
        in_specs=placed,
        out_specs=(
            P("shard", "seq", None),
            P("shard", "seq", None),
            P("shard", None),
            P("shard", None),
            P("shard", None),
            P("shard", None),
            P("shard", None),
            P("shard"),
            P("shard"),
            P("shard"),
            P("shard"),
        ),
        check_vma=False,
    )
```

```python
from functools import partial

import jax
import jax.numpy as jnp
from jax import lax
from jax.experimental import pallas as pl
from jax.experimental.pallas import tpu as pltpu
from jax.sharding import PartitionSpec as P

D = 768
H = 12
HD = 64
FF = 3072
HALF = 512
PAIRS = H // 2
BLK = 768
HW = D // 2
GW = 2 * BLK + HW
MW = GW + 2 * BLK
GA = 1024
QW = 3 * HW + 128
MIB = 1 << 20

rope_base = 1000.0
norm_eps = 1e-05
big_negative = -1e30

bf16 = jnp.bfloat16
f32 = jnp.float32
VM = pl.BlockSpec(memory_space=pltpu.VMEM)
SM = pl.BlockSpec(memory_space=pltpu.SMEM)
HBM = pl.BlockSpec(memory_space=pl.ANY)


def dot(a, b):
    return lax.dot_general(a, b, (((1,), (0,)), ((), ())), preferred_element_type=f32)


def dot_t(a, b):
    return lax.dot_general(a, b, (((1,), (1,)), ((), ())), preferred_element_type=f32)


def params(mib):
    return pltpu.CompilerParams(vmem_limit_bytes=mib * MIB)


def cost(flops, moved, trans=0):
    return pl.CostEstimate(flops=int(flops), bytes_accessed=int(moved), transcendentals=int(trans))


def shape(dims, kind):
    return jax.ShapeDtypeStruct(dims, kind)


def piece_copies(meta, pieces, dst, sems):
    x, z, y, c = meta[4], meta[1], meta[2], meta[3]
    copies = []
    for at in range(8):
        dc, dy, dh = at // 4, (at // 2) % 2, at % 2
        h = jnp.where(x == 0, dh, 1 - dh)
        yy = jnp.where(y == 0, dy, 1 - dy)
        cc = jnp.where(c == 0, dc, 1 - dc)
        for k in range(4):
            zz = lax.rem(z - k + 4, 4)
            row = pl.multiple_of(((zz * 2 + yy) * 2 + cc) * 48, 48)
            copies.append(
                pltpu.make_async_copy(
                    pieces[at * 2 + k // 2].at[k % 2], dst.at[h, pl.ds(row, 48)], sems.at[at * 4 + k]
                )
            )
    return copies


def spin(u, cosine, sine):
    lane = lax.broadcasted_iota(jnp.int32, u.shape, 1)
    swapped = jnp.where(lane % HD < HD // 2, pltpu.roll(u, 96, 1), pltpu.roll(u, 32, 1))
    return u * cosine + swapped * sine


def qkv_kernel(meta, own, other, cosine, sine, *rest):
    pieces = rest[:4]
    q_out, k_out, kt_out, v_out, vt_out, w_out, vecs, w, sems, out_sem = rest[4:]
    step = pl.program_id(0)

    @pl.when(step == 0)
    def _():
        z, y, c = meta[1], meta[2], meta[3]
        copies = []
        for at, piece in enumerate(pieces):
            yy = jnp.where(y == 0, at % 2, 1 - at % 2)
            cc = jnp.where(c == 0, at // 2, 1 - at // 2)
            for k in range(4):
                zz = lax.rem(z - k + 4, 4)
                row = pl.multiple_of(((zz * 2 + yy) * 2 + cc) * 48, 48)
                copies.append(
                    pltpu.make_async_copy(piece.at[k], w.at[pl.ds(row, 48)], sems.at[at * 4 + k])
                )
        for copy in copies:
            copy.start()
        for copy in copies:
            copy.wait()
        pltpu.make_async_copy(w, w_out, out_sem).start()
        vecs[...] = w[:, 3 * HW :].astype(f32).T[:8]

    part = w[:, pl.ds(pl.multiple_of(step * HW, HW), HW)]
    for half, rows in enumerate((own, other)):
        at = slice(half * HALF, (half + 1) * HALF)
        cs, sn = cosine[at, :], sine[at, :]
        qkv = dot(rows[...], part)
        q_out[at, :] = spin(qkv[:, :128], cs, sn).astype(bf16)
        kr = spin(qkv[:, 128:256], cs, sn).astype(bf16)
        vs = qkv[:, 256:].astype(bf16)
        k_out[at, :] = kr
        kt_out[:, at] = kr.T
        v_out[at, :] = vs
        vt_out[:, at] = vs.T

    @pl.when(step == 2)
    def _():
        pltpu.make_async_copy(w, w_out, out_sem).wait()


def qkv_call(meta, own, other, cosine, sine, pieces):
    rows = 2 * HALF
    full = pl.BlockSpec((rows, 128), lambda i: (0, 0))
    x_spec = pl.BlockSpec((HALF, D), lambda i: (0, 0))
    nat = pl.BlockSpec((rows, 128), lambda i: (0, i))
    tr = pl.BlockSpec((128, rows), lambda i: (i, 0))
    return pl.pallas_call(
        qkv_kernel,
        grid=(3,),
        in_specs=[SM, x_spec, x_spec, full, full] + [HBM] * 4,
        out_specs=[nat, nat, tr, nat, tr, HBM, pl.BlockSpec((8, D), lambda i: (0, 0))],
        out_shape=[
            shape((rows, HW), bf16),
            shape((rows, HW), bf16),
            shape((HW, rows), bf16),
            shape((rows, HW), bf16),
            shape((HW, rows), bf16),
            shape((D, QW), bf16),
            shape((8, D), f32),
        ],
        scratch_shapes=[
            pltpu.VMEM((D, QW), bf16),
            pltpu.SemaphoreType.DMA((16,)),
            pltpu.SemaphoreType.DMA,
        ],
        compiler_params=params(62),
        cost_estimate=cost(2 * rows * D * 3 * HW, 14e6),
        name="qkv",
    )(meta, own, other, cosine, sine, *pieces)


def segment_of(meta, pos):
    seg = jnp.zeros(pos.shape, jnp.int32)
    for d in range(8):
        seg = seg + jnp.where(pos >= meta[8 + d], 1, 0)
    return seg


def bias_of(meta, key_base, keys, query_base):
    row = lax.broadcasted_iota(jnp.int32, (keys, 128), 0)
    key_pos = jnp.where(row < HALF, row + key_base[0], row - HALF + key_base[1])
    key_seg = segment_of(meta, key_pos)[:, :1]
    key_pos = key_pos[:, :1]
    query_pos = lax.broadcasted_iota(jnp.int32, (8, HALF), 1) + query_base
    query_seg = segment_of(meta, query_pos)[:1]
    query_pos = query_pos[:1]
    near = jnp.abs(key_pos - query_pos) <= HALF
    return jnp.where((key_seg == query_seg) & near, 0.0, big_negative).astype(f32)


def head_part(block, hh, scale=None):
    lane = lax.broadcasted_iota(jnp.int32, block.shape, 1)
    kept = jnp.where((lane // HD) == hh, block, jnp.zeros_like(block))
    return kept if scale is None else kept * jnp.asarray(scale, block.dtype)


def bases(meta):
    return meta[0] * HALF, HALF - meta[0] * HALF


def attend_kernel(side, meta, q, k, vt, att, att_t, lse, bias):
    @pl.when(pl.program_id(0) == 0)
    def _():
        both = bases(meta)
        bias[...] = bias_of(meta, both, 2 * HALF, both[side])

    parts = []
    for hh in range(2):
        qz = head_part(q[...], hh, HD**-0.5)
        s = dot_t(k[...], qz) + bias[...]
        peak = jnp.max(s, axis=0, keepdims=True)
        e = jnp.exp(s - peak)
        total = jnp.sum(e, axis=0, keepdims=True)
        o = dot(vt[hh * HD : (hh + 1) * HD, :], e.astype(bf16)) * (1.0 / total)
        parts.append(o.astype(bf16))
        lse[0, hh : hh + 1, :] = peak + jnp.log(total)
    both = jnp.concatenate(parts, axis=0)
    att_t[...] = both
    att[...] = both.T


def attend_call(meta, q, k, vt, side):
    return pl.pallas_call(
        partial(attend_kernel, side),
        grid=(3,),
        in_specs=[
            SM,
            pl.BlockSpec((HALF, 128), lambda i: (side, i)),
            pl.BlockSpec((2 * HALF, 128), lambda i: (0, i)),
            pl.BlockSpec((128, 2 * HALF), lambda i: (i, 0)),
        ],
        out_specs=[
            pl.BlockSpec((HALF, 128), lambda i: (0, i)),
            pl.BlockSpec((128, HALF), lambda i: (i, 0)),
            pl.BlockSpec((1, 2, HALF), lambda i: (i, 0, 0)),
        ],
        out_shape=[
            shape((HALF, HW), bf16),
            shape((HW, HALF), bf16),
            shape((3, 2, HALF), f32),
        ],
        scratch_shapes=[pltpu.VMEM((2 * HALF, HALF), f32)],
        compiler_params=params(24),
        cost_estimate=cost(4 * 4 * 6 * 2 * HALF * HALF * HD, 4e6, 6 * 2 * HALF * HALF),
        name="attend",
    )(meta, q, k, vt)


def attend_back_kernel(
    meta, q, k, kt, v, g_own, g_other, at_own, at_other, lse_own, lse_other, cosine, sine, grads, bias,
):
    @pl.when(pl.program_id(0) == 0)
    def _():
        both = bases(meta)
        for side in range(2):
            bias[side] = bias_of(meta, both, 2 * HALF, both[side])

    dk = dv = None
    for side, (g, at, lse) in enumerate(((g_own, at_own, lse_own), (g_other, at_other, lse_other))):
        rows = slice(side * HALF, (side + 1) * HALF)
        prod = g[...].T.astype(f32) * at[...].astype(f32)
        parts = []
        for hh in range(2):
            qz = head_part(q[rows, :], hh, HD**-0.5)
            gz = head_part(g[...], hh)
            delta = jnp.sum(prod[hh * HD : (hh + 1) * HD, :], axis=0, keepdims=True)
            s = dot_t(k[...], qz) + bias[side]
            p = jnp.exp(s - lse[0, hh : hh + 1, :])
            dp = dot_t(v[...], gz)
            ds = (p * (dp - delta)).astype(bf16)
            parts.append(dot(kt[hh * HD : (hh + 1) * HD, :], ds) * HD**-0.5)
            gk, gv = dot(ds, qz), dot(p.astype(bf16), gz)
            dk, dv = (gk, gv) if dk is None else (dk + gk, dv + gv)
        dq = jnp.concatenate(parts, axis=0).T
        grads[rows, :128] = spin(dq, cosine[rows, :], -sine[rows, :]).astype(bf16)
    grads[:, 128:256] = spin(dk, cosine[...], -sine[...]).astype(bf16)
    grads[:, 256:] = dv.astype(bf16)


def attend_back_call(meta, q, k, kt, v, g_own, g_other, at_own, at_other, lse_own, lse_other, cosine, sine, begin, count, done=None):
    nat = pl.BlockSpec((HALF, 128), lambda i: (0, begin + i))
    wide = pl.BlockSpec((2 * HALF, 128), lambda i: (0, begin + i))
    tall = pl.BlockSpec((128, HALF), lambda i: (begin + i, 0))
    row = pl.BlockSpec((1, 2, HALF), lambda i: (begin + i, 0, 0))
    table = pl.BlockSpec((2 * HALF, 128), lambda i: (0, 0))
    extra = () if done is None else (done,)

    def kernel(*refs):
        attend_back_kernel(*refs[:13], *refs[13 + len(extra) :])

    return pl.pallas_call(
        kernel,
        grid=(count,),
        in_specs=[
            SM, wide, wide, pl.BlockSpec((128, 2 * HALF), lambda i: (begin + i, 0)), wide,
            nat, nat, tall, tall, row, row, table, table,
        ] + [HBM] * len(extra),
        out_specs=pl.BlockSpec((2 * HALF, HW), lambda i: (0, begin + i)),
        out_shape=shape((2 * HALF, 3 * HW), bf16),
        input_output_aliases={13: 0} if extra else {},
        scratch_shapes=[pltpu.VMEM((2, 2 * HALF, HALF), f32)],
        compiler_params=params(36),
        cost_estimate=cost(4 * 10 * 2 * count * 4 * HALF * HALF * HD, 12e6, 2 * count * 4 * HALF * HALF),
        name="attend_back",
    )(meta, q, k, kt, v, g_own, g_other, at_own, at_other, lse_own, lse_other, cosine, sine, *extra)


def norm_parts(r):
    centered = r - jnp.mean(r, axis=-1, keepdims=True)
    scale = lax.rsqrt(jnp.mean(centered * centered, axis=-1, keepdims=True) + norm_eps)
    return centered * scale, scale


def norm_back(c, z, scale, gain):
    e = c * gain
    return (e - jnp.mean(e, axis=-1, keepdims=True) - z * jnp.mean(e * z, axis=-1, keepdims=True)) * scale


def split_core(c, val):
    parts = val.astype(bf16).reshape(8, 2, 48, val.shape[1])
    return (
        jnp.where(c == 0, parts[:, 0], parts[:, 1]),
        jnp.where(c == 0, parts[:, 1], parts[:, 0]),
    )


def whole(dims):
    return pl.BlockSpec(dims, lambda i: (0,) * len(dims))


NAT = whole((HALF, D))
PART = pl.BlockSpec((1, HALF, BLK), lambda i: (i % 4, 0, 0))
WIDE = pl.BlockSpec((1, D, BLK), lambda i: ((i % 4) // 2, 0, i % 2))
DOWN = pl.BlockSpec((BLK, D), lambda i: (i % 4, 0))
HEADS = whole((HALF, HW))


def hidden_kernel(meta, rows, mine, theirs, vecs, *rest):
    res, low_t, att_t, hid, a_out, b_out, low, w, sems = rest[16:]
    step = pl.program_id(0)
    copies = piece_copies(meta, rest[:16], w, sems)

    @pl.when(step == 0)
    def _():
        for copy in copies:
            copy.start()
        first = meta[0] == 0
        m, t = mine[...], theirs[...]
        left, right = jnp.where(first, m, t), jnp.where(first, t, m)
        att_t[:HW, :] = left.T
        att_t[HW:, :] = right.T
        att = jnp.concatenate([left, right], axis=1)
        for copy in copies:
            copy.wait()
        branch = jnp.concatenate(
            [dot(att, w[0, :, 2 * BLK : GW]), dot(att, w[1, :, 2 * BLK : GW])], axis=1
        )
        r = rows[...].astype(f32) + branch
        res[...] = r
        z, _ = norm_parts(r)
        n1 = (z * vecs[0:1, :] + vecs[1:2, :]).astype(bf16)
        low[...] = n1
        low_t[...] = n1.T

    half = step // 2
    at = (step % 2) * BLK
    g = dot(low[...], w[half, :, pl.ds(pl.multiple_of(at, BLK), BLK)])
    u = dot(low[...], w[half, :, pl.ds(pl.multiple_of(GW + at, HW), BLK)])
    sig = 1.0 / (1.0 + jnp.exp(-g))
    gs = g * sig
    hid[0] = (gs * u).astype(bf16)
    a_out[0] = (u * (sig + gs * (1.0 - sig))).astype(bf16)
    b_out[0] = gs.astype(bf16)


def hidden_call(meta, rows, mine, theirs, vecs, pieces):
    part = shape((4, HALF, BLK), bf16)
    return pl.pallas_call(
        hidden_kernel,
        grid=(4,),
        in_specs=[SM, NAT, HEADS, HEADS, whole((8, D))] + [HBM] * 16,
        out_specs=[NAT, whole((D, HALF)), whole((D, HALF)), PART, PART, PART],
        out_shape=[
            shape((HALF, D), f32),
            shape((D, HALF), bf16),
            shape((D, HALF), bf16),
            part,
            part,
            part,
        ],
        scratch_shapes=[
            pltpu.VMEM((HALF, D), bf16),
            pltpu.VMEM((2, D, MW), bf16),
            pltpu.SemaphoreType.DMA((32,)),
        ],
        compiler_params=params(62),
        cost_estimate=cost(2 * HALF * D * (2 * FF + D), 30e6, HALF * FF),
        name="hidden",
    )(meta, rows, mine, theirs, vecs, *pieces)


def down_copies(meta, pieces, dst, sems):
    z, y, c = meta[1], meta[2], meta[3]
    copies = []
    for at, piece in enumerate(pieces):
        dc, k = at // 4, at % 4
        zz = lax.rem(z - k + 4, 4)
        cc = jnp.where(c == 0, dc, 1 - dc)
        for dy in range(2):
            yy = jnp.where(y == 0, dy, 1 - dy)
            row = pl.multiple_of(((zz * 2 + yy) * 2 + cc) * 192, 192)
            copies.append(
                pltpu.make_async_copy(piece.at[dy], dst.at[pl.ds(row, 192)], sems.at[at * 2 + dy])
            )
    return copies


def mlp_back_kernel(meta, res, cot, vecs, hid, a, b, *rest):
    pieces, downs = rest[:16], rest[16:24]
    out, keep, send, gate_g, up_g, g_one, low, mine, theirs, vgrads = rest[24:34]
    acc, held, m, w, wd, sems, down_sems = rest[34:]
    step = pl.program_id(0)
    copies = piece_copies(meta, pieces, w, sems)
    down = down_copies(meta, downs, wd, down_sems)

    @pl.when(step == 0)
    def _():
        for copy in down:
            copy.start()
        z, _ = norm_parts(res[...])
        acc[...] = z * vecs[0:1, :] + vecs[1:2, :]
        for copy in down:
            copy.wait()

    @pl.when(step == 1)
    def _():
        for copy in copies:
            copy.start()

    @pl.when(step < 4)
    def _():
        held[step] = hid[0]
        acc[...] += dot(hid[0], wd[pl.ds(pl.multiple_of(step * BLK, BLK), BLK), :])

    @pl.when(step == 3)
    def _():
        z, scale = norm_parts(acc[...])
        out[...] = (z * vecs[2:3, :] + vecs[3:4, :]).astype(bf16)
        c = cot[...].astype(f32)
        vgrads[2:3, :] = jnp.sum(c * z, axis=0, keepdims=True)
        vgrads[3:4, :] = jnp.sum(c, axis=0, keepdims=True)
        back = norm_back(c, z, scale, vecs[2:3, :])
        acc[...] = back
        m[...] = back.astype(bf16)

    @pl.when(step == 4)
    def _():
        for copy in copies:
            copy.wait()

    @pl.when(step >= 4)
    def _():
        j = step - 4
        half, at = j // 2, (j % 2) * BLK
        hg = dot_t(m[...], wd[pl.ds(pl.multiple_of(j * BLK, BLK), BLK), :])
        gg = (hg * a[0].astype(f32)).astype(bf16)
        ug = (hg * b[0].astype(f32)).astype(bf16)
        gate_g[0] = gg
        up_g[0] = ug
        acc[...] += dot_t(gg, w[half, :, pl.ds(pl.multiple_of(at, BLK), BLK)]) + dot_t(
            ug, w[half, :, pl.ds(pl.multiple_of(GW + at, HW), BLK)]
        )
        val = lax.dot_general(held[j], m[...], (((0,), (0,)), ((), ())), preferred_element_type=f32)
        c = meta[3]
        parts = val.astype(bf16).reshape(2, 2, 2, 96, D)
        for y in range(2):
            for h in range(2):
                keep[h, 0, y] = jnp.where(c == 0, parts[y, 0, h], parts[y, 1, h])
                send[h, 0, y] = jnp.where(c == 0, parts[y, 1, h], parts[y, 0, h])

    @pl.when(step == 7)
    def _():
        z, scale = norm_parts(res[...])
        c = acc[...]
        vgrads[0:1, :] = jnp.sum(c * z, axis=0, keepdims=True)
        vgrads[1:2, :] = jnp.sum(c, axis=0, keepdims=True)
        back = norm_back(c, z, scale, vecs[0:1, :])
        g_one[...] = back
        back = back.astype(bf16)
        low[...] = back
        ag = dot_t(back[:, :HW], w[0, :, 2 * BLK : GW]) + dot_t(back[:, HW:], w[1, :, 2 * BLK : GW])
        ag = ag.astype(bf16)
        first = meta[0] == 0
        mine[...] = jnp.where(first, ag[:, :HW], ag[:, HW:])
        theirs[...] = jnp.where(first, ag[:, HW:], ag[:, :HW])


def mlp_back_call(meta, res, cot, vecs, hid, a, b, pieces, downs):
    early = lambda i: jnp.minimum(i, 3)
    late = lambda i: jnp.maximum(i - 4, 0)
    part = pl.BlockSpec((1, HALF, BLK), lambda i: (late(i), 0, 0))
    grad = pl.BlockSpec((2, 1, 2, 96, D), lambda i: (0, late(i), 0, 0, 0))
    return pl.pallas_call(
        mlp_back_kernel,
        grid=(8,),
        in_specs=[
            SM, NAT, NAT, whole((8, D)), pl.BlockSpec((1, HALF, BLK), lambda i: (early(i), 0, 0)), part, part,
        ] + [HBM] * 24,
        out_specs=[NAT, grad, grad, part, part, NAT, NAT, HEADS, HEADS, whole((8, D))],
        out_shape=[
            shape((HALF, D), bf16),
            shape((2, 4, 2, 96, D), bf16),
            shape((2, 4, 2, 96, D), bf16),
            shape((4, HALF, BLK), bf16),
            shape((4, HALF, BLK), bf16),
            shape((HALF, D), f32),
            shape((HALF, D), bf16),
            shape((HALF, HW), bf16),
            shape((HALF, HW), bf16),
            shape((8, D), f32),
        ],
        scratch_shapes=[
            pltpu.VMEM((HALF, D), f32),
            pltpu.VMEM((4, HALF, BLK), bf16),
            pltpu.VMEM((HALF, D), bf16),
            pltpu.VMEM((2, D, MW), bf16),
            pltpu.VMEM((FF, D), bf16),
            pltpu.SemaphoreType.DMA((32,)),
            pltpu.SemaphoreType.DMA((16,)),
        ],
        compiler_params=params(62),
        cost_estimate=cost(2 * HALF * D * 5 * FF, 40e6),
        name="mlp_back",
    )(meta, res, cot, vecs, hid, a, b, *pieces, *downs)


def wide_grads_kernel(width, meta, low_t, grads, *rest):
    c = meta[3]
    keep, send = rest[-2:]

    def put(at, val):
        stay, leave = split_core(c, val)
        cols = slice(at, at + val.shape[1])
        for z in range(4):
            for y in range(2):
                keep[0, z, y, :, cols] = stay[2 * z + y]
                send[0, z, y, :, cols] = leave[2 * z + y]

    for i in range(2):
        put(i * BLK, dot(low_t[...], grads[i]))
    if width == GW:
        put(2 * BLK, dot(rest[0][...], rest[1][...]))


def wide_grads_call(meta, low_t, grads, *out_part):
    width = GW if out_part else 2 * BLK
    tall = whole((D, HALF))
    grad = pl.BlockSpec((1, 4, 2, 48, width), lambda i: (i, 0, 0, 0, 0))
    extra = [tall, pl.BlockSpec((HALF, HW), lambda i: (0, i))] if out_part else []
    return pl.pallas_call(
        partial(wide_grads_kernel, width),
        grid=(2,),
        in_specs=[SM, tall, pl.BlockSpec((2, HALF, BLK), lambda i: (i, 0, 0))] + extra,
        out_specs=[grad] * 2,
        out_shape=[shape((2, 4, 2, 48, width), bf16)] * 2,
        compiler_params=params(20),
        cost_estimate=cost(2 * HALF * D * FF, 9e6),
        name="wide_grads",
    )(meta, low_t, grads, *out_part)


def first_grads_kernel(meta, own, other, grads, vgrads, keep, send, rows_t):
    step = pl.program_id(0)

    @pl.when(step == 0)
    def _():
        rows_t[:, :HALF] = own[...].T
        rows_t[:, HALF:] = other[...].T
        row = lax.broadcasted_iota(jnp.int32, (8, D), 0)
        four = jnp.where(row < 4, vgrads[...], 0.0)
        four = jnp.concatenate([four, jnp.zeros((120, D), f32)], axis=0).T
        keep[:, :, 3 * HW :], send[:, :, 3 * HW :] = split_core(meta[3], four)

    for j in range(3):

        @pl.when(step == j)
        def _():
            at = slice(j * HW, (j + 1) * HW)
            keep[:, :, at], send[:, :, at] = split_core(meta[3], dot(rows_t[...], grads[...]))


def first_grads_call(meta, own, other, grads, vgrads):
    grad = whole((8, 48, QW))
    return pl.pallas_call(
        first_grads_kernel,
        grid=(3,),
        in_specs=[SM, NAT, NAT, pl.BlockSpec((2 * HALF, HW), lambda i: (0, i)), whole((8, D))],
        out_specs=[grad] * 2,
        out_shape=[shape((8, 48, QW), bf16)] * 2,
        scratch_shapes=[pltpu.VMEM((D, 2 * HALF), bf16)],
        compiler_params=params(24),
        cost_estimate=cost(2 * 2 * HALF * D * 3 * HW, 8e6),
        name="first_grads",
    )(meta, own, other, grads, vgrads)


def tokens_part_kernel(grads, w, out):
    out[...] = dot_t(grads[...], w[:, : 3 * HW]).astype(out.dtype)


def tokens_part_call(grads, w):
    return pl.pallas_call(
        tokens_part_kernel,
        grid=(2,),
        in_specs=[pl.BlockSpec((HALF // 2, 3 * HW), lambda i: (i + 2, 0)), whole((D, QW))],
        out_specs=pl.BlockSpec((HALF // 2, D), lambda i: (i, 0)),
        out_shape=shape((HALF, D), bf16),
        compiler_params=params(16),
        cost_estimate=cost(2 * HALF * D * 3 * HW, 5e6),
        name="tokens_part",
    )(grads, w)


def tokens_grad_kernel(g_one, theirs, grads, w, out):
    out[...] = g_one[...] + theirs[...].astype(f32) + dot_t(grads[...], w[:, : 3 * HW])


def tokens_grad_call(g_one, theirs, grads, w):
    part = pl.BlockSpec((HALF // 2, D), lambda i: (i, 0))
    return pl.pallas_call(
        tokens_grad_kernel,
        grid=(2,),
        in_specs=[part, part, pl.BlockSpec((HALF // 2, 3 * HW), lambda i: (i, 0)), whole((D, QW))],
        out_specs=part,
        out_shape=shape((HALF, D), f32),
        compiler_params=params(16),
        cost_estimate=cost(2 * HALF * D * 3 * HW, 8e6),
        name="tokens_grad",
    )(g_one, theirs, grads, w)


def pick(a, at, axis):
    return lax.dynamic_index_in_dim(a, at, axis, keepdims=False)


def flip_x(a):
    return lax.ppermute(a, "seq", [(0, 1), (1, 0)])


def flip(bit):
    def go(a):
        n = lax.axis_size("shard")
        return lax.ppermute(a, "shard", [(s, s ^ bit) for s in range(n)])

    return go


flip_c, flip_y, flip_z, flip_far = flip(1), flip(2), flip(4), flip(8)


def turn_z(a, k):
    return lax.ppermute(a, "shard", [(s, (s + 4 * k) % 16) for s in range(16)])


def after(a, *deps):
    return lax.optimization_barrier((a,) + deps)[0]


def slot(*arrays):
    return lax.optimization_barrier(arrays)


def around(mine):
    return [turn_z(mine, k) for k in (1, 2, 3)]


def pieces_of_whole(full):
    cut = full.reshape(full.shape[0], 4, 2, 2, 48, full.shape[2])
    order = jnp.array([0, 3, 2, 1])
    return [
        cut[dh, :, dy, dc][order]
        for dc in range(2)
        for dy in range(2)
        for dh in range(full.shape[0])
    ]


def in_two(pieces):
    return [part for piece in pieces for part in (piece[:2], piece[2:])]


def add(a, b):
    return a.astype(f32) + b.astype(f32)


def turns(sends):
    return [turn_z(send, k + 1) for k, send in enumerate(sends)]


def fold(meta, ins, outs, name):
    def kernel(*refs):
        spot = refs[0][0], refs[0][1], refs[0][2]
        for (_, give), out in zip(outs, refs[1 + len(ins) :]):
            out[...] = give(spot, *refs[1 : 1 + len(ins)]).astype(bf16)

    moved = 2 * sum(a.size for a in ins)
    return pl.pallas_call(
        kernel,
        grid=(1,),
        in_specs=[SM] + [whole(a.shape) for a in ins],
        out_specs=[whole(dims) for dims, _ in outs],
        out_shape=[shape(dims, bf16) for dims, _ in outs],
        compiler_params=params(32),
        cost_estimate=cost(moved, 2 * moved),
        name=name,
    )(meta, *ins)


def cut_core(rows, cols_x, cols_y):
    def along_x(flip):
        def give(spot, keep, got):
            at = spot[0] if flip == 0 else 1 - spot[0]
            return add(keep[at, :, :, :, :cols_x], got[at, :, :, :, :cols_x])

        return give

    def along_y(flip):
        def give(spot, keep, got):
            at = spot[2] if flip == 0 else 1 - spot[2]
            return add(keep[:, :, at, :, cols_x:], got[:, :, at, :, cols_x:])

        return give

    dims_x, dims_y = (4, 2, rows, cols_x), (2, 4, rows, cols_y)
    return [(dims_x, along_x(0)), (dims_x, along_x(1)), (dims_y, along_y(0)), (dims_y, along_y(1))]


def first_two(outs):
    return [(dims, lambda spot, *refs, give=give: give(spot, *refs[:2])) for dims, give in outs]


def cut_plane(rows, cols_x, cols_y, first):
    def along_y(flip):
        def give(spot, *refs):
            at = spot[2] if flip == 0 else 1 - spot[2]
            return add(refs[first][:, at], refs[first + 1][:, at])

        return give

    def along_x(flip):
        def give(spot, *refs):
            at = spot[0] if flip == 0 else 1 - spot[0]
            return add(refs[first + 2][at], refs[first + 3][at])

        return give

    dims_a, dims_b = (4, rows, cols_x), (4, rows, cols_y)
    return [(dims_a, along_y(0)), (dims_a, along_y(1)), (dims_b, along_x(0)), (dims_b, along_x(1))]


def cut_line(rows, cols, first, count):
    def part(k):
        def give(spot, *refs):
            at = lax.rem(spot[1] + k, 4)
            sums = [
                add(refs[first + 2 * i][at], refs[first + 2 * i + 1][at]) for i in range(count)
            ]
            return sums[0] if count == 1 else jnp.concatenate(sums, axis=-1)

        return give

    return [((rows, cols), part(k)) for k in range(4)]


def cut_near(rows, cols, first, count):
    def part(flip):
        def give(spot, *refs):
            odd = lax.rem(spot[1] + flip, 2)
            return jnp.stack(
                [
                    jnp.concatenate(
                        [
                            add(refs[first + 2 * i][odd + 2 * b], refs[first + 2 * i + 1][odd + 2 * b])
                            for i in range(count)
                        ],
                        axis=-1,
                    )
                    for b in range(2)
                ]
            )

        return give

    return [((2, rows, cols), part(0)), ((2, rows, cols), part(1))]


def cut_far(rows, cols, first):
    def part(flip):
        def give(spot, *refs):
            at = lax.rem(spot[1] // 2 + flip, 2)
            return add(refs[first][at], refs[first + 1][at])

        return give

    return [((rows, cols), part(0)), ((rows, cols), part(1))]


def cut_z(rows, cols):
    def part(k):
        def give(spot, keep, got, *_):
            at = lax.rem(spot[1] + k, 4)
            return add(keep[:, at], got[:, at])

        return give

    return [((2, 2, rows, cols), part(k)) for k in range(4)]


def pair(dims, first):
    return [(dims, lambda spot, *refs: add(refs[first][...], refs[first + 1][...]))]


def total_of(rows, cols, first):
    def give(spot, *refs):
        near, *gots = [refs[first + i][...].astype(f32) for i in range(4)]
        return near + gots[0] + gots[1] + gots[2]

    return [((rows, cols), give)]


def halves(mine, other, x):
    return jnp.where(x == 0, jnp.stack([mine, other]), jnp.stack([other, mine])).astype(f32)


def whole_of_split(keep, send):
    both = jnp.stack([keep, send], axis=3)
    return both.transpose(1, 2, 3, 4, 0, 5).reshape(D, -1)


def whole_of_down(keep, send):
    return jnp.stack([keep, send], axis=3).transpose(1, 2, 3, 0, 4, 5).reshape(FF, D)


def local(
    tokens,
    doc_lengths,
    qkv_weight,
    out_weight,
    gate_weight,
    up_weight,
    down_weight,
    norm1_gain,
    norm1_bias,
    norm2_gain,
    norm2_bias,
    cotangent,
):
    n = lax.axis_size("shard")
    fast = n == 16
    x = lax.axis_index("seq").astype(jnp.int32)
    shard = lax.axis_index("shard").astype(jnp.int32)
    zero = jnp.zeros((), jnp.int32)
    z, y, c = (shard // 4, (shard // 2) % 2, shard % 2) if fast else (zero, zero, zero)

    rows = tokens[0]
    cot = cotangent[0]
    lengths = lax.dynamic_slice_in_dim(doc_lengths, shard, 1, 0)[0]
    ends = jnp.cumsum(lengths).astype(jnp.int32)
    hx = x if fast else zero
    meta = jnp.concatenate([jnp.stack([x, z, y, c, hx]), jnp.zeros((3,), jnp.int32), ends])
    spots = jnp.arange(2 * HALF, dtype=jnp.int32)
    spots = jnp.where(spots < HALF, spots + x * HALF, spots - x * HALF)
    passed = spots[:, None] >= ends[None, :]
    place = spots - jnp.sum(jnp.where(passed, lengths[None, :], 0), axis=1)
    frequency = rope_base ** (-jnp.arange(HD // 2, dtype=f32) * 2.0 / HD)
    angles = place.astype(f32)[:, None] * frequency[None, :]
    cosine = jnp.tile(jnp.cos(angles), (1, 4))
    sine = jnp.sin(angles)
    sine = jnp.concatenate([-sine, sine, -sine, sine], axis=1)

    vec_block = jnp.stack([norm1_gain, norm1_bias, norm2_gain, norm2_bias], axis=1)
    vec_block = jnp.pad(vec_block, ((0, 0), (0, 124)))

    def my_heads(w):
        mine = lax.dynamic_slice_in_dim(w.reshape(w.shape[0], 3, 2, HW), x, 1, 2)
        mine = mine.reshape(w.shape[0], 3, 3, 128).transpose(0, 2, 1, 3)
        return mine.reshape(w.shape[0], 3 * HW)

    def half_of(w, at):
        cols = w.shape[1] // 2
        return jnp.where(at == 0, w[:, :cols], w[:, cols:])

    if fast:
        first = jnp.concatenate([my_heads(qkv_weight), vec_block], axis=1)
        wide, wide_o = [
            jnp.concatenate([half_of(w, at) for w in (gate_weight, out_weight, up_weight)], axis=1)
            for at in (x, 1 - x)
        ]
        zq, yd, yo = around(first), flip_y(down_weight), flip_y(wide_o)
        first, zq, wide, cosine, sine, rows_late, yd = slot(
            first, zq, wide, cosine, sine, rows, yd
        )
        wide_late, wide1 = wide, turn_z(wide, 1)
        aq = jnp.stack([first] + zq)
        byq, rows_other = flip_y(aq), flip_x(rows_late)
        wide2, wide3 = turn_z(wide_late, 2), turn_z(wide_late, 3)
        aq, byq, wide, wide1, wide3, down, yd, yo = slot(aq, byq, wide, wide1, wide3, down_weight, yd, yo)
        a0 = jnp.stack([wide, wide1])
        d0 = jnp.stack([down, yd])
        caq, cbyq = flip_c(aq), flip_c(byq)
        caq, cbyq, a0, rows_other, d0 = slot(caq, cbyq, a0, rows_other, d0)
        by0, bx0, ca0 = flip_y(a0), flip_x(a0), flip_c(a0)
        first_pieces = [aq, byq, caq, cbyq]
    else:
        rows_other = flip_x(rows)

        def gathered(w):
            return lax.all_gather(w, "shard", axis=0, tiled=True)

        first = jnp.concatenate([my_heads(gathered(qkv_weight)), gathered(vec_block)], axis=1)
        first_pieces = pieces_of_whole(first[None])

        def in_halves(w):
            return gathered(w).reshape(D, 2, -1).transpose(1, 0, 2)

        wide_all = jnp.concatenate([in_halves(w) for w in (gate_weight, out_weight, up_weight)], axis=2)
        pieces = in_two(pieces_of_whole(wide_all))
        down_all = gathered(down_weight).reshape(4, 2, 2, 192, D)
        down_pieces = [down_all[(4 - k) % 4, :, dc] for dc in range(2) for k in range(4)]

    q, k, kt, v, vt, w1, vecs = qkv_call(meta, rows, rows_other, cosine, sine, first_pieces)
    if fast:
        q, by0, bx0, wide2, d0, ca0 = slot(q, by0, bx0, wide2, d0, ca0)
        a1 = jnp.stack([wide2, wide3])
        q, a1 = slot(q, a1)
        by1, bx1, d1 = flip_y(a1), flip_x(a1), turn_z(d0, 1)
        cby0, cbx0 = flip_c(by0), flip_c(bx0)
    att_theirs, at_other, lse_other = attend_call(meta, q, k, vt, 1)
    if fast:
        q, att_theirs, by1, bx1, cby0, cbx0, d1, by0, a1 = slot(
            q, att_theirs, by1, bx1, cby0, cbx0, d1, by0, a1
        )
    att_got = flip_x(att_theirs)
    if fast:
        bxy0, bxy1, d2 = flip_x(by0[1]), flip_y(bx1), turn_z(d1, 1)
        ca1 = flip_c(a1)
    att_mine, at_own, lse_own = attend_call(meta, q, k, vt, 0)
    if fast:
        att_mine, att_got, bxy0, bxy1, d2, ca1, by1, bx1 = slot(
            att_mine, att_got, bxy0, bxy1, d2, ca1, by1, bx1
        )
        bxy0 = jnp.stack([yo, bxy0])
        cby1 = flip_c(by1)
        cbx1, cbxy0, cbxy1 = flip_c(bx1), flip_c(bxy0), flip_c(bxy1)
        att_mine, cbx1, cby1, cbxy0, cbxy1, d0, d1, d2 = slot(
            att_mine, cbx1, cby1, cbxy0, cbxy1, d0, d1, d2
        )
        d3, cd0, cd1, cd2 = turn_z(d2, 1), flip_c(d0), flip_c(d1), flip_c(d2)
        pieces = [a0, a1, bx0, bx1, by0, by1, bxy0, bxy1]
        pieces += [ca0, ca1, cbx0, cbx1, cby0, cby1, cbxy0, cbxy1]
    res, low_t, att_t, hid, part_a, part_b = hidden_call(
        meta, rows, att_mine, att_got, vecs, pieces
    )
    if fast:
        hid, d3, cd0, cd1, cd2 = slot(hid, d3, cd0, cd1, cd2)
        down_pieces = [d0, d1, d2, d3, cd0, cd1, cd2, flip_c(d3)]
    out, keep_d, send_d, gate_g, up_g, g_one, g_low, g_mine, g_theirs, vgrads = mlp_back_call(
        meta, res, cot, vecs, hid, part_a, part_b, pieces, down_pieces
    )

    if fast:
        keep_d, send_d, g_theirs, gate_g = slot(keep_d, send_d, g_theirs, gate_g)
        got_d = flip_c(send_d)
    keep_g, send_g = wide_grads_call(meta, low_t, gate_g, att_t, g_low)
    if fast:
        send_g, g_theirs, got_d, up_g = slot(send_g, g_theirs, got_d, up_g)
        got_g = flip_c(send_g)
    g_other = flip_x(g_theirs)
    keep_u, send_u = wide_grads_call(meta, low_t, up_g)
    if fast:
        send_u, got_g, got_d, g_other = slot(send_u, got_g, got_d, g_other)
        near_ga, sent_ga, near_gb, sent_gb, *part_d = fold(
            meta,
            (keep_g, got_g, keep_d, got_d),
            first_two(cut_core(48, GA, GW - GA))
            + [(dims, lambda spot, *refs, give=give: give(spot, *refs[2:])) for dims, give in cut_z(96, D)],
            "fold",
        )
        sent_ga, sent_gb, g_other, part_d, send_u = slot(sent_ga, sent_gb, g_other, part_d, send_u)
        got_ga, got_gb, got_u = flip_x(sent_ga), flip_y(sent_gb), flip_c(send_u)
        got_d = turn_z(part_d[3], 1)
    back_args = (q, k, kt, v, g_mine, g_other, at_own, at_other, lse_own, lse_other, cosine, sine)
    grads = attend_back_call(meta, *back_args, 0, 2)
    if fast:
        grads, got_ga, got_gb, got_u, got_d = slot(grads, got_ga, got_gb, got_u, got_d)
        near_ga, sent_ga, near_gb, sent_gb, near_ua, sent_ua, near_ub, sent_ub, sent_d = fold(
            meta,
            (keep_u, got_u, near_ga, got_ga, near_gb, got_gb, part_d[2], got_d),
            cut_plane(48, GA, GW - GA, 2) + first_two(cut_core(48, BLK, BLK)) + pair((2, 2, 96, D), 6),
            "fold",
        )
        grads, sent_ua, sent_ub, sent_ga, sent_gb, sent_d = slot(
            grads, sent_ua, sent_ub, sent_ga, sent_gb, sent_d
        )
        got_ua, got_ub, got_d = flip_x(sent_ua), flip_y(sent_ub), turn_z(sent_d, 1)
    grads = attend_back_call(meta, *back_args, 2, 1, grads)
    if fast:
        grads, got_ua, got_ub, got_d, sent_ga, sent_gb = slot(
            grads, got_ua, got_ub, got_d, sent_ga, sent_gb
        )
        near_ua, sent_ua, near_ub, sent_ub, sent_d = fold(
            meta,
            (near_ua, got_ua, near_ub, got_ub, part_d[1], got_d),
            cut_plane(48, BLK, BLK, 0) + pair((2, 2, 96, D), 4),
            "fold",
        )
        grads, sent_ga, sent_gb, sent_ua, sent_ub, sent_d = slot(
            grads, sent_ga, sent_gb, sent_ua, sent_ub, sent_d
        )
        got_ga, got_gb, got_ua, got_ub = flip_y(sent_ga), flip_x(sent_gb), flip_y(sent_ua), flip_x(sent_ub)
        got_d = turn_z(sent_d, 1)
    keep_q, send_q = first_grads_call(meta, rows, rows_other, grads, vgrads)
    if fast:
        keep_q, send_q, got_ga, got_gb, got_d, grads = slot(
            keep_q, send_q, got_ga, got_gb, got_d, grads
        )
        near_g, sent_g = fold(
            meta, (near_ga, got_ga, near_gb, got_gb), cut_near(48, GW, 0, 2), "fold"
        )
        sent_g, send_q, grads = slot(sent_g, send_q, grads)
        got_g, got_q = flip_z(sent_g), flip_c(send_q)
    theirs = tokens_part_call(grads, w1)
    if fast:
        got_g, got_ua, got_ub, got_q, theirs = slot(got_g, got_ua, got_ub, got_q, theirs)
        cut = (4, 2, 48, QW)
        near_u, sent_u, near_g, sent_g, near_d, sent_d, near_q, sent_q = fold(
            meta,
            (
                near_ua, got_ua, near_ub, got_ub, near_g, got_g, part_d[0], got_d,
                keep_q.reshape(cut), got_q.reshape(cut),
            ),
            cut_near(48, 2 * BLK, 0, 2)
            + cut_far(48, GW, 4)
            + [
                ((2, 96, D), lambda spot, *refs: add(refs[6][:, spot[2]], refs[7][:, spot[2]])),
                ((2, 96, D), lambda spot, *refs: add(refs[6][:, 1 - spot[2]], refs[7][:, 1 - spot[2]])),
                ((4, 48, QW), lambda spot, *refs: add(refs[8][:, spot[2]], refs[9][:, spot[2]])),
                ((4, 48, QW), lambda spot, *refs: add(refs[8][:, 1 - spot[2]], refs[9][:, 1 - spot[2]])),
            ],
            "fold",
        )
        sent_u, sent_g, sent_d, sent_q, theirs = slot(sent_u, sent_g, sent_d, sent_q, theirs)
        got_q, theirs, got_u = flip_y(sent_q), flip_x(theirs), flip_z(sent_u)
        got_d, got_g = flip_y(sent_d), flip_far(sent_g)
        got_q, got_u, got_d, got_g = slot(got_q, got_u, got_d, got_g)
        near_q, sent_q, near_u, sent_u, total_d, total_g = fold(
            meta,
            (near_q, got_q, near_u, got_u, near_d, got_d, near_g, got_g),
            cut_near(48, QW, 0, 1) + cut_far(48, 2 * BLK, 2) + pair((2, 96, D), 4) + pair((48, GW), 6),
            "fold",
        )
        sent_q, sent_u, total_d, total_g, theirs = slot(sent_q, sent_u, total_d, total_g, theirs)
        got_q, got_u, other_d, other_g = flip_z(sent_q), flip_far(sent_u), flip_x(total_d), flip_x(total_g)
        got_q, got_u = slot(got_q, got_u)
        near_q, sent_q, total_u = fold(
            meta,
            (near_q, got_q, near_u, got_u),
            cut_far(48, QW, 0) + pair((48, 2 * BLK), 2),
            "fold",
        )
        sent_q, total_u = slot(sent_q, total_u)
        got_q, other_u = flip_far(sent_q), flip_x(total_u)
    else:
        theirs = flip_x(theirs)
    grad_in = tokens_grad_call(g_one, theirs, grads, w1)
    if fast:
        got_q, grad_in, other_u, other_d, other_g = slot(got_q, grad_in, other_u, other_d, other_g)
        (total_q,) = fold(meta, (near_q, got_q), pair((48, QW), 0), "fold")
        other_q = flip_x(total_q)

    def joined(part):
        n_rows = part.shape[1]
        part = part.reshape(2, n_rows, 3, 3, 128).transpose(1, 3, 0, 2, 4)
        return part.reshape(n_rows, 3 * D)

    if fast:
        grad_qkv = joined(halves(total_q[:, : 3 * HW], other_q[:, : 3 * HW], x))
        grad_g = halves(total_g, other_g, x)
        grad_gate = jnp.concatenate([grad_g[0, :, : 2 * BLK], grad_g[1, :, : 2 * BLK]], axis=1)
        grad_out = jnp.concatenate([grad_g[0, :, 2 * BLK :], grad_g[1, :, 2 * BLK :]], axis=1)
        grad_up = jnp.concatenate(list(halves(total_u, other_u, x)), axis=1)
        grad_down = add(total_d, other_d).reshape(-1, D)
        vec_own = add(total_q[:, 3 * HW : 3 * HW + 4], other_q[:, 3 * HW : 3 * HW + 4]).T
    else:

        def owned(a):
            part = lax.psum_scatter(a, "shard", scatter_dimension=0, tiled=True)
            return lax.psum(part, "seq").astype(f32)

        grad_g = whole_of_split(keep_g, send_g)
        grad_gate = owned(jnp.concatenate([grad_g[:, : 2 * BLK], grad_g[:, GW : GW + 2 * BLK]], axis=1))
        grad_out = owned(jnp.concatenate([grad_g[:, 2 * BLK : GW], grad_g[:, GW + 2 * BLK :]], axis=1))
        grad_up = owned(whole_of_split(keep_u, send_u))
        grad_down = owned(whole_of_down(keep_d, send_d))
        mine = jnp.stack([keep_q, send_q], axis=1).reshape(D, QW)[:, : 3 * HW]
        none = jnp.zeros_like(mine)
        both = jnp.stack([jnp.where(x == 0, mine, none), jnp.where(x == 0, none, mine)])
        grad_qkv = owned(joined(both))
        vec_grads = lax.psum(vgrads[:4], ("seq", "shard"))
        vec_own = lax.dynamic_slice_in_dim(vec_grads, shard * (D // n), D // n, 1)
    return (
        out[None],
        grad_in[None],
        grad_qkv,
        grad_out,
        grad_gate,
        grad_up,
        grad_down,
        vec_own[0],
        vec_own[1],
        vec_own[2],
        vec_own[3],
    )


def solution(mesh):
    placed = (
        P("shard", "seq", None),
        P(),
        P("shard", None),
        P("shard", None),
        P("shard", None),
        P("shard", None),
        P("shard", None),
        P("shard"),
        P("shard"),
        P("shard"),
        P("shard"),
        P("shard", "seq", None),
    )
    return jax.shard_map(
        local,
        mesh=mesh,
        in_specs=placed,
        out_specs=(
            P("shard", "seq", None),
            P("shard", "seq", None),
            P("shard", None),
            P("shard", None),
            P("shard", None),
            P("shard", None),
            P("shard", None),
            P("shard"),
            P("shard"),
            P("shard"),
            P("shard"),
        ),
        check_vma=False,
    )
```

```python
from functools import partial

import jax
import jax.numpy as jnp
from jax import lax
from jax.experimental import pallas as pl
from jax.experimental.pallas import tpu as pltpu
from jax.sharding import PartitionSpec as P

D = 768
H = 12
HD = 64
FF = 3072
HALF = 512
PAIRS = H // 2
BLK = 768
HW = D // 2
GW = 2 * BLK + HW
MW = GW + 2 * BLK
GA = 1024
QW = 3 * HW + 128
MIB = 1 << 20

rope_base = 1000.0
norm_eps = 1e-05
big_negative = -1e30

bf16 = jnp.bfloat16
f32 = jnp.float32
VM = pl.BlockSpec(memory_space=pltpu.VMEM)
SM = pl.BlockSpec(memory_space=pltpu.SMEM)
HBM = pl.BlockSpec(memory_space=pl.ANY)


def dot(a, b):
    return lax.dot_general(a, b, (((1,), (0,)), ((), ())), preferred_element_type=f32)


def dot_t(a, b):
    return lax.dot_general(a, b, (((1,), (1,)), ((), ())), preferred_element_type=f32)


def params(mib):
    return pltpu.CompilerParams(vmem_limit_bytes=mib * MIB)


def cost(flops, moved, trans=0):
    return pl.CostEstimate(flops=int(flops), bytes_accessed=int(moved), transcendentals=int(trans))


def shape(dims, kind):
    return jax.ShapeDtypeStruct(dims, kind)


def piece_copies(meta, pieces, dst, sems):
    x, z, y, c = meta[4], meta[1], meta[2], meta[3]
    copies = []
    for at in range(8):
        dc, dy, dh = at // 4, (at // 2) % 2, at % 2
        h = jnp.where(x == 0, dh, 1 - dh)
        yy = jnp.where(y == 0, dy, 1 - dy)
        cc = jnp.where(c == 0, dc, 1 - dc)
        for k in range(4):
            zz = lax.rem(z - k + 4, 4)
            row = pl.multiple_of(((zz * 2 + yy) * 2 + cc) * 48, 48)
            copies.append(
                pltpu.make_async_copy(
                    pieces[at * 2 + k // 2].at[k % 2], dst.at[h, pl.ds(row, 48)], sems.at[at * 4 + k]
                )
            )
    return copies


def spin(u, cosine, sine):
    lane = lax.broadcasted_iota(jnp.int32, u.shape, 1)
    swapped = jnp.where(lane % HD < HD // 2, pltpu.roll(u, 96, 1), pltpu.roll(u, 32, 1))
    return u * cosine + swapped * sine


def qkv_kernel(meta, own, other, cosine, sine, *rest):
    pieces = rest[:4]
    q_out, k_out, kt_out, v_out, vt_out, w_out, vecs, w, sems, out_sem = rest[4:]
    step = pl.program_id(0)

    @pl.when(step == 0)
    def _():
        z, y, c = meta[1], meta[2], meta[3]
        copies = []
        for at, piece in enumerate(pieces):
            yy = jnp.where(y == 0, at % 2, 1 - at % 2)
            cc = jnp.where(c == 0, at // 2, 1 - at // 2)
            for k in range(4):
                zz = lax.rem(z - k + 4, 4)
                row = pl.multiple_of(((zz * 2 + yy) * 2 + cc) * 48, 48)
                copies.append(
                    pltpu.make_async_copy(piece.at[k], w.at[pl.ds(row, 48)], sems.at[at * 4 + k])
                )
        for copy in copies:
            copy.start()
        for copy in copies:
            copy.wait()
        pltpu.make_async_copy(w, w_out, out_sem).start()
        vecs[...] = w[:, 3 * HW :].astype(f32).T[:8]

    part = w[:, pl.ds(pl.multiple_of(step * HW, HW), HW)]
    for half, rows in enumerate((own, other)):
        at = slice(half * HALF, (half + 1) * HALF)
        cs, sn = cosine[at, :], sine[at, :]
        qkv = dot(rows[...], part)
        q_out[at, :] = spin(qkv[:, :128], cs, sn).astype(bf16)
        kr = spin(qkv[:, 128:256], cs, sn).astype(bf16)
        vs = qkv[:, 256:].astype(bf16)
        k_out[at, :] = kr
        kt_out[:, at] = kr.T
        v_out[at, :] = vs
        vt_out[:, at] = vs.T

    @pl.when(step == 2)
    def _():
        pltpu.make_async_copy(w, w_out, out_sem).wait()


def qkv_call(meta, own, other, cosine, sine, pieces):
    rows = 2 * HALF
    full = pl.BlockSpec((rows, 128), lambda i: (0, 0))
    x_spec = pl.BlockSpec((HALF, D), lambda i: (0, 0))
    nat = pl.BlockSpec((rows, 128), lambda i: (0, i))
    tr = pl.BlockSpec((128, rows), lambda i: (i, 0))
    return pl.pallas_call(
        qkv_kernel,
        grid=(3,),
        in_specs=[SM, x_spec, x_spec, full, full] + [HBM] * 4,
        out_specs=[nat, nat, tr, nat, tr, HBM, pl.BlockSpec((8, D), lambda i: (0, 0))],
        out_shape=[
            shape((rows, HW), bf16),
            shape((rows, HW), bf16),
            shape((HW, rows), bf16),
            shape((rows, HW), bf16),
            shape((HW, rows), bf16),
            shape((D, QW), bf16),
            shape((8, D), f32),
        ],
        scratch_shapes=[
            pltpu.VMEM((D, QW), bf16),
            pltpu.SemaphoreType.DMA((16,)),
            pltpu.SemaphoreType.DMA,
        ],
        compiler_params=params(62),
        cost_estimate=cost(2 * rows * D * 3 * HW, 14e6),
        name="qkv",
    )(meta, own, other, cosine, sine, *pieces)


def segment_of(meta, pos):
    seg = jnp.zeros(pos.shape, jnp.int32)
    for d in range(8):
        seg = seg + jnp.where(pos >= meta[8 + d], 1, 0)
    return seg


def bias_of(meta, key_base, keys, query_base):
    row = lax.broadcasted_iota(jnp.int32, (keys, 128), 0)
    key_pos = jnp.where(row < HALF, row + key_base[0], row - HALF + key_base[1])
    key_seg = segment_of(meta, key_pos)[:, :1]
    key_pos = key_pos[:, :1]
    query_pos = lax.broadcasted_iota(jnp.int32, (8, HALF), 1) + query_base
    query_seg = segment_of(meta, query_pos)[:1]
    query_pos = query_pos[:1]
    near = jnp.abs(key_pos - query_pos) <= HALF
    return jnp.where((key_seg == query_seg) & near, 0.0, big_negative).astype(f32)


def head_part(block, hh, scale=None):
    lane = lax.broadcasted_iota(jnp.int32, block.shape, 1)
    kept = jnp.where((lane // HD) == hh, block, jnp.zeros_like(block))
    return kept if scale is None else kept * jnp.asarray(scale, block.dtype)


def bases(meta):
    return meta[0] * HALF, HALF - meta[0] * HALF


def attend_kernel(side, meta, q, k, vt, att, att_t, lse, bias):
    @pl.when(pl.program_id(0) == 0)
    def _():
        both = bases(meta)
        bias[...] = bias_of(meta, both, 2 * HALF, both[side])

    parts = []
    for hh in range(2):
        qz = head_part(q[...], hh, HD**-0.5)
        s = dot_t(k[...], qz) + bias[...]
        peak = jnp.max(s, axis=0, keepdims=True)
        e = jnp.exp(s - peak)
        total = jnp.sum(e, axis=0, keepdims=True)
        o = dot(vt[hh * HD : (hh + 1) * HD, :], e.astype(bf16)) * (1.0 / total)
        parts.append(o.astype(bf16))
        lse[0, hh : hh + 1, :] = peak + jnp.log(total)
    both = jnp.concatenate(parts, axis=0)
    att_t[...] = both
    att[...] = both.T


def attend_call(meta, q, k, vt, side):
    return pl.pallas_call(
        partial(attend_kernel, side),
        grid=(3,),
        in_specs=[
            SM,
            pl.BlockSpec((HALF, 128), lambda i: (side, i)),
            pl.BlockSpec((2 * HALF, 128), lambda i: (0, i)),
            pl.BlockSpec((128, 2 * HALF), lambda i: (i, 0)),
        ],
        out_specs=[
            pl.BlockSpec((HALF, 128), lambda i: (0, i)),
            pl.BlockSpec((128, HALF), lambda i: (i, 0)),
            pl.BlockSpec((1, 2, HALF), lambda i: (i, 0, 0)),
        ],
        out_shape=[
            shape((HALF, HW), bf16),
            shape((HW, HALF), bf16),
            shape((3, 2, HALF), f32),
        ],
        scratch_shapes=[pltpu.VMEM((2 * HALF, HALF), f32)],
        compiler_params=params(24),
        cost_estimate=cost(4 * 4 * 6 * 2 * HALF * HALF * HD, 4e6, 6 * 2 * HALF * HALF),
        name="attend",
    )(meta, q, k, vt)


def attend_back_kernel(
    meta, q, k, kt, v, g_own, g_other, at_own, at_other, lse_own, lse_other, cosine, sine, grads, bias,
):
    @pl.when(pl.program_id(0) == 0)
    def _():
        both = bases(meta)
        for side in range(2):
            bias[side] = bias_of(meta, both, 2 * HALF, both[side])

    dk = dv = None
    for side, (g, at, lse) in enumerate(((g_own, at_own, lse_own), (g_other, at_other, lse_other))):
        rows = slice(side * HALF, (side + 1) * HALF)
        prod = g[...].T.astype(f32) * at[...].astype(f32)
        parts = []
        for hh in range(2):
            qz = head_part(q[rows, :], hh, HD**-0.5)
            gz = head_part(g[...], hh)
            delta = jnp.sum(prod[hh * HD : (hh + 1) * HD, :], axis=0, keepdims=True)
            s = dot_t(k[...], qz) + bias[side]
            p = jnp.exp(s - lse[0, hh : hh + 1, :])
            dp = dot_t(v[...], gz)
            ds = (p * (dp - delta)).astype(bf16)
            parts.append(dot(kt[hh * HD : (hh + 1) * HD, :], ds) * HD**-0.5)
            gk, gv = dot(ds, qz), dot(p.astype(bf16), gz)
            dk, dv = (gk, gv) if dk is None else (dk + gk, dv + gv)
        dq = jnp.concatenate(parts, axis=0).T
        grads[rows, :128] = spin(dq, cosine[rows, :], -sine[rows, :]).astype(bf16)
    grads[:, 128:256] = spin(dk, cosine[...], -sine[...]).astype(bf16)
    grads[:, 256:] = dv.astype(bf16)


def attend_back_call(meta, q, k, kt, v, g_own, g_other, at_own, at_other, lse_own, lse_other, cosine, sine, begin, count, done=None):
    nat = pl.BlockSpec((HALF, 128), lambda i: (0, begin + i))
    wide = pl.BlockSpec((2 * HALF, 128), lambda i: (0, begin + i))
    tall = pl.BlockSpec((128, HALF), lambda i: (begin + i, 0))
    row = pl.BlockSpec((1, 2, HALF), lambda i: (begin + i, 0, 0))
    table = pl.BlockSpec((2 * HALF, 128), lambda i: (0, 0))
    extra = () if done is None else (done,)

    def kernel(*refs):
        attend_back_kernel(*refs[:13], *refs[13 + len(extra) :])

    return pl.pallas_call(
        kernel,
        grid=(count,),
        in_specs=[
            SM, wide, wide, pl.BlockSpec((128, 2 * HALF), lambda i: (begin + i, 0)), wide,
            nat, nat, tall, tall, row, row, table, table,
        ] + [HBM] * len(extra),
        out_specs=pl.BlockSpec((2 * HALF, HW), lambda i: (0, begin + i)),
        out_shape=shape((2 * HALF, 3 * HW), bf16),
        input_output_aliases={13: 0} if extra else {},
        scratch_shapes=[pltpu.VMEM((2, 2 * HALF, HALF), f32)],
        compiler_params=params(36),
        cost_estimate=cost(4 * 10 * 2 * count * 4 * HALF * HALF * HD, 12e6, 2 * count * 4 * HALF * HALF),
        name="attend_back",
    )(meta, q, k, kt, v, g_own, g_other, at_own, at_other, lse_own, lse_other, cosine, sine, *extra)


def norm_parts(r):
    centered = r - jnp.mean(r, axis=-1, keepdims=True)
    scale = lax.rsqrt(jnp.mean(centered * centered, axis=-1, keepdims=True) + norm_eps)
    return centered * scale, scale


def norm_back(c, z, scale, gain):
    e = c * gain
    return (e - jnp.mean(e, axis=-1, keepdims=True) - z * jnp.mean(e * z, axis=-1, keepdims=True)) * scale


def split_core(c, val):
    parts = val.astype(bf16).reshape(8, 2, 48, val.shape[1])
    return (
        jnp.where(c == 0, parts[:, 0], parts[:, 1]),
        jnp.where(c == 0, parts[:, 1], parts[:, 0]),
    )


def whole(dims):
    return pl.BlockSpec(dims, lambda i: (0,) * len(dims))


NAT = whole((HALF, D))
PART = pl.BlockSpec((1, HALF, BLK), lambda i: (i % 4, 0, 0))
WIDE = pl.BlockSpec((1, D, BLK), lambda i: ((i % 4) // 2, 0, i % 2))
DOWN = pl.BlockSpec((BLK, D), lambda i: (i % 4, 0))
HEADS = whole((HALF, HW))


def hidden_kernel(meta, rows, mine, theirs, vecs, *rest):
    res, low_t, att_t, hid, a_out, b_out, low, w, sems = rest[16:]
    step = pl.program_id(0)
    copies = piece_copies(meta, rest[:16], w, sems)

    @pl.when(step == 0)
    def _():
        for copy in copies:
            copy.start()
        first = meta[0] == 0
        m, t = mine[...], theirs[...]
        left, right = jnp.where(first, m, t), jnp.where(first, t, m)
        att_t[:HW, :] = left.T
        att_t[HW:, :] = right.T
        att = jnp.concatenate([left, right], axis=1)
        for copy in copies:
            copy.wait()
        branch = jnp.concatenate(
            [dot(att, w[0, :, 2 * BLK : GW]), dot(att, w[1, :, 2 * BLK : GW])], axis=1
        )
        r = rows[...].astype(f32) + branch
        res[...] = r
        z, _ = norm_parts(r)
        n1 = (z * vecs[0:1, :] + vecs[1:2, :]).astype(bf16)
        low[...] = n1
        low_t[...] = n1.T

    half = step // 2
    at = (step % 2) * BLK
    g = dot(low[...], w[half, :, pl.ds(pl.multiple_of(at, BLK), BLK)])
    u = dot(low[...], w[half, :, pl.ds(pl.multiple_of(GW + at, HW), BLK)])
    sig = 1.0 / (1.0 + jnp.exp(-g))
    gs = g * sig
    hid[0] = (gs * u).astype(bf16)
    a_out[0] = (u * (sig + gs * (1.0 - sig))).astype(bf16)
    b_out[0] = gs.astype(bf16)


def hidden_call(meta, rows, mine, theirs, vecs, pieces):
    part = shape((4, HALF, BLK), bf16)
    return pl.pallas_call(
        hidden_kernel,
        grid=(4,),
        in_specs=[SM, NAT, HEADS, HEADS, whole((8, D))] + [HBM] * 16,
        out_specs=[NAT, whole((D, HALF)), whole((D, HALF)), PART, PART, PART],
        out_shape=[
            shape((HALF, D), f32),
            shape((D, HALF), bf16),
            shape((D, HALF), bf16),
            part,
            part,
            part,
        ],
        scratch_shapes=[
            pltpu.VMEM((HALF, D), bf16),
            pltpu.VMEM((2, D, MW), bf16),
            pltpu.SemaphoreType.DMA((32,)),
        ],
        compiler_params=params(62),
        cost_estimate=cost(2 * HALF * D * (2 * FF + D), 30e6, HALF * FF),
        name="hidden",
    )(meta, rows, mine, theirs, vecs, *pieces)


def down_copies(meta, pieces, dst, sems):
    z, y, c = meta[1], meta[2], meta[3]
    copies = []
    for at, piece in enumerate(pieces):
        dc, k = at // 4, at % 4
        zz = lax.rem(z - k + 4, 4)
        cc = jnp.where(c == 0, dc, 1 - dc)
        for dy in range(2):
            yy = jnp.where(y == 0, dy, 1 - dy)
            row = pl.multiple_of(((zz * 2 + yy) * 2 + cc) * 192, 192)
            copies.append(
                pltpu.make_async_copy(piece.at[dy], dst.at[pl.ds(row, 192)], sems.at[at * 2 + dy])
            )
    return copies


def mlp_back_kernel(meta, res, cot, vecs, hid, a, b, *rest):
    pieces, downs = rest[:16], rest[16:24]
    out, keep, send, gate_g, up_g, g_one, low, mine, theirs, vgrads = rest[24:34]
    acc, held, m, w, wd, sems, down_sems = rest[34:]
    step = pl.program_id(0)
    copies = piece_copies(meta, pieces, w, sems)
    down = down_copies(meta, downs, wd, down_sems)

    @pl.when(step == 0)
    def _():
        for copy in down:
            copy.start()
        z, _ = norm_parts(res[...])
        acc[...] = z * vecs[0:1, :] + vecs[1:2, :]
        for copy in down:
            copy.wait()

    @pl.when(step == 1)
    def _():
        for copy in copies:
            copy.start()

    @pl.when(step < 4)
    def _():
        held[step] = hid[0]
        acc[...] += dot(hid[0], wd[pl.ds(pl.multiple_of(step * BLK, BLK), BLK), :])

    @pl.when(step == 3)
    def _():
        z, scale = norm_parts(acc[...])
        out[...] = (z * vecs[2:3, :] + vecs[3:4, :]).astype(bf16)
        c = cot[...].astype(f32)
        vgrads[2:3, :] = jnp.sum(c * z, axis=0, keepdims=True)
        vgrads[3:4, :] = jnp.sum(c, axis=0, keepdims=True)
        back = norm_back(c, z, scale, vecs[2:3, :])
        acc[...] = back
        m[...] = back.astype(bf16)

    @pl.when(step == 4)
    def _():
        for copy in copies:
            copy.wait()

    @pl.when(step >= 4)
    def _():
        j = step - 4
        half, at = j // 2, (j % 2) * BLK
        hg = dot_t(m[...], wd[pl.ds(pl.multiple_of(j * BLK, BLK), BLK), :])
        gg = (hg * a[0].astype(f32)).astype(bf16)
        ug = (hg * b[0].astype(f32)).astype(bf16)
        gate_g[0] = gg
        up_g[0] = ug
        acc[...] += dot_t(gg, w[half, :, pl.ds(pl.multiple_of(at, BLK), BLK)]) + dot_t(
            ug, w[half, :, pl.ds(pl.multiple_of(GW + at, HW), BLK)]
        )
        val = lax.dot_general(held[j], m[...], (((0,), (0,)), ((), ())), preferred_element_type=f32)
        c = meta[3]
        parts = val.astype(bf16).reshape(2, 2, 2, 96, D)
        for y in range(2):
            for h in range(2):
                keep[h, 0, y] = jnp.where(c == 0, parts[y, 0, h], parts[y, 1, h])
                send[h, 0, y] = jnp.where(c == 0, parts[y, 1, h], parts[y, 0, h])

    @pl.when(step == 7)
    def _():
        z, scale = norm_parts(res[...])
        c = acc[...]
        vgrads[0:1, :] = jnp.sum(c * z, axis=0, keepdims=True)
        vgrads[1:2, :] = jnp.sum(c, axis=0, keepdims=True)
        back = norm_back(c, z, scale, vecs[0:1, :])
        g_one[...] = back
        back = back.astype(bf16)
        low[...] = back
        ag = dot_t(back[:, :HW], w[0, :, 2 * BLK : GW]) + dot_t(back[:, HW:], w[1, :, 2 * BLK : GW])
        ag = ag.astype(bf16)
        first = meta[0] == 0
        mine[...] = jnp.where(first, ag[:, :HW], ag[:, HW:])
        theirs[...] = jnp.where(first, ag[:, HW:], ag[:, :HW])


def mlp_back_call(meta, res, cot, vecs, hid, a, b, pieces, downs):
    early = lambda i: jnp.minimum(i, 3)
    late = lambda i: jnp.maximum(i - 4, 0)
    part = pl.BlockSpec((1, HALF, BLK), lambda i: (late(i), 0, 0))
    grad = pl.BlockSpec((2, 1, 2, 96, D), lambda i: (0, late(i), 0, 0, 0))
    return pl.pallas_call(
        mlp_back_kernel,
        grid=(8,),
        in_specs=[
            SM, NAT, NAT, whole((8, D)), pl.BlockSpec((1, HALF, BLK), lambda i: (early(i), 0, 0)), part, part,
        ] + [HBM] * 24,
        out_specs=[NAT, grad, grad, part, part, NAT, NAT, HEADS, HEADS, whole((8, D))],
        out_shape=[
            shape((HALF, D), bf16),
            shape((2, 4, 2, 96, D), bf16),
            shape((2, 4, 2, 96, D), bf16),
            shape((4, HALF, BLK), bf16),
            shape((4, HALF, BLK), bf16),
            shape((HALF, D), f32),
            shape((HALF, D), bf16),
            shape((HALF, HW), bf16),
            shape((HALF, HW), bf16),
            shape((8, D), f32),
        ],
        scratch_shapes=[
            pltpu.VMEM((HALF, D), f32),
            pltpu.VMEM((4, HALF, BLK), bf16),
            pltpu.VMEM((HALF, D), bf16),
            pltpu.VMEM((2, D, MW), bf16),
            pltpu.VMEM((FF, D), bf16),
            pltpu.SemaphoreType.DMA((32,)),
            pltpu.SemaphoreType.DMA((16,)),
        ],
        compiler_params=params(62),
        cost_estimate=cost(2 * HALF * D * 5 * FF, 40e6),
        name="mlp_back",
    )(meta, res, cot, vecs, hid, a, b, *pieces, *downs)


def wide_grads_kernel(width, meta, low_t, grads, *rest):
    c = meta[3]
    keep, send = rest[-2:]

    def put(at, val):
        stay, leave = split_core(c, val)
        cols = slice(at, at + val.shape[1])
        for z in range(4):
            for y in range(2):
                keep[0, z, y, :, cols] = stay[2 * z + y]
                send[0, z, y, :, cols] = leave[2 * z + y]

    for i in range(2):
        put(i * BLK, dot(low_t[...], grads[i]))
    if width == GW:
        put(2 * BLK, dot(rest[0][...], rest[1][...]))


def wide_grads_call(meta, low_t, grads, *out_part):
    width = GW if out_part else 2 * BLK
    tall = whole((D, HALF))
    grad = pl.BlockSpec((1, 4, 2, 48, width), lambda i: (i, 0, 0, 0, 0))
    extra = [tall, pl.BlockSpec((HALF, HW), lambda i: (0, i))] if out_part else []
    return pl.pallas_call(
        partial(wide_grads_kernel, width),
        grid=(2,),
        in_specs=[SM, tall, pl.BlockSpec((2, HALF, BLK), lambda i: (i, 0, 0))] + extra,
        out_specs=[grad] * 2,
        out_shape=[shape((2, 4, 2, 48, width), bf16)] * 2,
        compiler_params=params(20),
        cost_estimate=cost(2 * HALF * D * FF, 9e6),
        name="wide_grads",
    )(meta, low_t, grads, *out_part)


def first_grads_kernel(meta, own, other, grads, vgrads, keep, send, rows_t):
    step = pl.program_id(0)

    @pl.when(step == 0)
    def _():
        rows_t[:, :HALF] = own[...].T
        rows_t[:, HALF:] = other[...].T
        row = lax.broadcasted_iota(jnp.int32, (8, D), 0)
        four = jnp.where(row < 4, vgrads[...], 0.0)
        four = jnp.concatenate([four, jnp.zeros((120, D), f32)], axis=0).T
        keep[:, :, 3 * HW :], send[:, :, 3 * HW :] = split_core(meta[3], four)

    for j in range(3):

        @pl.when(step == j)
        def _():
            at = slice(j * HW, (j + 1) * HW)
            keep[:, :, at], send[:, :, at] = split_core(meta[3], dot(rows_t[...], grads[...]))


def first_grads_call(meta, own, other, grads, vgrads):
    grad = whole((8, 48, QW))
    return pl.pallas_call(
        first_grads_kernel,
        grid=(3,),
        in_specs=[SM, NAT, NAT, pl.BlockSpec((2 * HALF, HW), lambda i: (0, i)), whole((8, D))],
        out_specs=[grad] * 2,
        out_shape=[shape((8, 48, QW), bf16)] * 2,
        scratch_shapes=[pltpu.VMEM((D, 2 * HALF), bf16)],
        compiler_params=params(24),
        cost_estimate=cost(2 * 2 * HALF * D * 3 * HW, 8e6),
        name="first_grads",
    )(meta, own, other, grads, vgrads)


def tokens_part_kernel(grads, w, first, second):
    val = dot_t(grads[...], w[:, : 3 * HW]).astype(bf16)

    @pl.when(pl.program_id(0) == 0)
    def _():
        first[...] = val

    @pl.when(pl.program_id(0) == 1)
    def _():
        second[...] = val


def tokens_part_call(grads, w):
    return pl.pallas_call(
        tokens_part_kernel,
        grid=(2,),
        in_specs=[pl.BlockSpec((HALF // 2, 3 * HW), lambda i: (i + 2, 0)), whole((D, QW))],
        out_specs=[whole((HALF // 2, D))] * 2,
        out_shape=[shape((HALF // 2, D), bf16)] * 2,
        compiler_params=params(16),
        cost_estimate=cost(2 * HALF * D * 3 * HW, 5e6),
        name="tokens_part",
    )(grads, w)


def tokens_grad_kernel(g_one, first, second, grads, w, out):
    theirs = jnp.where(pl.program_id(0) == 0, first[...], second[...]).astype(f32)
    out[...] = g_one[...] + theirs + dot_t(grads[...], w[:, : 3 * HW])


def tokens_grad_call(g_one, theirs, grads, w):
    part = pl.BlockSpec((HALF // 2, D), lambda i: (i, 0))
    half = whole((HALF // 2, D))
    return pl.pallas_call(
        tokens_grad_kernel,
        grid=(2,),
        in_specs=[part, half, half, pl.BlockSpec((HALF // 2, 3 * HW), lambda i: (i, 0)), whole((D, QW))],
        out_specs=part,
        out_shape=shape((HALF, D), f32),
        compiler_params=params(16),
        cost_estimate=cost(2 * HALF * D * 3 * HW, 8e6),
        name="tokens_grad",
    )(g_one, *theirs, grads, w)


def pick(a, at, axis):
    return lax.dynamic_index_in_dim(a, at, axis, keepdims=False)


def flip_x(a):
    return lax.ppermute(a, "seq", [(0, 1), (1, 0)])


def flip(bit):
    def go(a):
        n = lax.axis_size("shard")
        return lax.ppermute(a, "shard", [(s, s ^ bit) for s in range(n)])

    return go


flip_c, flip_y, flip_z, flip_far = flip(1), flip(2), flip(4), flip(8)


def turn_z(a, k):
    return lax.ppermute(a, "shard", [(s, (s + 4 * k) % 16) for s in range(16)])


def after(a, *deps):
    return lax.optimization_barrier((a,) + deps)[0]


def slot(*arrays):
    return lax.optimization_barrier(arrays)


def around(mine):
    return [turn_z(mine, k) for k in (1, 2, 3)]


def pieces_of_whole(full):
    cut = full.reshape(full.shape[0], 4, 2, 2, 48, full.shape[2])
    order = jnp.array([0, 3, 2, 1])
    return [
        cut[dh, :, dy, dc][order]
        for dc in range(2)
        for dy in range(2)
        for dh in range(full.shape[0])
    ]


def in_two(pieces):
    return [part for piece in pieces for part in (piece[:2], piece[2:])]


def add(a, b):
    return a.astype(f32) + b.astype(f32)


def turns(sends):
    return [turn_z(send, k + 1) for k, send in enumerate(sends)]


def fold(meta, ins, outs, name):
    def kernel(*refs):
        spot = refs[0][0], refs[0][1], refs[0][2]
        for (_, give), out in zip(outs, refs[1 + len(ins) :]):
            out[...] = give(spot, *refs[1 : 1 + len(ins)]).astype(bf16)

    moved = 2 * sum(a.size for a in ins)
    return pl.pallas_call(
        kernel,
        grid=(1,),
        in_specs=[SM] + [whole(a.shape) for a in ins],
        out_specs=[whole(dims) for dims, _ in outs],
        out_shape=[shape(dims, bf16) for dims, _ in outs],
        compiler_params=params(32),
        cost_estimate=cost(moved, 2 * moved),
        name=name,
    )(meta, *ins)


def cut_core(rows, cols_x, cols_y):
    def along_x(flip):
        def give(spot, keep, got):
            at = spot[0] if flip == 0 else 1 - spot[0]
            return add(keep[at, :, :, :, :cols_x], got[at, :, :, :, :cols_x])

        return give

    def along_y(flip):
        def give(spot, keep, got):
            at = spot[2] if flip == 0 else 1 - spot[2]
            return add(keep[:, :, at, :, cols_x:], got[:, :, at, :, cols_x:])

        return give

    dims_x, dims_y = (4, 2, rows, cols_x), (2, 4, rows, cols_y)
    return [(dims_x, along_x(0)), (dims_x, along_x(1)), (dims_y, along_y(0)), (dims_y, along_y(1))]


def first_two(outs):
    return [(dims, lambda spot, *refs, give=give: give(spot, *refs[:2])) for dims, give in outs]


def cut_plane(rows, cols_x, cols_y, first):
    def along_y(flip):
        def give(spot, *refs):
            at = spot[2] if flip == 0 else 1 - spot[2]
            return add(refs[first][:, at], refs[first + 1][:, at])

        return give

    def along_x(flip):
        def give(spot, *refs):
            at = spot[0] if flip == 0 else 1 - spot[0]
            return add(refs[first + 2][at], refs[first + 3][at])

        return give

    dims_a, dims_b = (4, rows, cols_x), (4, rows, cols_y)
    return [(dims_a, along_y(0)), (dims_a, along_y(1)), (dims_b, along_x(0)), (dims_b, along_x(1))]


def cut_line(rows, cols, first, count):
    def part(k):
        def give(spot, *refs):
            at = lax.rem(spot[1] + k, 4)
            sums = [
                add(refs[first + 2 * i][at], refs[first + 2 * i + 1][at]) for i in range(count)
            ]
            return sums[0] if count == 1 else jnp.concatenate(sums, axis=-1)

        return give

    return [((rows, cols), part(k)) for k in range(4)]


def cut_near(rows, cols, first, count):
    def part(flip):
        def give(spot, *refs):
            odd = lax.rem(spot[1] + flip, 2)
            return jnp.stack(
                [
                    jnp.concatenate(
                        [
                            add(refs[first + 2 * i][odd + 2 * b], refs[first + 2 * i + 1][odd + 2 * b])
                            for i in range(count)
                        ],
                        axis=-1,
                    )
                    for b in range(2)
                ]
            )

        return give

    return [((2, rows, cols), part(0)), ((2, rows, cols), part(1))]


def cut_far(rows, cols, first):
    def part(flip):
        def give(spot, *refs):
            at = lax.rem(spot[1] // 2 + flip, 2)
            return add(refs[first][at], refs[first + 1][at])

        return give

    return [((rows, cols), part(0)), ((rows, cols), part(1))]


def cut_z(rows, cols):
    def part(k):
        def give(spot, keep, got, *_):
            at = lax.rem(spot[1] + k, 4)
            return add(keep[:, at], got[:, at])

        return give

    return [((2, 2, rows, cols), part(k)) for k in range(4)]


def pair(dims, first):
    return [(dims, lambda spot, *refs: add(refs[first][...], refs[first + 1][...]))]


def total_of(rows, cols, first):
    def give(spot, *refs):
        near, *gots = [refs[first + i][...].astype(f32) for i in range(4)]
        return near + gots[0] + gots[1] + gots[2]

    return [((rows, cols), give)]


def halves(mine, other, x):
    return jnp.where(x == 0, jnp.stack([mine, other]), jnp.stack([other, mine])).astype(f32)


def whole_of_split(keep, send):
    both = jnp.stack([keep, send], axis=3)
    return both.transpose(1, 2, 3, 4, 0, 5).reshape(D, -1)


def whole_of_down(keep, send):
    return jnp.stack([keep, send], axis=3).transpose(1, 2, 3, 0, 4, 5).reshape(FF, D)


def local(
    tokens,
    doc_lengths,
    qkv_weight,
    out_weight,
    gate_weight,
    up_weight,
    down_weight,
    norm1_gain,
    norm1_bias,
    norm2_gain,
    norm2_bias,
    cotangent,
):
    n = lax.axis_size("shard")
    fast = n == 16
    x = lax.axis_index("seq").astype(jnp.int32)
    shard = lax.axis_index("shard").astype(jnp.int32)
    zero = jnp.zeros((), jnp.int32)
    z, y, c = (shard // 4, (shard // 2) % 2, shard % 2) if fast else (zero, zero, zero)

    rows = tokens[0]
    cot = cotangent[0]
    lengths = lax.dynamic_slice_in_dim(doc_lengths, shard, 1, 0)[0]
    ends = jnp.cumsum(lengths).astype(jnp.int32)
    hx = x if fast else zero
    meta = jnp.concatenate([jnp.stack([x, z, y, c, hx]), jnp.zeros((3,), jnp.int32), ends])
    spots = jnp.arange(2 * HALF, dtype=jnp.int32)
    spots = jnp.where(spots < HALF, spots + x * HALF, spots - x * HALF)
    passed = spots[:, None] >= ends[None, :]
    place = spots - jnp.sum(jnp.where(passed, lengths[None, :], 0), axis=1)
    frequency = rope_base ** (-jnp.arange(HD // 2, dtype=f32) * 2.0 / HD)
    angles = place.astype(f32)[:, None] * frequency[None, :]
    cosine = jnp.tile(jnp.cos(angles), (1, 4))
    sine = jnp.sin(angles)
    sine = jnp.concatenate([-sine, sine, -sine, sine], axis=1)

    vec_block = jnp.stack([norm1_gain, norm1_bias, norm2_gain, norm2_bias], axis=1)
    vec_block = jnp.pad(vec_block, ((0, 0), (0, 124)))

    def my_heads(w):
        mine = lax.dynamic_slice_in_dim(w.reshape(w.shape[0], 3, 2, HW), x, 1, 2)
        mine = mine.reshape(w.shape[0], 3, 3, 128).transpose(0, 2, 1, 3)
        return mine.reshape(w.shape[0], 3 * HW)

    def half_of(w, at):
        cols = w.shape[1] // 2
        return jnp.where(at == 0, w[:, :cols], w[:, cols:])

    if fast:
        first = jnp.concatenate([my_heads(qkv_weight), vec_block], axis=1)
        wide, wide_o = [
            jnp.concatenate([half_of(w, at) for w in (gate_weight, out_weight, up_weight)], axis=1)
            for at in (x, 1 - x)
        ]
        zq, yd, yo = around(first), flip_y(down_weight), flip_y(wide_o)
        first, zq, wide, cosine, sine, rows_late, yd = slot(
            first, zq, wide, cosine, sine, rows, yd
        )
        wide_late, wide1 = wide, turn_z(wide, 1)
        aq = jnp.stack([first] + zq)
        byq, rows_other = flip_y(aq), flip_x(rows_late)
        wide2, wide3 = turn_z(wide_late, 2), turn_z(wide_late, 3)
        aq, byq, wide, wide1, wide3, down, yd, yo = slot(aq, byq, wide, wide1, wide3, down_weight, yd, yo)
        a0 = jnp.stack([wide, wide1])
        d0 = jnp.stack([down, yd])
        caq, cbyq = flip_c(aq), flip_c(byq)
        caq, cbyq, a0, rows_other, d0 = slot(caq, cbyq, a0, rows_other, d0)
        by0, bx0, ca0 = flip_y(a0), flip_x(a0), flip_c(a0)
        first_pieces = [aq, byq, caq, cbyq]
    else:
        rows_other = flip_x(rows)

        def gathered(w):
            return lax.all_gather(w, "shard", axis=0, tiled=True)

        first = jnp.concatenate([my_heads(gathered(qkv_weight)), gathered(vec_block)], axis=1)
        first_pieces = pieces_of_whole(first[None])

        def in_halves(w):
            return gathered(w).reshape(D, 2, -1).transpose(1, 0, 2)

        wide_all = jnp.concatenate([in_halves(w) for w in (gate_weight, out_weight, up_weight)], axis=2)
        pieces = in_two(pieces_of_whole(wide_all))
        down_all = gathered(down_weight).reshape(4, 2, 2, 192, D)
        down_pieces = [down_all[(4 - k) % 4, :, dc] for dc in range(2) for k in range(4)]

    q, k, kt, v, vt, w1, vecs = qkv_call(meta, rows, rows_other, cosine, sine, first_pieces)
    if fast:
        q, by0, bx0, wide2, d0, ca0 = slot(q, by0, bx0, wide2, d0, ca0)
        a1 = jnp.stack([wide2, wide3])
        q, a1 = slot(q, a1)
        by1, bx1, d1 = flip_y(a1), flip_x(a1), turn_z(d0, 1)
        cby0, cbx0 = flip_c(by0), flip_c(bx0)
    att_theirs, at_other, lse_other = attend_call(meta, q, k, vt, 1)
    if fast:
        q, att_theirs, by1, bx1, cby0, cbx0, d1, by0, a1 = slot(
            q, att_theirs, by1, bx1, cby0, cbx0, d1, by0, a1
        )
    att_got = flip_x(att_theirs)
    if fast:
        bxy0, bxy1, d2 = flip_x(by0[1]), flip_y(bx1), turn_z(d1, 1)
        ca1 = flip_c(a1)
    att_mine, at_own, lse_own = attend_call(meta, q, k, vt, 0)
    if fast:
        att_mine, att_got, bxy0, bxy1, d2, ca1, by1, bx1 = slot(
            att_mine, att_got, bxy0, bxy1, d2, ca1, by1, bx1
        )
        bxy0 = jnp.stack([yo, bxy0])
        cby1 = flip_c(by1)
        cbx1, cbxy0, cbxy1 = flip_c(bx1), flip_c(bxy0), flip_c(bxy1)
        att_mine, cbx1, cby1, cbxy0, cbxy1, d0, d1, d2 = slot(
            att_mine, cbx1, cby1, cbxy0, cbxy1, d0, d1, d2
        )
        d3, cd0, cd1, cd2 = turn_z(d2, 1), flip_c(d0), flip_c(d1), flip_c(d2)
        pieces = [a0, a1, bx0, bx1, by0, by1, bxy0, bxy1]
        pieces += [ca0, ca1, cbx0, cbx1, cby0, cby1, cbxy0, cbxy1]
    res, low_t, att_t, hid, part_a, part_b = hidden_call(
        meta, rows, att_mine, att_got, vecs, pieces
    )
    if fast:
        hid, d3, cd0, cd1, cd2 = slot(hid, d3, cd0, cd1, cd2)
        down_pieces = [d0, d1, d2, d3, cd0, cd1, cd2, flip_c(d3)]
    out, keep_d, send_d, gate_g, up_g, g_one, g_low, g_mine, g_theirs, vgrads = mlp_back_call(
        meta, res, cot, vecs, hid, part_a, part_b, pieces, down_pieces
    )

    if fast:
        keep_d, send_d, g_theirs, gate_g = slot(keep_d, send_d, g_theirs, gate_g)
        got_d = flip_c(send_d)
    keep_g, send_g = wide_grads_call(meta, low_t, gate_g, att_t, g_low)
    if fast:
        send_g, g_theirs, got_d, up_g = slot(send_g, g_theirs, got_d, up_g)
        got_g = flip_c(send_g)
    g_other = flip_x(g_theirs)
    keep_u, send_u = wide_grads_call(meta, low_t, up_g)
    if fast:
        send_u, got_g, got_d, g_other = slot(send_u, got_g, got_d, g_other)
        near_ga, sent_ga, near_gb, sent_gb, *part_d = fold(
            meta,
            (keep_g, got_g, keep_d, got_d),
            first_two(cut_core(48, GA, GW - GA))
            + [(dims, lambda spot, *refs, give=give: give(spot, *refs[2:])) for dims, give in cut_z(96, D)],
            "fold",
        )
        sent_ga, sent_gb, g_other, part_d, send_u = slot(sent_ga, sent_gb, g_other, part_d, send_u)
        got_ga, got_gb, got_u = flip_x(sent_ga), flip_y(sent_gb), flip_c(send_u)
        got_d = turn_z(part_d[3], 1)
    back_args = (q, k, kt, v, g_mine, g_other, at_own, at_other, lse_own, lse_other, cosine, sine)
    grads = attend_back_call(meta, *back_args, 0, 2)
    if fast:
        grads, got_ga, got_gb, got_u, got_d = slot(grads, got_ga, got_gb, got_u, got_d)
        near_ga, sent_ga, near_gb, sent_gb, near_ua, sent_ua, near_ub, sent_ub, sent_d = fold(
            meta,
            (keep_u, got_u, near_ga, got_ga, near_gb, got_gb, part_d[2], got_d),
            cut_plane(48, GA, GW - GA, 2) + first_two(cut_core(48, BLK, BLK)) + pair((2, 2, 96, D), 6),
            "fold",
        )
        grads, sent_ua, sent_ub, sent_ga, sent_gb, sent_d = slot(
            grads, sent_ua, sent_ub, sent_ga, sent_gb, sent_d
        )
        got_ua, got_ub, got_d = flip_x(sent_ua), flip_y(sent_ub), turn_z(sent_d, 1)
    grads = attend_back_call(meta, *back_args, 2, 1, grads)
    if fast:
        grads, got_ua, got_ub, got_d, sent_ga, sent_gb = slot(
            grads, got_ua, got_ub, got_d, sent_ga, sent_gb
        )
        near_ua, sent_ua, near_ub, sent_ub, sent_d = fold(
            meta,
            (near_ua, got_ua, near_ub, got_ub, part_d[1], got_d),
            cut_plane(48, BLK, BLK, 0) + pair((2, 2, 96, D), 4),
            "fold",
        )
        grads, sent_ga, sent_gb, sent_ua, sent_ub, sent_d = slot(
            grads, sent_ga, sent_gb, sent_ua, sent_ub, sent_d
        )
        got_ga, got_gb, got_ua, got_ub = flip_y(sent_ga), flip_x(sent_gb), flip_y(sent_ua), flip_x(sent_ub)
        got_d = turn_z(sent_d, 1)
    keep_q, send_q = first_grads_call(meta, rows, rows_other, grads, vgrads)
    if fast:
        keep_q, send_q, got_ga, got_gb, got_ua, got_ub, got_d, grads = slot(
            keep_q, send_q, got_ga, got_gb, got_ua, got_ub, got_d, grads
        )
        near_g, sent_g, near_d, sent_d = fold(
            meta,
            (near_ga, got_ga, near_gb, got_gb, part_d[0], got_d),
            cut_near(48, GW, 0, 2)
            + [
                ((2, 96, D), lambda spot, *refs: add(refs[4][:, spot[2]], refs[5][:, spot[2]])),
                ((2, 96, D), lambda spot, *refs: add(refs[4][:, 1 - spot[2]], refs[5][:, 1 - spot[2]])),
            ],
            "fold",
        )
        sent_g, sent_d, send_q, grads = slot(sent_g, sent_d, send_q, grads)
        got_g, got_q, got_d = flip_z(sent_g), flip_c(send_q), flip_y(sent_d)
    theirs = tokens_part_call(grads, w1)
    if fast:
        theirs_0 = flip_x(theirs[0])
        got_g, got_q, got_d, theirs_0, theirs_1 = slot(got_g, got_q, got_d, theirs_0, theirs[1])
        cut = (4, 2, 48, QW)
        near_u, sent_u, near_g, sent_g, total_d, near_q, sent_q = fold(
            meta,
            (
                near_ua, got_ua, near_ub, got_ub, near_g, got_g, near_d, got_d,
                keep_q.reshape(cut), got_q.reshape(cut),
            ),
            cut_near(48, 2 * BLK, 0, 2)
            + cut_far(48, GW, 4)
            + pair((2, 96, D), 6)
            + [
                ((4, 48, QW), lambda spot, *refs: add(refs[8][:, spot[2]], refs[9][:, spot[2]])),
                ((4, 48, QW), lambda spot, *refs: add(refs[8][:, 1 - spot[2]], refs[9][:, 1 - spot[2]])),
            ],
            "fold",
        )
        sent_u, sent_g, total_d, sent_q, theirs_1 = slot(sent_u, sent_g, total_d, sent_q, theirs_1)
        got_q, theirs_1, got_u, got_g = flip_y(sent_q), flip_x(theirs_1), flip_z(sent_u), flip_far(sent_g)
        got_q, got_u, got_g, total_d, theirs_1 = slot(got_q, got_u, got_g, total_d, theirs_1)
        theirs = theirs_0, theirs_1
        near_q, sent_q, near_u, sent_u, total_g = fold(
            meta,
            (near_q, got_q, near_u, got_u, near_g, got_g),
            cut_near(48, QW, 0, 1) + cut_far(48, 2 * BLK, 2) + pair((48, GW), 4),
            "fold",
        )
        sent_q, sent_u, total_d, total_g = slot(sent_q, sent_u, total_d, total_g)
        got_q, got_u, other_d, other_g = flip_z(sent_q), flip_far(sent_u), flip_x(total_d), flip_x(total_g)
        got_q, got_u = slot(got_q, got_u)
        near_q, sent_q, total_u = fold(
            meta,
            (near_q, got_q, near_u, got_u),
            cut_far(48, QW, 0) + pair((48, 2 * BLK), 2),
            "fold",
        )
        sent_q, total_u = slot(sent_q, total_u)
        got_q, other_u = flip_far(sent_q), flip_x(total_u)
    else:
        theirs = flip_x(theirs[0]), flip_x(theirs[1])
    grad_in = tokens_grad_call(g_one, theirs, grads, w1)
    if fast:
        got_q, grad_in, other_u, other_d, other_g = slot(got_q, grad_in, other_u, other_d, other_g)
        (total_q,) = fold(meta, (near_q, got_q), pair((48, QW), 0), "fold")
        other_q = flip_x(total_q)

    def joined(part):
        n_rows = part.shape[1]
        part = part.reshape(2, n_rows, 3, 3, 128).transpose(1, 3, 0, 2, 4)
        return part.reshape(n_rows, 3 * D)

    if fast:
        grad_qkv = joined(halves(total_q[:, : 3 * HW], other_q[:, : 3 * HW], x))
        grad_g = halves(total_g, other_g, x)
        grad_gate = jnp.concatenate([grad_g[0, :, : 2 * BLK], grad_g[1, :, : 2 * BLK]], axis=1)
        grad_out = jnp.concatenate([grad_g[0, :, 2 * BLK :], grad_g[1, :, 2 * BLK :]], axis=1)
        grad_up = jnp.concatenate(list(halves(total_u, other_u, x)), axis=1)
        grad_down = add(total_d, other_d).reshape(-1, D)
        vec_own = add(total_q[:, 3 * HW : 3 * HW + 4], other_q[:, 3 * HW : 3 * HW + 4]).T
    else:

        def owned(a):
            part = lax.psum_scatter(a, "shard", scatter_dimension=0, tiled=True)
            return lax.psum(part, "seq").astype(f32)

        grad_g = whole_of_split(keep_g, send_g)
        grad_gate = owned(jnp.concatenate([grad_g[:, : 2 * BLK], grad_g[:, GW : GW + 2 * BLK]], axis=1))
        grad_out = owned(jnp.concatenate([grad_g[:, 2 * BLK : GW], grad_g[:, GW + 2 * BLK :]], axis=1))
        grad_up = owned(whole_of_split(keep_u, send_u))
        grad_down = owned(whole_of_down(keep_d, send_d))
        mine = jnp.stack([keep_q, send_q], axis=1).reshape(D, QW)[:, : 3 * HW]
        none = jnp.zeros_like(mine)
        both = jnp.stack([jnp.where(x == 0, mine, none), jnp.where(x == 0, none, mine)])
        grad_qkv = owned(joined(both))
        vec_grads = lax.psum(vgrads[:4], ("seq", "shard"))
        vec_own = lax.dynamic_slice_in_dim(vec_grads, shard * (D // n), D // n, 1)
    return (
        out[None],
        grad_in[None],
        grad_qkv,
        grad_out,
        grad_gate,
        grad_up,
        grad_down,
        vec_own[0],
        vec_own[1],
        vec_own[2],
        vec_own[3],
    )


def solution(mesh):
    placed = (
        P("shard", "seq", None),
        P(),
        P("shard", None),
        P("shard", None),
        P("shard", None),
        P("shard", None),
        P("shard", None),
        P("shard"),
        P("shard"),
        P("shard"),
        P("shard"),
        P("shard", "seq", None),
    )
    return jax.shard_map(
        local,
        mesh=mesh,
        in_specs=placed,
        out_specs=(
            P("shard", "seq", None),
            P("shard", "seq", None),
            P("shard", None),
            P("shard", None),
            P("shard", None),
            P("shard", None),
            P("shard", None),
            P("shard"),
            P("shard"),
            P("shard"),
            P("shard"),
        ),
        check_vma=False,
    )
```
